512 devices in a mesh: gx: 16 (over z), gy: 4 (over x_lo, core), gz: 8 (over x_hi, y).
Axes of the slice: x: 4 (x_hi: 2, x_lo: 2; x = x_hi * 2 + x_lo), y: 4, z: 16, core: 2. Of those that a mesh axis runs over, the one named last changes fastest.
Arguments:
- fine_start: float32 [5, 32, 256, 512], P(None, 'gz', 'gx', 'gy'), as said below
- fine_section: float32 [5, 32, 256, 512], P(None, 'gz', 'gx', 'gy'), as said below
- fine_noise: float32 [3, 32, 256, 512], P(None, 'gz', 'gx', 'gy'), may hold values from -6 to 6
- coarse_start: float32 [5, 16, 128, 256], P(None, 'gz', 'gx', 'gy'), as said below
- coarse_section: float32 [5, 16, 128, 256], P(None, 'gz', 'gx', 'gy'), as said below
- kernel: float32 [3, 9], replicated, may hold values from -3 to 3
- owner: int32 [8], replicated, may hold values from 0 to 7, each once
Outputs:
- fine_next: float32 [5, 32, 256, 512], P(None, 'gz', 'gx', 'gy')
- coarse_next: float32 [5, 16, 128, 256], P(None, 'gz', 'gx', 'gy')
The draws below stay inside these ranges and needn't reach their ends.
Inputs may be any that keep to these rules, and one draw needn't show every extreme that they name: owner is a permutation of 0 to 7. `fine_section`: density lies in [0.5, 2], each velocity component within [-1.2, 1.2], pressure (0.4 (E - |m|^2 / (2 rho))) in [0.4, 2]. `fine_start`: as for fine_section. `coarse_section`: as for fine_section. `coarse_start`: as for fine_section.
All inputs are finite; a program needn't handle non-finite values.
Results may differ from the reference program's by a relative error of at most 0.00005.
Values sent between devices are 32-bit elements; how exact they have to be, the bound alone decides.
A program may use at most 64 MiB of HBM per device.

```python
import jax
import jax.numpy as jnp
from jax import lax

CZ = 4
NX = 256
NY = 512
NZ = 32
N_GZ = 8


def assemble_state(key, shape, rho_low, rho_high, pres_low, pres_high, vel_scale):
    key_rho, key_pres, key_normal = jax.random.split(key, 3)
    cells = tuple(shape)
    density = jnp.exp(jax.random.uniform(key_rho, cells, jnp.float32, jnp.log(rho_low), jnp.log(rho_high)))
    pressure = jnp.exp(jax.random.uniform(key_pres, cells, jnp.float32, jnp.log(pres_low), jnp.log(pres_high)))
    normal_part = jnp.clip(vel_scale * jax.random.normal(key_normal, (3,) + cells, jnp.float32), -1.2, 1.2)
    velocity = normal_part
    momentum = density * velocity
    energy = pressure / 0.4 + 0.5 * density * jnp.sum(velocity * velocity, axis=0)
    return jnp.concatenate([density[None], momentum, energy[None]], axis=0)


def draw_fine_start(key, part):
    key = jax.random.fold_in(key, 11)
    return assemble_state(key, (NZ, NX, NY), 0.7, 1.5, 0.5, 1.5, 0.4)


def draw_fine_section(key, part):
    key = jax.random.fold_in(key, 12)
    return assemble_state(key, (NZ, NX, NY), 0.7, 1.5, 0.5, 1.5, 0.4)


def draw_coarse_start(key, part):
    key = jax.random.fold_in(key, 13)
    return assemble_state(key, (NZ // 2, NX // 2, NY // 2), 0.7, 1.5, 0.5, 1.5, 0.4)


def draw_coarse_section(key, part):
    key = jax.random.fold_in(key, 14)
    return assemble_state(key, (NZ // 2, NX // 2, NY // 2), 0.7, 1.5, 0.5, 1.5, 0.4)


def block_scale(key, dims, pieces, least, largest):
    factor_of = 1.0
    for position, shards_of in pieces:
        draws = jax.random.uniform(jax.random.fold_in(jax.random.fold_in(key, 6), position), (shards_of,), jnp.float32, least / len(pieces), largest / len(pieces))
        factor_of = factor_of * jnp.repeat(jnp.exp(draws), dims[position] // shards_of).reshape((-1,) + (1,) * (len(dims) - 1 - position))
    return factor_of


def bell_draw(own_key, shape, spread, reach, cuts=(), held_as=jnp.bfloat16):
    level = block_scale(own_key, shape, cuts, -0.22, 0.18) if cuts else 1.0
    result = jax.random.normal(own_key, shape, jnp.float32) * spread * level
    return jnp.minimum(jnp.maximum(result, -reach), reach).astype(held_as)


def setup_inputs(seed: int = 0) -> dict:
    keys = jax.random.split(jax.random.key(seed), 8)
    return {
        "fine_start": draw_fine_start(jax.random.fold_in(keys[7], 71), 0),
        "fine_section": draw_fine_section(jax.random.fold_in(keys[7], 71), 0),
        "fine_noise": bell_draw(keys[2], (3, NZ, NX, NY), 1.0, 6.0, ((1, 8), (2, 16), (3, 4)), jnp.float32),
        "coarse_start": draw_coarse_start(jax.random.fold_in(keys[7], 71), 0),
        "coarse_section": draw_coarse_section(jax.random.fold_in(keys[7], 71), 0),
        "kernel": bell_draw(keys[5], (3, 9), 0.55, 3.0, (), jnp.float32),
        "owner": jax.random.permutation(keys[6], N_GZ).astype(jnp.int32),
    }


GAMMA = 1.4
CFL_NUMBER = 0.4
WENO_EPS = 1e-06
RESTRICT_SCALE = 0.35355339059327373

def flux_fields(state, component):
    density = state[0]
    velocity = state[component] / density
    pressure = (GAMMA - 1.0) * (state[4] - 0.5 * (state[1] * state[1] + state[2] * state[2] + state[3] * state[3]) / density)
    entries = [state[component], state[1] * velocity, state[2] * velocity, state[3] * velocity, (state[4] + pressure) * velocity]
    entries[component] = entries[component] + pressure
    return jnp.stack(entries)

def weno_side(first, second, third, fourth, fifth):
    cand_low = (2.0 * first - 7.0 * second + 11.0 * third) / 6.0
    cand_mid = (-second + 5.0 * third + 2.0 * fourth) / 6.0
    cand_high = (2.0 * third + 5.0 * fourth - fifth) / 6.0
    smooth_low = 13.0 / 12.0 * (first - 2.0 * second + third) ** 2 + 0.25 * (first - 4.0 * second + 3.0 * third) ** 2
    smooth_mid = 13.0 / 12.0 * (second - 2.0 * third + fourth) ** 2 + 0.25 * (second - fourth) ** 2
    smooth_high = 13.0 / 12.0 * (third - 2.0 * fourth + fifth) ** 2 + 0.25 * (3.0 * third - 4.0 * fourth + fifth) ** 2
    weight_low = 0.1 / (WENO_EPS + smooth_low) ** 2
    weight_mid = 0.6 / (WENO_EPS + smooth_mid) ** 2
    weight_high = 0.3 / (WENO_EPS + smooth_high) ** 2
    return (weight_low * cand_low + weight_mid * cand_mid + weight_high * cand_high) / (weight_low + weight_mid + weight_high)

def sweep(extended, direction, wave_speed):
    extent = extended.shape[direction] - 6
    component = {1: 3, 2: 1, 3: 2}[direction]
    fluxes = flux_fields(extended, component)
    upwind = 0.5 * (fluxes + wave_speed * extended)
    downwind = 0.5 * (fluxes - wave_speed * extended)

    def pick(values, start):
        return lax.slice_in_dim(values, start, start + extent + 1, axis=direction)
    face_flux = weno_side(pick(upwind, 0), pick(upwind, 1), pick(upwind, 2), pick(upwind, 3), pick(upwind, 4))
    face_flux = face_flux + weno_side(pick(downwind, 5), pick(downwind, 4), pick(downwind, 3), pick(downwind, 2), pick(downwind, 1))
    return lax.slice_in_dim(face_flux, 1, extent + 1, axis=direction) - lax.slice_in_dim(face_flux, 0, extent, axis=direction)

def wave_speed_of(state):
    density = state[0]
    pressure = (GAMMA - 1.0) * (state[4] - 0.5 * (state[1] * state[1] + state[2] * state[2] + state[3] * state[3]) / density)
    sound = jnp.sqrt(GAMMA * pressure / density)
    fastest = jnp.maximum(jnp.maximum(jnp.abs(state[1]), jnp.abs(state[2])), jnp.abs(state[3])) / density + sound
    return jnp.max(fastest)

def advance(start, section, div_z, div_x, div_y, forcing, wave_speed, factor):
    density = section[0]
    source = jnp.stack([jnp.zeros_like(density), factor * density * forcing[0], factor * density * forcing[1], factor * density * forcing[2], factor * (section[1] * forcing[0] + section[2] * forcing[1] + section[3] * forcing[2])])
    change = -(div_z + div_x + div_y) + source
    return 0.75 * start + 0.25 * (section + CFL_NUMBER / wave_speed * change)

def conv_roll(field, taps, direction):
    total = taps[0] * jnp.roll(field, 4, axis=direction)
    for offset in range(1, 9):
        total = total + taps[offset] * jnp.roll(field, 4 - offset, axis=direction)
    return total

def filtered(field, kernel):
    return conv_roll(conv_roll(conv_roll(field, kernel[0], 2), kernel[1], 3), kernel[2], 1)

def wrap_pad(field, direction, width):
    widths = [(0, 0)] * 4
    widths[direction] = (width, width)
    return jnp.pad(field, widths, mode='wrap')

def grid_section(start, section, forcing, wave_speed, factor):
    div_z = sweep(wrap_pad(section, 1, 3), 1, wave_speed)
    div_x = sweep(wrap_pad(section, 2, 3), 2, wave_speed)
    div_y = sweep(wrap_pad(section, 3, 3), 3, wave_speed)
    return advance(start, section, div_z, div_x, div_y, forcing, wave_speed, factor)

def reference(fine_start, fine_section, fine_noise, coarse_start, coarse_section, kernel, owner):
    half_z = CZ // 2
    coarse_shape = coarse_section.shape
    block_shape = (5, N_GZ, half_z, coarse_shape[2], coarse_shape[3])
    owner_index = owner.astype(jnp.int32)
    geo_start = jnp.take(coarse_start.reshape(block_shape), owner_index, axis=1).reshape(coarse_shape)
    geo_section = jnp.take(coarse_section.reshape(block_shape), owner_index, axis=1).reshape(coarse_shape)
    speed_fine = wave_speed_of(fine_section)
    speed_coarse = wave_speed_of(coarse_section)
    forcing_fine = filtered(fine_noise, kernel)
    restricted = fine_noise.reshape(3, NZ // 2, 2, NX // 2, 2, NY // 2, 2).sum(axis=(2, 4, 6)) * RESTRICT_SCALE
    forcing_coarse = filtered(restricted, kernel)
    fine_next = grid_section(fine_start, fine_section, forcing_fine, speed_fine, 1.0)
    geo_next = grid_section(geo_start, geo_section, forcing_coarse, speed_coarse, 2.0)
    inverse = jnp.argsort(owner_index).astype(jnp.int32)
    coarse_next = jnp.take(geo_next.reshape(block_shape), inverse, axis=1).reshape(coarse_shape)
    return (fine_next, coarse_next)
```

```python
import jax
import jax.numpy as jnp
from jax import lax
from jax.experimental import pallas as pl
from jax.experimental.pallas import tpu as pltpu
from jax.sharding import PartitionSpec as P

MESH = pl.DeviceIdType.MESH
GX, GY, GZ = 16, 4, 8
GAMMA = 1.4
SPEED_EPS = 3e-06
RESTRICT_SCALE = 0.35355339059327373
NEAR = [(i, j) for i in range(GY) for j in range(GZ) if (i, j) != (0, 0)]
ALONG = [8, 7, 9, 6, 10, 5, 11, 4, 12, 3, 13, 2, 14, 1, 15]
CLOSE = [1, 2, 3, 4, 12, 13, 14, 15]


def pressure_of(state, inverse):
    kinetic = 0.5 * (state[1] * state[1] + state[2] * state[2] + state[3] * state[3])
    return (GAMMA - 1.0) * (state[4] - kinetic * inverse)


def flux_entries(state, inverse, pressure, component):
    velocity = state[component] * inverse
    entries = [
        state[component],
        state[1] * velocity,
        state[2] * velocity,
        state[3] * velocity,
        (state[4] + pressure) * velocity,
    ]
    entries[component] = entries[component] + pressure
    return entries


def flux_alone(state, component):
    inverse = 1.0 / state[0]
    return flux_entries(state, inverse, pressure_of(state, inverse), component)


def fastest_of(state, inverse, pressure):
    largest = jnp.maximum(jnp.maximum(jnp.abs(state[1]), jnp.abs(state[2])), jnp.abs(state[3]))
    return largest * inverse + jnp.sqrt(GAMMA * pressure * inverse)


def side(low, mid, high, p, q, r, s):
    m0 = mid * high
    m1 = low * high
    m2 = low * mid
    w0 = m0 * m0
    w1 = 6.0 * (m1 * m1)
    w2 = 3.0 * (m2 * m2)
    total = w0 + w1 + w2
    sums = w0 * (5.0 * q - 2.0 * p) + w1 * (q + 2.0 * r) + w2 * (4.0 * r - s)
    guess = pl.reciprocal(total, approx=True)
    return sums * (guess * (2.0 - total * guess))


def indicators(steps):
    squares = [e * e for e in steps]
    low, mid, high = [], [], []
    for i in range(len(steps) - 1):
        cross = steps[i] * steps[i + 1]
        both = squares[i] + squares[i + 1] + SPEED_EPS
        base = both - 2.75 * cross
        low.append(base + 1.5 * squares[i + 1])
        high.append(base + 1.5 * squares[i])
        mid.append(both - 1.25 * cross)
    return low, mid, high


def sweep(flux_steps, state_steps, speed, cells):
    scaled = [speed * u for u in state_steps]
    up = [f + u for f, u in zip(flux_steps, scaled)]
    down = [f - u for f, u in zip(flux_steps, scaled)]
    low_u, mid_u, high_u = indicators(up)
    low_d, mid_d, high_d = indicators(down)
    faces = []
    for j in range(cells + 1):
        right = side(low_u[j], mid_u[j + 1], high_u[j + 2], up[j], up[j + 1], up[j + 2], up[j + 3])
        left = side(
            high_d[j + 3], mid_d[j + 2], low_d[j + 1], down[j + 4], down[j + 3], down[j + 2], down[j + 1]
        )
        faces.append(right - left)
    return [
        up[c + 2] + down[c + 3] + (faces[c + 1] - faces[c]) * (1.0 / 6.0) for c in range(cells)
    ]


def swap_halves(values):
    return pltpu.roll(values, 64, 1)


def kernel(
    us, noise, cs, taps, owner, fine_out, coarse_out,
    sp1, sp2, cp, fcp, ux, fx, ty, fy, uz, fz, nz, gat, nx, wx, nt, force, halves,
    dz, d16, d8, d1, az, a16, a8, a1,
    far_sem, s1_send, s1_recv, s2_send, s2_recv, gat_send, gat_recv, hs, hr,
):
    gx, gy, gz = lax.axis_index("gx"), lax.axis_index("gy"), lax.axis_index("gz")

    def near(step):
        return {"gy": lax.rem(gy + step[0], GY), "gz": lax.rem(gz + step[1], GZ)}

    def along(step):
        return {"gx": lax.rem(gx + step, GX)}

    barrier = pltpu.get_barrier_semaphore()
    for step in NEAR:
        pl.semaphore_signal(barrier, inc=1, device_id=near(step), device_id_type=MESH)
    for step in CLOSE:
        pl.semaphore_signal(barrier, inc=1, device_id=along(step), device_id_type=MESH)

    lane = lax.broadcasted_iota(jnp.int32, (8, 128), 1)
    first_half = lane < 64
    first_half_40 = lax.broadcasted_iota(jnp.int32, (40, 128), 1) < 64

    best = jnp.zeros((16, 128), jnp.float32)
    for z in range(4):
        state = [us[(f * 4 + z) * 16 : (f * 4 + z) * 16 + 16, :] for f in range(5)]
        inverse = 1.0 / state[0]
        pressure = pressure_of(state, inverse)
        best = jnp.maximum(best, fastest_of(state, inverse, pressure))
        for f, entry in enumerate(flux_entries(state, inverse, pressure, 2)):
            fy[(f * 4 + z) * 16 : (f * 4 + z) * 16 + 16, :] = entry
        for f, entry in enumerate(flux_entries(state, inverse, pressure, 3)):
            fz[f, 3 + z] = entry
        for f in range(5):
            uz[f, 3 + z] = state[f]
    best = jnp.maximum(best[0:8], best[8:16])
    for f in range(5):
        cp[f * 8 : f * 8 + 8, :] = jnp.concatenate(
            [cs[f * 16 : f * 16 + 8, :], cs[f * 16 + 8 : f * 16 + 16, :]], axis=1
        )
    coarse = [cp[f * 8 : f * 8 + 8, :] for f in range(5)]
    coarse_inverse = 1.0 / coarse[0]
    coarse_pressure = pressure_of(coarse, coarse_inverse)
    coarse_best = fastest_of(coarse, coarse_inverse, coarse_pressure)
    best = jnp.where(
        first_half,
        jnp.maximum(best, swap_halves(best)),
        jnp.maximum(coarse_best, swap_halves(coarse_best)),
    )
    sp1[31:32, :] = jnp.max(best, axis=0, keepdims=True)

    for c in range(3):
        for z in range(4):
            nz[c, 4 + z] = noise[(c * 4 + z) * 16 : (c * 4 + z) * 16 + 16, :]
        for pair in range(2):
            row = (c * 4 + 2 * pair) * 16
            halves[(c * 2 + pair) * 16 : (c * 2 + pair) * 16 + 16, :] = (
                noise[row : row + 16, :] + noise[row + 16 : row + 32, :]
            )
    from_lane = lax.broadcasted_iota(jnp.int32, (128, 128), 0)
    to_lane = lax.broadcasted_iota(jnp.int32, (128, 128), 1)
    restricted = jnp.zeros((24, 128), jnp.float32)
    for pair in range(2):
        rows = jnp.concatenate(
            [
                halves[pl.ds((c * 2 + pair) * 16, 8, stride=2), :]
                + halves[pl.ds((c * 2 + pair) * 16 + 1, 8, stride=2), :]
                for c in range(3)
            ],
            axis=0,
        )
        pick = (lax.shift_right_logical(from_lane, 1) + 64 * pair == to_lane).astype(jnp.float32)
        restricted = restricted + lax.dot(
            rows, pick, precision=lax.Precision.HIGHEST, preferred_element_type=jnp.float32
        )
    restricted = restricted * RESTRICT_SCALE
    for f in range(5):
        gat[gz, f] = coarse[f]
    for c in range(3):
        gat[gz, 5 + c] = restricted[c * 8 : c * 8 + 8]

    pl.semaphore_wait(barrier, len(NEAR) + len(CLOSE))
    for step in (4, GX - 4):
        pl.semaphore_signal(far_sem, inc=1, device_id=along(step), device_id_type=MESH)

    def send(index, src, dst, device):
        copy = pltpu.make_async_remote_copy(
            src_ref=src, dst_ref=dst, send_sem=hs.at[index], recv_sem=hr.at[index],
            device_id=device, device_id_type=MESH,
        )
        copy.start()
        return copy

    for n, step in enumerate(NEAR):
        pltpu.make_async_remote_copy(
            src_ref=sp1.at[pl.ds(31, 1)], dst_ref=sp1.at[pl.ds(n, 1)], send_sem=s1_send,
            recv_sem=s1_recv, device_id=near(step), device_id_type=MESH,
        ).start()
    next_z, last_z = near((0, 1)), near((0, GZ - 1))
    next_x, last_x = along(1), along(GX - 1)
    next_y, last_y = near((1, 0)), near((GY - 1, 0))
    noise_z = [
        send(0, nz.at[:, pl.ds(4, 4)], nz.at[:, pl.ds(0, 4)], next_z),
        send(1, nz.at[:, pl.ds(4, 4)], nz.at[:, pl.ds(8, 4)], last_z),
    ]
    for step in range(1, GZ):
        pltpu.make_async_remote_copy(
            src_ref=gat.at[gz], dst_ref=gat.at[gz], send_sem=gat_send, recv_sem=gat_recv.at[step - 1],
            device_id=near((0, step)), device_id_type=MESH,
        ).start()

    for k in range(16):
        for group in range(2):
            ux[(3 + k) * 32 + group * 8 : (3 + k) * 32 + group * 8 + 8, :] = us[
                pl.ds(group * 128 + k, 8, stride=16), :
            ]
        ux[(3 + k) * 32 + 16 : (3 + k) * 32 + 20, :] = us[pl.ds(256 + k, 4, stride=16), :]
    for k in range(8):
        row = cp[pl.ds(k, 5, stride=8), :]
        ux[(3 + k) * 32 + 24 : (3 + k) * 32 + 29, :] = row
        ux[(11 + k) * 32 + 24 : (11 + k) * 32 + 29, :] = row
    state_x = [
        send(2, ux.at[pl.ds(16 * 32, 96)], ux.at[pl.ds(0, 96)], next_x),
        send(3, ux.at[pl.ds(3 * 32, 96)], ux.at[pl.ds(19 * 32, 96)], last_x),
    ]

    for t in range(2):
        ty[t, 8:136, :] = us[t * 128 : t * 128 + 128, :].T
        ty[3 + t, 8:136, :] = fy[t * 128 : t * 128 + 128, :].T
    tail = us[256:320, :]
    ty[2, 8:136, :] = jnp.concatenate([tail, tail], axis=0).T
    tail = fy[256:320, :]
    ty[5, 8:136, :] = jnp.concatenate([tail, tail], axis=0).T
    for f, entry in enumerate(flux_entries(coarse, coarse_inverse, coarse_pressure, 2)):
        fcp[f * 8 : f * 8 + 8, :] = entry
    for t, ref in ((6, cp), (7, fcp)):
        packed = ref[0:40, :]
        swapped = swap_halves(packed)
        front = jnp.where(first_half_40, packed, swapped)
        back = jnp.where(first_half_40, swapped, packed)
        ty[t, 8:136, :] = jnp.concatenate([front, front[0:24], back, back[0:24]], axis=0).T
    state_y = [
        send(4, ty.at[:, pl.ds(128, 8)], ty.at[:, pl.ds(0, 8)], next_y),
        send(5, ty.at[:, pl.ds(8, 8)], ty.at[:, pl.ds(136, 8)], last_y),
    ]
    state_z = [
        send(6, uz.at[:, pl.ds(4, 3)], uz.at[:, pl.ds(0, 3)], next_z),
        send(7, uz.at[:, pl.ds(3, 3)], uz.at[:, pl.ds(7, 3)], last_z),
    ]

    def flux_x(k, carry):
        base = k * 32
        state = [ux[pl.ds(base + 4 * f, 4), :] for f in range(5)]
        for f, entry in enumerate(flux_alone(state, 1)):
            fx[pl.ds(base + 4 * f, 4), :] = entry
        return carry

    lax.fori_loop(3, 19, flux_x, 0)
    for f, entry in enumerate(flux_entries(coarse, coarse_inverse, coarse_pressure, 1)):
        fcp[f * 8 : f * 8 + 8, :] = entry
    for k in range(8):
        fx[(3 + k) * 32 + 24 : (3 + k) * 32 + 29, :] = fcp[pl.ds(k, 5, stride=8), :]

    def total_wait(ref, count, send_sem, recv_sem):
        return pltpu.make_async_remote_copy(
            src_ref=ref.at[pl.ds(0, count)], dst_ref=ref.at[pl.ds(0, count)], send_sem=send_sem,
            recv_sem=recv_sem, device_id=next_x, device_id_type=MESH,
        )

    first_round = total_wait(sp1, 31, s1_send, s1_recv)
    first_round.wait_recv()
    sp2[15:16, :] = jnp.max(sp1[...], axis=0, keepdims=True)
    pl.semaphore_wait(far_sem, 2)
    for n, step in enumerate(ALONG):
        pltpu.make_async_remote_copy(
            src_ref=sp2.at[pl.ds(15, 1)], dst_ref=sp2.at[pl.ds(n, 1)], send_sem=s2_send,
            recv_sem=s2_recv, device_id=along(step), device_id_type=MESH,
        ).start()

    for copy in noise_z:
        copy.wait_recv()

    def noise_along_z(c, carry):
        for h in range(2):
            planes = [nz[c, z, h * 8 : h * 8 + 8, :] for z in range(12)]
            for z in range(4):
                total = taps[2, 0] * planes[z]
                for t in range(1, 9):
                    total = total + taps[2, t] * planes[z + t]
                nx[c * 4 + z, 8 + h * 8 : 16 + h * 8, :] = total
        return carry

    lax.fori_loop(0, 3, noise_along_z, 0)
    for step in range(1, GZ):
        origin = lax.rem(gz + GZ - step, GZ)
        pltpu.make_async_remote_copy(
            src_ref=gat.at[gz], dst_ref=gat.at[origin], send_sem=gat_send, recv_sem=gat_recv.at[step - 1],
            device_id=next_x, device_id_type=MESH,
        ).wait_recv()
    block = jnp.int32(0)
    for j in range(GZ):
        block = block + j * (owner[j] == gz).astype(jnp.int32)

    def mixed(left, right):
        return jnp.where(first_half, swap_halves(left), swap_halves(right))

    around = [lax.rem(block + GZ + m, GZ) for m in range(-2, 3)]
    for c in range(3):
        pairs = [gat[j, 5 + c] for j in around]
        total = taps[2, 0] * pairs[0]
        for t in range(1, 9):
            plane = pairs[t // 2] if t % 2 == 0 else mixed(pairs[t // 2], pairs[t // 2 + 1])
            total = total + taps[2, t] * plane
        nx[12 + c, 8:16, :] = total
        nx[12 + c, 16:24, :] = total
    noise_x = [
        send(8, nx.at[:, pl.ds(16, 8)], nx.at[:, pl.ds(0, 8)], next_x),
        send(9, nx.at[:, pl.ds(8, 8)], nx.at[:, pl.ds(24, 8)], last_x),
    ]

    for copy in state_x:
        copy.wait_recv()
    lax.fori_loop(0, 3, flux_x, 0)
    lax.fori_loop(19, 22, flux_x, 0)
    for k in (0, 1, 2, 19, 20, 21):
        state = [ux[k * 32 + 24 + f : k * 32 + 25 + f, :] for f in range(5)]
        target = k if k < 3 else k - 8
        for f, entry in enumerate(flux_alone(state, 1)):
            fx[target * 32 + 24 + f : target * 32 + 25 + f, :] = entry
    state_x[1].wait_send()
    state_x[0].wait_send()
    for k in (11, 12, 13):
        ux[k * 32 + 24 : k * 32 + 32, :] = ux[(k + 8) * 32 + 24 : (k + 8) * 32 + 32, :]

    def steps_x(k, carry):
        for n, ref in enumerate((fx, ux)):
            for group in range(3):
                d16[n, group, k] = ref[pl.ds((k + 1) * 32 + group * 8, 8), :] - ref[
                    pl.ds(k * 32 + group * 8, 8), :
                ]
        return carry

    lax.fori_loop(0, 21, steps_x, 0)
    for n, ref in enumerate((fx, ux)):
        for k in range(13):
            d8[n, 0, k] = ref[(k + 1) * 32 + 24 : (k + 1) * 32 + 32, :] - ref[k * 32 + 24 : k * 32 + 32, :]

    for copy in noise_x:
        copy.wait_recv()

    def noise_along_x(n, carry):
        total = taps[0, 0] * nx[n, 4:20, :]
        for t in range(1, 9):
            total = total + taps[0, t] * nx[n, 4 + t : 20 + t, :]
        wx[pl.ds(pl.multiple_of(n * 16, 16), 16), :] = total
        return carry

    lax.fori_loop(0, 12, noise_along_x, 0)
    for c in range(3):
        total = taps[0, 0] * nx[12 + c, 4:12, :]
        for t in range(1, 9):
            base = 4 + t if t <= 4 else 12 + t
            total = total + taps[0, t] * nx[12 + c, base : base + 8, :]
        swapped = swap_halves(total)
        wx[192 + c * 8 : 200 + c * 8, :] = jnp.where(first_half, total, swapped)
        wx[216 + c * 8 : 224 + c * 8, :] = jnp.where(first_half, swapped, total)
    for t in range(2):
        nt[t, 8:136, :] = wx[t * 128 : t * 128 + 128, :].T
    noise_y = [
        send(10, nt.at[:, pl.ds(128, 8)], nt.at[:, pl.ds(0, 8)], next_y),
        send(11, nt.at[:, pl.ds(8, 8)], nt.at[:, pl.ds(136, 8)], last_y),
    ]

    for copy in state_y:
        copy.wait_recv()
    for n in range(2):

        def steps_y(t, carry):
            rows = [ty[3 - 3 * n + t, pl.ds(5 + k, 8, stride=16), :] for k in range(22)]
            for k in range(21):
                d16[n, 3 + t, k] = rows[k + 1] - rows[k]
            return carry

        lax.fori_loop(0, 3, steps_y, 0)
    for copy in state_y:
        copy.wait_send()
    for n, t in enumerate((7, 6)):
        ty[t, 72:80, :] = ty[t, 136:144, :]
        rows = [ty[t, pl.ds(5 + k, 8, stride=8), :] for k in range(14)]
        for k in range(13):
            d8[n, 1, k] = rows[k + 1] - rows[k]

    for copy in state_z:
        copy.wait_recv()
    for k in (0, 1, 2, 7, 8, 9):
        state = [uz[f, k] for f in range(5)]
        for f, entry in enumerate(flux_alone(state, 3)):
            fz[f, k] = entry

    def steps_z(f, carry):
        for n, ref in enumerate((fz, uz)):
            for h in range(2):
                for k in range(9):
                    d4 = ref[f, k + 1, h * 8 : h * 8 + 8, :] - ref[f, k, h * 8 : h * 8 + 8, :]
                    dz[n, f * 2 + h, k] = d4
        return carry

    lax.fori_loop(0, 5, steps_z, 0)
    pairs_u, pairs_f = [], []
    for j in around:
        state = [gat[owner[j], f] for f in range(5)]
        pairs_u.append(state)
        pairs_f.append(flux_alone(state, 3))
    for n, pairs in enumerate((pairs_f, pairs_u)):
        for f in range(5):
            planes = []
            for j in range(-3, 4):
                m = (j + 4) // 2
                planes.append(pairs[m][f] if j % 2 == 0 else mixed(pairs[m][f], pairs[m + 1][f]))
            for k in range(6):
                d1[n, f, k] = planes[k + 1] - planes[k]

    for copy in noise_y:
        copy.wait_recv()
    total = taps[1, 0] * nt[0, 4:132, :]
    for t in range(1, 9):
        total = total + taps[1, t] * nt[0, 4 + t : 132 + t, :]
    force[0:128, :] = total.T
    left = taps[1, 0] * nt[1, 4:132, :]
    for t in range(1, 5):
        left = left + taps[1, t] * nt[1, 4 + t : 132 + t, :]
    total = left
    for t in range(5, 9):
        total = total + taps[1, t] * nt[1, 4 + t : 132 + t, :]
    own = left[0:64]
    for t in range(5, 9):
        own = own + taps[1, t] * nt[1, 68 + t : 132 + t, :]
    front = jnp.where(lax.broadcasted_iota(jnp.int32, (64, 128), 1) < 64, total[0:64], own)
    force[128:256, :] = jnp.concatenate([front, total[64:128]], axis=0).T

    second_round = total_wait(sp2, 15, s2_send, s2_recv)
    second_round.wait_recv()
    speeds = jnp.max(sp2[...], axis=0, keepdims=True)
    front_row = lax.broadcasted_iota(jnp.int32, (1, 128), 1) < 64
    speed_fine = jnp.broadcast_to(
        jnp.max(jnp.where(front_row, speeds, 0.0), axis=1, keepdims=True), (8, 128)
    )
    speed_coarse = jnp.broadcast_to(
        jnp.max(jnp.where(front_row, 0.0, speeds), axis=1, keepdims=True), (8, 128)
    )

    def sweep_16(g, carry):
        out = sweep([d16[0, g, k] for k in range(21)], [d16[1, g, k] for k in range(21)], speed_fine, 16)
        for k in range(16):
            a16[pl.ds(g * 128 + k, 8, stride=16), :] = out[k]
        return carry

    def sweep_4(g, carry):
        out = sweep([dz[0, g, k] for k in range(9)], [dz[1, g, k] for k in range(9)], speed_fine, 4)
        for z in range(4):
            az[g, z] = out[z]
        return carry

    def sweep_8(g, carry):
        out = sweep([d8[0, g, k] for k in range(13)], [d8[1, g, k] for k in range(13)], speed_coarse, 8)
        for k in range(8):
            a8[pl.ds(g * 64 + k, 8, stride=8), :] = out[k]
        return carry

    def sweep_1(g, carry):
        out = sweep([d1[0, g, k] for k in range(6)], [d1[1, g, k] for k in range(6)], speed_coarse, 1)
        a1[g] = out[0]
        return carry

    lax.fori_loop(0, 6, sweep_16, 0)
    lax.fori_loop(0, 10, sweep_4, 0)
    lax.fori_loop(0, 2, sweep_8, 0)
    lax.fori_loop(0, 5, sweep_1, 0)

    for t in range(3):
        wide = a16[384 + t * 128 : 512 + t * 128, :].T
        a16[384 + t * 128 : 512 + t * 128, :] = wide
    rate_fine = 0.1 / speed_fine
    rate_coarse = 0.1 / speed_coarse
    for z in range(4):
        for h in range(2):
            state, push = [], []
            for f in range(5):
                row = (f * 4 + z) * 16 + h * 8
                state.append(us[row : row + 8, :])
            for c in range(3):
                row = (c * 4 + z) * 16 + h * 8
                push.append(force[row : row + 8, :])
            work = state[1] * push[0] + state[2] * push[1] + state[3] * push[2]
            source = [None, state[0] * push[0], state[0] * push[1], state[0] * push[2], work]
            for f in range(5):
                row = (f * 4 + z) * 16 + h * 8
                change = -0.5 * (a16[row : row + 8, :] + a16[384 + row : 392 + row, :] + az[f * 2 + h, z])
                if source[f] is not None:
                    change = change + source[f]
                fine_out[row : row + 8, :] = 0.25 * state[f] + rate_fine * change

    along_y = a8[64:128, :]
    turned = jnp.concatenate([along_y, along_y], axis=0).T
    along_y = jnp.where(first_half_40, turned[0:40], turned[64:104])
    push = []
    for c in range(3):
        push.append(
            jnp.where(
                first_half,
                force[192 + c * 8 : 200 + c * 8, :],
                swap_halves(force[216 + c * 8 : 224 + c * 8, :]),
            )
        )
    state = [cp[f * 8 : f * 8 + 8, :] for f in range(5)]
    work = state[1] * push[0] + state[2] * push[1] + state[3] * push[2]
    source = [None, state[0] * push[0], state[0] * push[1], state[0] * push[2], work]
    for f in range(5):
        change = -0.5 * (a8[f * 8 : f * 8 + 8, :] + along_y[f * 8 : f * 8 + 8] + a1[f])
        if source[f] is not None:
            change = change + 2.0 * source[f]
        result = 0.25 * state[f] + rate_coarse * change
        coarse_out[f * 16 : f * 16 + 8, :] = result[:, 0:64]
        coarse_out[f * 16 + 8 : f * 16 + 16, :] = swap_halves(result)[:, 0:64]

    first_round.wait_send()
    second_round.wait_send()
    for copy in noise_z + state_z + noise_x + noise_y:
        copy.wait_send()
    pltpu.make_async_remote_copy(
        src_ref=gat.at[pl.ds(0, 7)], dst_ref=gat.at[pl.ds(0, 7)], send_sem=gat_send,
        recv_sem=gat_recv.at[0], device_id=next_x, device_id_type=MESH,
    ).wait_send()


def local(fine_start, fine_section, fine_noise, coarse_start, coarse_section, taps, owner):
    f32 = jnp.float32
    vmem = pl.BlockSpec(memory_space=pltpu.VMEM)
    smem = pl.BlockSpec(memory_space=pltpu.SMEM)
    dma = pltpu.SemaphoreType.DMA
    fine, coarse = pl.pallas_call(
        kernel,
        out_shape=(jax.ShapeDtypeStruct((320, 128), f32), jax.ShapeDtypeStruct((80, 64), f32)),
        in_specs=[vmem, vmem, vmem, smem, smem],
        out_specs=(vmem, vmem),
        scratch_shapes=[
            pltpu.VMEM((32, 128), f32),
            pltpu.VMEM((16, 128), f32),
            pltpu.VMEM((40, 128), f32),
            pltpu.VMEM((40, 128), f32),
            pltpu.VMEM((704, 128), f32),
            pltpu.VMEM((704, 128), f32),
            pltpu.VMEM((8, 144, 128), f32),
            pltpu.VMEM((320, 128), f32),
            pltpu.VMEM((5, 10, 16, 128), f32),
            pltpu.VMEM((5, 10, 16, 128), f32),
            pltpu.VMEM((3, 12, 16, 128), f32),
            pltpu.VMEM((8, 8, 8, 128), f32),
            pltpu.VMEM((15, 32, 128), f32),
            pltpu.VMEM((256, 128), f32),
            pltpu.VMEM((2, 144, 128), f32),
            pltpu.VMEM((256, 128), f32),
            pltpu.VMEM((96, 128), f32),
            pltpu.VMEM((2, 10, 9, 8, 128), f32),
            pltpu.VMEM((2, 6, 21, 8, 128), f32),
            pltpu.VMEM((2, 2, 13, 8, 128), f32),
            pltpu.VMEM((2, 5, 6, 8, 128), f32),
            pltpu.VMEM((10, 4, 8, 128), f32),
            pltpu.VMEM((768, 128), f32),
            pltpu.VMEM((128, 128), f32),
            pltpu.VMEM((5, 8, 128), f32),
            pltpu.SemaphoreType.REGULAR,
            dma, dma, dma, dma, dma, dma((7,)), dma((12,)), dma((12,)),
        ],
        compiler_params=pltpu.CompilerParams(
            collective_id=0, has_side_effects=True, vmem_limit_bytes=24 * 1024 * 1024
        ),
        name="section",
    )(
        fine_section.reshape(320, 128), fine_noise.reshape(192, 128), coarse_section.reshape(80, 64),
        taps, owner,
    )
    return (
        0.75 * fine_start + fine.reshape(fine_start.shape),
        0.75 * coarse_start + coarse.reshape(coarse_start.shape),
    )


def solution(mesh):
    cells = P(None, "gz", "gx", "gy")
    return jax.shard_map(
        local,
        mesh=mesh,
        in_specs=(cells, cells, cells, cells, cells, P(), P()),
        out_specs=(cells, cells),
        check_vma=False,
    )
```

```python
import jax
import jax.numpy as jnp
from jax import lax
from jax.experimental import pallas as pl
from jax.experimental.pallas import tpu as pltpu
from jax.sharding import PartitionSpec as P

MESH = pl.DeviceIdType.MESH
GX, GY, GZ = 16, 4, 8
GAMMA = 1.4
SPEED_EPS = 3e-06
RESTRICT_SCALE = 0.35355339059327373
NEAR = [(i, j) for i in range(GY) for j in range(GZ) if (i, j) != (0, 0)]
ALONG = [8, 7, 9, 6, 10, 5, 11, 4, 12, 3, 13, 2, 14, 1, 15]
CLOSE = [1, 2, 3, 4, 12, 13, 14, 15]
CORNERS = [(1, 1), (1, GY - 1), (GX - 1, 1), (GX - 1, GY - 1)]


def pressure_of(state, inverse):
    kinetic = 0.5 * (state[1] * state[1] + state[2] * state[2] + state[3] * state[3])
    return (GAMMA - 1.0) * (state[4] - kinetic * inverse)


def flux_entries(state, inverse, pressure, component):
    velocity = state[component] * inverse
    entries = [
        state[component],
        state[1] * velocity,
        state[2] * velocity,
        state[3] * velocity,
        (state[4] + pressure) * velocity,
    ]
    entries[component] = entries[component] + pressure
    return entries


def flux_alone(state, component):
    inverse = 1.0 / state[0]
    return flux_entries(state, inverse, pressure_of(state, inverse), component)


def fastest_of(state, inverse, pressure):
    largest = jnp.maximum(jnp.maximum(jnp.abs(state[1]), jnp.abs(state[2])), jnp.abs(state[3]))
    return largest * inverse + jnp.sqrt(GAMMA * pressure * inverse)


def side(low, mid, high, p, q, r, s):
    m0 = mid * high
    m1 = low * high
    m2 = low * mid
    w0 = m0 * m0
    w1 = 6.0 * (m1 * m1)
    w2 = 3.0 * (m2 * m2)
    total = w0 + w1 + w2
    sums = w0 * (5.0 * q - 2.0 * p) + w1 * (q + 2.0 * r) + w2 * (4.0 * r - s)
    guess = pl.reciprocal(total, approx=True)
    return sums * (guess * (2.0 - total * guess))


def indicators(steps):
    squares = [e * e for e in steps]
    low, mid, high = [], [], []
    for i in range(len(steps) - 1):
        cross = steps[i] * steps[i + 1]
        both = squares[i] + squares[i + 1] + SPEED_EPS
        base = both - 2.75 * cross
        low.append(base + 1.5 * squares[i + 1])
        high.append(base + 1.5 * squares[i])
        mid.append(both - 1.25 * cross)
    return low, mid, high


def sweep(flux_steps, state_steps, speed, cells):
    scaled = [speed * u for u in state_steps]
    up = [f + u for f, u in zip(flux_steps, scaled)]
    down = [f - u for f, u in zip(flux_steps, scaled)]
    low_u, mid_u, high_u = indicators(up)
    low_d, mid_d, high_d = indicators(down)
    faces = []
    for j in range(cells + 1):
        right = side(low_u[j], mid_u[j + 1], high_u[j + 2], up[j], up[j + 1], up[j + 2], up[j + 3])
        left = side(
            high_d[j + 3], mid_d[j + 2], low_d[j + 1], down[j + 4], down[j + 3], down[j + 2], down[j + 1]
        )
        faces.append(right - left)
    return [
        up[c + 2] + down[c + 3] + (faces[c + 1] - faces[c]) * (1.0 / 6.0) for c in range(cells)
    ]


def swap_halves(values):
    return pltpu.roll(values, 64, 1)


def kernel(
    us_hbm, noise_hbm, cs_hbm, taps_hbm, owner_hbm, fine_out, coarse_out,
    us, noise, cs, taps, owner, sp1, sp2, cp, fcp, ux, fx, ty, fy, uz, fz, nz, gs, gr, nx, pk, hb, wx, nt,
    force, halves, dz, d16, d8, d1, az, a16, a8, a1,
    ins, far_sem, s1_send, s1_recv, s2_send, s2_recv, gs_send, gs_recv, gr_send, gr_recv, hs, hr,
):
    loads = [
        pltpu.make_async_copy(src, dst, ins.at[n])
        for n, (src, dst) in enumerate(
            ((us_hbm, us), (cs_hbm, cs), (noise_hbm, noise), (taps_hbm, taps), (owner_hbm, owner))
        )
    ]
    for load in loads:
        load.start()
    gx, gy, gz = lax.axis_index("gx"), lax.axis_index("gy"), lax.axis_index("gz")

    def near(step):
        return {"gy": lax.rem(gy + step[0], GY), "gz": lax.rem(gz + step[1], GZ)}

    def along(step):
        return {"gx": lax.rem(gx + step, GX)}

    def corner(step):
        return {"gx": lax.rem(gx + step[0], GX), "gy": lax.rem(gy + step[1], GY)}

    barrier = pltpu.get_barrier_semaphore()
    greeted = [near(step) for step in NEAR] + [along(step) for step in CLOSE] + [corner(step) for step in CORNERS]
    for device in greeted:
        pl.semaphore_signal(barrier, inc=1, device_id=device, device_id_type=MESH)

    lane = lax.broadcasted_iota(jnp.int32, (8, 128), 1)
    first_half = lane < 64
    first_half_40 = lax.broadcasted_iota(jnp.int32, (40, 128), 1) < 64

    loads[0].wait()
    best = jnp.zeros((16, 128), jnp.float32)
    for z in range(4):
        state = [us[(f * 4 + z) * 16 : (f * 4 + z) * 16 + 16, :] for f in range(5)]
        inverse = 1.0 / state[0]
        pressure = pressure_of(state, inverse)
        best = jnp.maximum(best, fastest_of(state, inverse, pressure))
        for f, entry in enumerate(flux_entries(state, inverse, pressure, 2)):
            fy[(f * 4 + z) * 16 : (f * 4 + z) * 16 + 16, :] = entry
        for f, entry in enumerate(flux_entries(state, inverse, pressure, 3)):
            fz[f, 3 + z] = entry
        for f in range(5):
            uz[f, 3 + z] = state[f]
    best = jnp.maximum(best[0:8], best[8:16])
    loads[1].wait()
    for f in range(5):
        cp[f * 8 : f * 8 + 8, :] = jnp.concatenate(
            [cs[f * 16 : f * 16 + 8, :], cs[f * 16 + 8 : f * 16 + 16, :]], axis=1
        )
    coarse = [cp[f * 8 : f * 8 + 8, :] for f in range(5)]
    coarse_inverse = 1.0 / coarse[0]
    coarse_pressure = pressure_of(coarse, coarse_inverse)
    coarse_best = fastest_of(coarse, coarse_inverse, coarse_pressure)
    best = jnp.where(
        first_half,
        jnp.maximum(best, swap_halves(best)),
        jnp.maximum(coarse_best, swap_halves(coarse_best)),
    )
    sp1[31:32, :] = jnp.max(best, axis=0, keepdims=True)

    for load in loads[2:]:
        load.wait()
    eighth = jnp.bitwise_and(lane, 7)
    group_of_lane = lax.shift_right_logical(lane, 3)
    packed = [jnp.zeros((8, 128), jnp.float32) for _ in range(2)]
    for c in range(3):
        for z in range(4):
            n = c * 4 + z
            for h in range(2):
                tile = noise[n * 16 + h * 8 : n * 16 + h * 8 + 8, :]
                nx[n, 8 + h * 8 : 16 + h * 8, :] = tile
                packed[h] = jnp.where(group_of_lane == n, pltpu.roll(tile, (n * 8 + 4) % 128, 1), packed[h])
        for pair in range(2):
            row = (c * 4 + 2 * pair) * 16
            halves[(c * 2 + pair) * 16 : (c * 2 + pair) * 16 + 16, :] = (
                noise[row : row + 16, :] + noise[row + 16 : row + 32, :]
            )
    for h in range(2):
        pk[0, h * 8 : h * 8 + 8, :] = packed[h]
    from_lane = lax.broadcasted_iota(jnp.int32, (128, 128), 0)
    to_lane = lax.broadcasted_iota(jnp.int32, (128, 128), 1)
    restricted = jnp.zeros((24, 128), jnp.float32)
    for pair in range(2):
        rows = jnp.concatenate(
            [
                halves[pl.ds((c * 2 + pair) * 16, 8, stride=2), :]
                + halves[pl.ds((c * 2 + pair) * 16 + 1, 8, stride=2), :]
                for c in range(3)
            ],
            axis=0,
        )
        pick = (lax.shift_right_logical(from_lane, 1) + 64 * pair == to_lane).astype(jnp.float32)
        restricted = restricted + lax.dot(
            rows, pick, precision=lax.Precision.HIGHEST, preferred_element_type=jnp.float32
        )
    restricted = restricted * RESTRICT_SCALE
    coarse_packed = jnp.zeros((8, 128), jnp.float32)
    for c in range(3):
        tile = restricted[c * 8 : c * 8 + 8]
        nx[12 + c, 8:16, :] = tile
        nx[12 + c, 16:24, :] = tile
        swapped = swap_halves(tile)
        for p in range(2):
            m = c * 2 + p
            doubled = jnp.where(first_half, tile, swapped) if p == 0 else jnp.where(first_half, swapped, tile)
            coarse_packed = jnp.where(group_of_lane == m, pltpu.roll(doubled, m * 8 + 4, 1), coarse_packed)
    pk[1, 0:8, :] = coarse_packed
    pk[1, 8:16, :] = coarse_packed
    for f in range(5):
        gs[gz, f] = coarse[f]

    for k in range(16):
        for group in range(2):
            ux[(3 + k) * 32 + group * 8 : (3 + k) * 32 + group * 8 + 8, :] = us[
                pl.ds(group * 128 + k, 8, stride=16), :
            ]
        ux[(3 + k) * 32 + 16 : (3 + k) * 32 + 20, :] = us[pl.ds(256 + k, 4, stride=16), :]
    for k in range(8):
        row = cp[pl.ds(k, 5, stride=8), :]
        ux[(3 + k) * 32 + 24 : (3 + k) * 32 + 29, :] = row
        ux[(11 + k) * 32 + 24 : (11 + k) * 32 + 29, :] = row

    for t in range(2):
        ty[t, 8:136, :] = us[t * 128 : t * 128 + 128, :].T
        ty[3 + t, 8:136, :] = fy[t * 128 : t * 128 + 128, :].T
    tail = us[256:320, :]
    ty[2, 8:136, :] = jnp.concatenate([tail, tail], axis=0).T
    tail = fy[256:320, :]
    ty[5, 8:136, :] = jnp.concatenate([tail, tail], axis=0).T
    for f, entry in enumerate(flux_entries(coarse, coarse_inverse, coarse_pressure, 2)):
        fcp[f * 8 : f * 8 + 8, :] = entry
    for t, ref in ((6, cp), (7, fcp)):
        both = ref[0:40, :]
        swapped = swap_halves(both)
        front = jnp.where(first_half_40, both, swapped)
        back = jnp.where(first_half_40, swapped, both)
        ty[t, 8:136, :] = jnp.concatenate([front, front[0:24], back, back[0:24]], axis=0).T

    pl.semaphore_wait(barrier, len(greeted))
    next_z, last_z = near((0, 1)), near((0, GZ - 1))
    next_x, last_x = along(1), along(GX - 1)
    next_y, last_y = near((1, 0)), near((GY - 1, 0))

    def send(index, src, dst, device):
        copy = pltpu.make_async_remote_copy(
            src_ref=src, dst_ref=dst, send_sem=hs.at[index], recv_sem=hr.at[index],
            device_id=device, device_id_type=MESH,
        )
        copy.start()
        return copy

    for n, step in enumerate(NEAR):
        pltpu.make_async_remote_copy(
            src_ref=sp1.at[pl.ds(31, 1)], dst_ref=sp1.at[pl.ds(n, 1)], send_sem=s1_send,
            recv_sem=s1_recv, device_id=near(step), device_id_type=MESH,
        ).start()
    for step in (4, GX - 4):
        pl.semaphore_signal(far_sem, inc=1, device_id=along(step), device_id_type=MESH)
    noise_xy = [
        send(0, nx.at[:, pl.ds(16, 8)], nx.at[:, pl.ds(0, 8)], next_x),
        send(1, nx.at[:, pl.ds(8, 8)], nx.at[:, pl.ds(24, 8)], last_x),
        send(2, pk, hb.at[0, :, pl.ds(8, 16)], next_y),
        send(3, pk, hb.at[1, :, pl.ds(8, 16)], last_y),
        send(4, pk.at[:, pl.ds(8, 8)], hb.at[0, :, pl.ds(0, 8)], corner(CORNERS[0])),
        send(5, pk.at[:, pl.ds(8, 8)], hb.at[1, :, pl.ds(0, 8)], corner(CORNERS[1])),
        send(6, pk.at[:, pl.ds(0, 8)], hb.at[0, :, pl.ds(24, 8)], corner(CORNERS[2])),
        send(7, pk.at[:, pl.ds(0, 8)], hb.at[1, :, pl.ds(24, 8)], corner(CORNERS[3])),
    ]
    state_x = [
        send(8, ux.at[pl.ds(16 * 32, 96)], ux.at[pl.ds(0, 96)], next_x),
        send(9, ux.at[pl.ds(3 * 32, 96)], ux.at[pl.ds(19 * 32, 96)], last_x),
    ]
    state_y = [
        send(10, ty.at[:, pl.ds(128, 8)], ty.at[:, pl.ds(0, 8)], next_y),
        send(11, ty.at[:, pl.ds(8, 8)], ty.at[:, pl.ds(136, 8)], last_y),
    ]
    state_z = [
        send(12, uz.at[:, pl.ds(4, 3)], uz.at[:, pl.ds(0, 3)], next_z),
        send(13, uz.at[:, pl.ds(3, 3)], uz.at[:, pl.ds(7, 3)], last_z),
    ]

    def column(ref, send_sem, recv_sem):
        copies = []
        for step in range(1, GZ):
            copy = pltpu.make_async_remote_copy(
                src_ref=ref.at[gz], dst_ref=ref.at[gz], send_sem=send_sem, recv_sem=recv_sem.at[step - 1],
                device_id=near((0, step)), device_id_type=MESH,
            )
            copy.start()
            origin = lax.rem(gz + GZ - step, GZ)
            copies.append(
                pltpu.make_async_remote_copy(
                    src_ref=ref.at[gz], dst_ref=ref.at[origin], send_sem=send_sem,
                    recv_sem=recv_sem.at[step - 1], device_id=next_z, device_id_type=MESH,
                )
            )
        whole = pltpu.make_async_remote_copy(
            src_ref=ref.at[pl.ds(0, GZ - 1)], dst_ref=ref.at[pl.ds(0, GZ - 1)], send_sem=send_sem,
            recv_sem=recv_sem.at[0], device_id=next_z, device_id_type=MESH,
        )
        return copies, whole

    state_column, state_column_sent = column(gs, gs_send, gs_recv)

    def flux_x(k, carry):
        base = k * 32
        state = [ux[pl.ds(base + 4 * f, 4), :] for f in range(5)]
        for f, entry in enumerate(flux_alone(state, 1)):
            fx[pl.ds(base + 4 * f, 4), :] = entry
        return carry

    lax.fori_loop(3, 19, flux_x, 0)
    for f, entry in enumerate(flux_entries(coarse, coarse_inverse, coarse_pressure, 1)):
        fcp[f * 8 : f * 8 + 8, :] = entry
    for k in range(8):
        fx[(3 + k) * 32 + 24 : (3 + k) * 32 + 29, :] = fcp[pl.ds(k, 5, stride=8), :]

    def total_wait(ref, count, send_sem, recv_sem):
        return pltpu.make_async_remote_copy(
            src_ref=ref.at[pl.ds(0, count)], dst_ref=ref.at[pl.ds(0, count)], send_sem=send_sem,
            recv_sem=recv_sem, device_id=next_x, device_id_type=MESH,
        )

    first_round = total_wait(sp1, 31, s1_send, s1_recv)
    first_round.wait_recv()
    sp2[15:16, :] = jnp.max(sp1[...], axis=0, keepdims=True)
    pl.semaphore_wait(far_sem, 2)
    for n, step in enumerate(ALONG):
        pltpu.make_async_remote_copy(
            src_ref=sp2.at[pl.ds(15, 1)], dst_ref=sp2.at[pl.ds(n, 1)], send_sem=s2_send,
            recv_sem=s2_recv, device_id=along(step), device_id_type=MESH,
        ).start()

    for copy in noise_xy:
        copy.wait_recv()

    def noise_along_x(n, carry):
        total = taps[0, 0] * nx[n, 4:20, :]
        for t in range(1, 9):
            total = total + taps[0, t] * nx[n, 4 + t : 20 + t, :]
        wx[pl.ds(pl.multiple_of(n * 16, 16), 16), :] = total
        return carry

    lax.fori_loop(0, 12, noise_along_x, 0)
    for c in range(3):
        total = taps[0, 0] * nx[12 + c, 4:12, :]
        for t in range(1, 9):
            base = 4 + t if t <= 4 else 12 + t
            total = total + taps[0, t] * nx[12 + c, base : base + 8, :]
        swapped = swap_halves(total)
        wx[192 + c * 8 : 200 + c * 8, :] = jnp.where(first_half, total, swapped)
        wx[216 + c * 8 : 224 + c * 8, :] = jnp.where(first_half, swapped, total)
    for b in range(2):
        for r in range(4):
            hb[0, b, r * 8 : r * 8 + 8, :] = jnp.where(
                eighth < 4, hb[0, b, r * 8 : r * 8 + 8, :], hb[1, b, r * 8 : r * 8 + 8, :]
            )
    beside = taps[0, 0] * hb[0, 0, 4:20, :]
    for t in range(1, 9):
        beside = beside + taps[0, t] * hb[0, 0, 4 + t : 20 + t, :]
    coarse_beside = taps[0, 0] * hb[0, 1, 4:12, :]
    for t in range(1, 9):
        base = 4 + t if t <= 4 else 12 + t
        coarse_beside = coarse_beside + taps[0, t] * hb[0, 1, base : base + 8, :]

    turned = jnp.concatenate([beside, coarse_beside, jnp.zeros((104, 128), jnp.float32)], axis=0).T
    rims = [jnp.zeros((8, 128), jnp.float32) for _ in range(2)]
    sixteenth = lax.shift_right_logical(lane, 4)
    for n in range(12):
        shift = (n % 8) * 16
        rolled = pltpu.roll(turned[n * 8 : n * 8 + 8], shift, 1) if shift else turned[n * 8 : n * 8 + 8]
        rims[n // 8] = jnp.where(sixteenth == n % 8, rolled, rims[n // 8])
    for c in range(3):
        for p in range(2):
            m = c * 2 + p
            target = 64 + p * 24 + c * 8
            rolled = pltpu.roll(turned[m * 8 : m * 8 + 8], target - 16, 1)
            rims[1] = jnp.where(group_of_lane == target // 8, rolled, rims[1])
    for t in range(2):
        nt[t, 8:136, :] = wx[t * 128 : t * 128 + 128, :].T
        nt[t, 4:8, :] = rims[t][0:4]
        nt[t, 136:140, :] = rims[t][4:8]
    total = taps[1, 0] * nt[0, 4:132, :]
    for t in range(1, 9):
        total = total + taps[1, t] * nt[0, 4 + t : 132 + t, :]
    total = total.T
    for n in range(8):
        nz[n // 4, 4 + n % 4] = total[n * 16 : n * 16 + 16]
    left = taps[1, 0] * nt[1, 4:132, :]
    for t in range(1, 5):
        left = left + taps[1, t] * nt[1, 4 + t : 132 + t, :]
    total = left
    for t in range(5, 9):
        total = total + taps[1, t] * nt[1, 4 + t : 132 + t, :]
    own = left[0:64]
    for t in range(5, 9):
        own = own + taps[1, t] * nt[1, 68 + t : 132 + t, :]
    front = jnp.where(lax.broadcasted_iota(jnp.int32, (64, 128), 1) < 64, total[0:64], own)
    total = jnp.concatenate([front, total[64:128]], axis=0).T
    for n in range(8, 12):
        nz[n // 4, 4 + n % 4] = total[(n - 8) * 16 : (n - 8) * 16 + 16]
    for c in range(3):
        gr[gz, c] = jnp.where(
            first_half, total[64 + c * 8 : 72 + c * 8], swap_halves(total[88 + c * 8 : 96 + c * 8])
        )
    noise_z = [
        send(14, nz.at[:, pl.ds(4, 4)], nz.at[:, pl.ds(0, 4)], next_z),
        send(15, nz.at[:, pl.ds(4, 4)], nz.at[:, pl.ds(8, 4)], last_z),
    ]
    noise_column, noise_column_sent = column(gr, gr_send, gr_recv)

    for copy in state_x:
        copy.wait_recv()
    lax.fori_loop(0, 3, flux_x, 0)
    lax.fori_loop(19, 22, flux_x, 0)
    for k in (0, 1, 2, 19, 20, 21):
        state = [ux[k * 32 + 24 + f : k * 32 + 25 + f, :] for f in range(5)]
        target = k if k < 3 else k - 8
        for f, entry in enumerate(flux_alone(state, 1)):
            fx[target * 32 + 24 + f : target * 32 + 25 + f, :] = entry
    for copy in state_x:
        copy.wait_send()
    for k in (11, 12, 13):
        ux[k * 32 + 24 : k * 32 + 32, :] = ux[(k + 8) * 32 + 24 : (k + 8) * 32 + 32, :]

    def steps_x(k, carry):
        for n, ref in enumerate((fx, ux)):
            for group in range(3):
                d16[n, group, k] = ref[pl.ds((k + 1) * 32 + group * 8, 8), :] - ref[
                    pl.ds(k * 32 + group * 8, 8), :
                ]
        return carry

    lax.fori_loop(0, 21, steps_x, 0)
    for n, ref in enumerate((fx, ux)):
        for k in range(13):
            d8[n, 0, k] = ref[(k + 1) * 32 + 24 : (k + 1) * 32 + 32, :] - ref[k * 32 + 24 : k * 32 + 32, :]

    for copy in state_y:
        copy.wait_recv()
    for n in range(2):

        def steps_y(t, carry):
            rows = [ty[3 - 3 * n + t, pl.ds(5 + k, 8, stride=16), :] for k in range(22)]
            for k in range(21):
                d16[n, 3 + t, k] = rows[k + 1] - rows[k]
            return carry

        lax.fori_loop(0, 3, steps_y, 0)
    for copy in state_y:
        copy.wait_send()
    for n, t in enumerate((7, 6)):
        ty[t, 72:80, :] = ty[t, 136:144, :]
        rows = [ty[t, pl.ds(5 + k, 8, stride=8), :] for k in range(14)]
        for k in range(13):
            d8[n, 1, k] = rows[k + 1] - rows[k]

    for copy in state_z:
        copy.wait_recv()
    for k in (0, 1, 2, 7, 8, 9):
        state = [uz[f, k] for f in range(5)]
        for f, entry in enumerate(flux_alone(state, 3)):
            fz[f, k] = entry

    def steps_z(f, carry):
        for n, ref in enumerate((fz, uz)):
            for h in range(2):
                for k in range(9):
                    d4 = ref[f, k + 1, h * 8 : h * 8 + 8, :] - ref[f, k, h * 8 : h * 8 + 8, :]
                    dz[n, f * 2 + h, k] = d4
        return carry

    lax.fori_loop(0, 5, steps_z, 0)
    block = jnp.int32(0)
    for j in range(GZ):
        block = block + j * (owner[j] == gz).astype(jnp.int32)

    def mixed(left, right):
        return jnp.where(first_half, swap_halves(left), swap_halves(right))

    around = [lax.rem(block + GZ + m, GZ) for m in range(-2, 3)]
    for copy in state_column:
        copy.wait_recv()
    pairs_u, pairs_f = [], []
    for j in around:
        state = [gs[owner[j], f] for f in range(5)]
        pairs_u.append(state)
        pairs_f.append(flux_alone(state, 3))
    for n, pairs in enumerate((pairs_f, pairs_u)):
        for f in range(5):
            planes = []
            for j in range(-3, 4):
                m = (j + 4) // 2
                planes.append(pairs[m][f] if j % 2 == 0 else mixed(pairs[m][f], pairs[m + 1][f]))
            for k in range(6):
                d1[n, f, k] = planes[k + 1] - planes[k]

    for copy in noise_z:
        copy.wait_recv()
    for h in range(2):

        def noise_along_z(c, carry):
            planes = [nz[c, z, h * 8 : h * 8 + 8, :] for z in range(12)]
            for z in range(4):
                total = taps[2, 0] * planes[z]
                for t in range(1, 9):
                    total = total + taps[2, t] * planes[z + t]
                force[c * 4 + z, h * 8 : h * 8 + 8, :] = total
            return carry

        lax.fori_loop(0, 3, noise_along_z, 0)

    def sources(z, carry):
        state = [us[pl.ds(pl.multiple_of((f * 4 + z) * 16, 16), 16), :] for f in range(4)]
        push = [force[c * 4 + z] for c in range(3)]
        for c in range(3):
            force[c * 4 + z] = state[0] * push[c]
        force[12 + z] = state[1] * push[0] + state[2] * push[1] + state[3] * push[2]
        return carry

    lax.fori_loop(0, 4, sources, 0)
    for copy in noise_column:
        copy.wait_recv()
    push = []
    for c in range(3):
        pairs = [gr[j, c] for j in around]
        total = taps[2, 0] * pairs[0]
        for t in range(1, 9):
            plane = pairs[t // 2] if t % 2 == 0 else mixed(pairs[t // 2], pairs[t // 2 + 1])
            total = total + taps[2, t] * plane
        push.append(2.0 * total)
    work = coarse[1] * push[0] + coarse[2] * push[1] + coarse[3] * push[2]
    coarse_source = [None, coarse[0] * push[0], coarse[0] * push[1], coarse[0] * push[2], work]
    for f in range(1, 5):
        fcp[f * 8 : f * 8 + 8, :] = coarse_source[f]

    second_round = total_wait(sp2, 15, s2_send, s2_recv)
    second_round.wait_recv()
    speeds = jnp.max(sp2[...], axis=0, keepdims=True)
    front_row = lax.broadcasted_iota(jnp.int32, (1, 128), 1) < 64
    speed_fine = jnp.broadcast_to(
        jnp.max(jnp.where(front_row, speeds, 0.0), axis=1, keepdims=True), (8, 128)
    )
    speed_coarse = jnp.broadcast_to(
        jnp.max(jnp.where(front_row, 0.0, speeds), axis=1, keepdims=True), (8, 128)
    )

    def sweep_16(g, carry):
        out = sweep([d16[0, g, k] for k in range(21)], [d16[1, g, k] for k in range(21)], speed_fine, 16)
        for k in range(16):
            a16[pl.ds(g * 128 + k, 8, stride=16), :] = out[k]
        return carry

    def sweep_4(g, carry):
        out = sweep([dz[0, g, k] for k in range(9)], [dz[1, g, k] for k in range(9)], speed_fine, 4)
        for z in range(4):
            az[g, z] = out[z]
        return carry

    def sweep_8(g, carry):
        out = sweep([d8[0, g, k] for k in range(13)], [d8[1, g, k] for k in range(13)], speed_coarse, 8)
        for k in range(8):
            a8[pl.ds(g * 64 + k, 8, stride=8), :] = out[k]
        return carry

    def sweep_1(g, carry):
        out = sweep([d1[0, g, k] for k in range(6)], [d1[1, g, k] for k in range(6)], speed_coarse, 1)
        a1[g] = out[0]
        return carry

    lax.fori_loop(0, 6, sweep_16, 0)
    lax.fori_loop(0, 10, sweep_4, 0)
    lax.fori_loop(0, 2, sweep_8, 0)
    lax.fori_loop(0, 5, sweep_1, 0)

    rate_fine = 0.1 / speed_fine
    rate_coarse = 0.1 / speed_coarse
    for t in range(3):
        wide = a16[384 + t * 128 : 512 + t * 128, :].T
        for tile in range(16 if t < 2 else 8):
            index = t * 16 + tile
            f, z, h = index // 8, (index // 2) % 4, index % 2
            row = index * 8
            change = -0.5 * (a16[row : row + 8, :] + wide[tile * 8 : tile * 8 + 8] + az[f * 2 + h, z])
            if f > 0:
                change = change + force[(f - 1) * 4 + z, h * 8 : h * 8 + 8, :]
            fine_out[row : row + 8, :] = 0.25 * us[row : row + 8, :] + rate_fine * change

    along_y = a8[64:128, :]
    turned = jnp.concatenate([along_y, along_y], axis=0).T
    along_y = jnp.where(first_half_40, turned[0:40], turned[64:104])
    for f in range(5):
        change = -0.5 * (a8[f * 8 : f * 8 + 8, :] + along_y[f * 8 : f * 8 + 8] + a1[f])
        if f > 0:
            change = change + fcp[f * 8 : f * 8 + 8, :]
        result = 0.25 * cp[f * 8 : f * 8 + 8, :] + rate_coarse * change
        coarse_out[f * 16 : f * 16 + 8, :] = result[:, 0:64]
        coarse_out[f * 16 + 8 : f * 16 + 16, :] = swap_halves(result)[:, 0:64]

    first_round.wait_send()
    second_round.wait_send()
    for copy in noise_xy + state_z + noise_z:
        copy.wait_send()
    state_column_sent.wait_send()
    noise_column_sent.wait_send()


def local(fine_start, fine_section, fine_noise, coarse_start, coarse_section, taps, owner):
    f32 = jnp.float32
    vmem = pl.BlockSpec(memory_space=pltpu.VMEM)
    hbm = pl.BlockSpec(memory_space=pltpu.HBM)
    dma = pltpu.SemaphoreType.DMA
    fine, coarse = pl.pallas_call(
        kernel,
        out_shape=(jax.ShapeDtypeStruct((320, 128), f32), jax.ShapeDtypeStruct((80, 64), f32)),
        in_specs=[hbm] * 5,
        out_specs=(vmem, vmem),
        scratch_shapes=[
            pltpu.VMEM((320, 128), f32),
            pltpu.VMEM((192, 128), f32),
            pltpu.VMEM((80, 64), f32),
            pltpu.SMEM((3, 9), f32),
            pltpu.SMEM((8,), jnp.int32),
            pltpu.VMEM((32, 128), f32),
            pltpu.VMEM((16, 128), f32),
            pltpu.VMEM((40, 128), f32),
            pltpu.VMEM((40, 128), f32),
            pltpu.VMEM((704, 128), f32),
            pltpu.VMEM((704, 128), f32),
            pltpu.VMEM((8, 144, 128), f32),
            pltpu.VMEM((320, 128), f32),
            pltpu.VMEM((5, 10, 16, 128), f32),
            pltpu.VMEM((5, 10, 16, 128), f32),
            pltpu.VMEM((3, 12, 16, 128), f32),
            pltpu.VMEM((8, 5, 8, 128), f32),
            pltpu.VMEM((8, 3, 8, 128), f32),
            pltpu.VMEM((15, 32, 128), f32),
            pltpu.VMEM((2, 16, 128), f32),
            pltpu.VMEM((2, 2, 32, 128), f32),
            pltpu.VMEM((256, 128), f32),
            pltpu.VMEM((2, 144, 128), f32),
            pltpu.VMEM((16, 16, 128), f32),
            pltpu.VMEM((96, 128), f32),
            pltpu.VMEM((2, 10, 9, 8, 128), f32),
            pltpu.VMEM((2, 6, 21, 8, 128), f32),
            pltpu.VMEM((2, 2, 13, 8, 128), f32),
            pltpu.VMEM((2, 5, 6, 8, 128), f32),
            pltpu.VMEM((10, 4, 8, 128), f32),
            pltpu.VMEM((768, 128), f32),
            pltpu.VMEM((128, 128), f32),
            pltpu.VMEM((5, 8, 128), f32),
            dma((5,)),
            pltpu.SemaphoreType.REGULAR,
            dma, dma, dma, dma, dma, dma((7,)), dma, dma((7,)), dma((16,)), dma((16,)),
        ],
        compiler_params=pltpu.CompilerParams(
            collective_id=0, has_side_effects=True, vmem_limit_bytes=24 * 1024 * 1024
        ),
        name="section",
    )(
        *(
            pltpu.with_memory_space_constraint(operand, pltpu.HBM)
            for operand in (
                fine_section.reshape(320, 128), fine_noise.reshape(192, 128),
                coarse_section.reshape(80, 64), taps, owner,
            )
        )
    )
    return (
        0.75 * fine_start + fine.reshape(fine_start.shape),
        0.75 * coarse_start + coarse.reshape(coarse_start.shape),
    )


def solution(mesh):
    cells = P(None, "gz", "gx", "gy")
    return jax.shard_map(
        local,
        mesh=mesh,
        in_specs=(cells, cells, cells, cells, cells, P(), P()),
        out_specs=(cells, cells),
        check_vma=False,
    )
```

```python
import jax
import jax.numpy as jnp
from jax import lax
from jax.experimental import pallas as pl
from jax.experimental.pallas import tpu as pltpu
from jax.sharding import PartitionSpec as P

MESH = pl.DeviceIdType.MESH
GX, GY, GZ = 16, 4, 8
GAMMA = 1.4
SPEED_EPS = 3e-06
RESTRICT_SCALE = 0.35355339059327373
NEAR = sorted(
    ((i, j) for i in range(GY) for j in range(GZ) if (i, j) != (0, 0)),
    key=lambda step: -((step[0] + 1) // 2 % 2 + 2 * (step[1] // 4) + min(step[1] % 4, -step[1] % 4)),
)
ALONG = [8, 7, 9, 6, 10, 5, 11, 4, 12, 3, 13, 2, 14, 1, 15]
CLOSE = [4, 12, 3, 13, 2, 14, 1, 15]
CORNERS = [(1, 1), (1, GY - 1), (GX - 1, 1), (GX - 1, GY - 1)]


def pressure_of(state, inverse):
    kinetic = 0.5 * (state[1] * state[1] + state[2] * state[2] + state[3] * state[3])
    return (GAMMA - 1.0) * (state[4] - kinetic * inverse)


def flux_entries(state, inverse, pressure, component):
    velocity = state[component] * inverse
    entries = [
        state[component],
        state[1] * velocity,
        state[2] * velocity,
        state[3] * velocity,
        (state[4] + pressure) * velocity,
    ]
    entries[component] = entries[component] + pressure
    return entries


def flux_alone(state, component):
    inverse = 1.0 / state[0]
    return flux_entries(state, inverse, pressure_of(state, inverse), component)


def fastest_of(state, inverse, pressure):
    largest = jnp.maximum(jnp.maximum(jnp.abs(state[1]), jnp.abs(state[2])), jnp.abs(state[3]))
    return largest * inverse + jnp.sqrt(GAMMA * pressure * inverse)


def side(low, mid, high, p, q, r, s):
    m0 = mid * high
    m1 = low * high
    m2 = low * mid
    w0 = m0 * m0
    w1 = 6.0 * (m1 * m1)
    w2 = 3.0 * (m2 * m2)
    total = w0 + w1 + w2
    sums = w0 * (5.0 * q - 2.0 * p) + w1 * (q + 2.0 * r) + w2 * (4.0 * r - s)
    guess = pl.reciprocal(total, approx=True)
    return sums * (guess * (2.0 - total * guess))


def indicators(steps):
    squares = [e * e for e in steps]
    low, mid, high = [], [], []
    for i in range(len(steps) - 1):
        cross = steps[i] * steps[i + 1]
        both = squares[i] + squares[i + 1] + SPEED_EPS
        base = both - 2.75 * cross
        low.append(base + 1.5 * squares[i + 1])
        high.append(base + 1.5 * squares[i])
        mid.append(both - 1.25 * cross)
    return low, mid, high


def sweep(flux_steps, state_steps, speed, cells):
    scaled = [speed * u for u in state_steps]
    up = [f + u for f, u in zip(flux_steps, scaled)]
    down = [f - u for f, u in zip(flux_steps, scaled)]
    low_u, mid_u, high_u = indicators(up)
    low_d, mid_d, high_d = indicators(down)
    faces = []
    for j in range(cells + 1):
        right = side(low_u[j], mid_u[j + 1], high_u[j + 2], up[j], up[j + 1], up[j + 2], up[j + 3])
        left = side(
            high_d[j + 3], mid_d[j + 2], low_d[j + 1], down[j + 4], down[j + 3], down[j + 2], down[j + 1]
        )
        faces.append(right - left)
    return [
        up[c + 2] + down[c + 3] + (faces[c + 1] - faces[c]) * (1.0 / 6.0) for c in range(cells)
    ]


def swap_halves(values):
    return pltpu.roll(values, 64, 1)


def kernel(
    us_hbm, noise_hbm, cs_hbm, taps_hbm, owner_hbm, fine_out, coarse_out,
    us, noise, cs, taps, owner, sp1, sp2, cp, fcp, ux, fx, ty, fy, uz, fz, nz, gs, gr, nx, pk, hb, wx, nt,
    force, halves, dz, d16, d8, d1, az, a16, a8, a1,
    ins, far_sem, s1_send, s1_recv, s2_send, s2_recv, gs_send, gs_recv, gr_send, gr_recv, hs, hr,
):
    loads = [
        pltpu.make_async_copy(src, dst, ins.at[n])
        for n, (src, dst) in enumerate(
            ((us_hbm, us), (cs_hbm, cs), (noise_hbm, noise), (taps_hbm, taps), (owner_hbm, owner))
        )
    ]
    for load in loads:
        load.start()
    gx, gy, gz = lax.axis_index("gx"), lax.axis_index("gy"), lax.axis_index("gz")

    def near(step):
        return {"gy": lax.rem(gy + step[0], GY), "gz": lax.rem(gz + step[1], GZ)}

    def along(step):
        return {"gx": lax.rem(gx + step, GX)}

    def corner(step):
        return {"gx": lax.rem(gx + step[0], GX), "gy": lax.rem(gy + step[1], GY)}

    barrier = pltpu.get_barrier_semaphore()
    greeted = [along(step) for step in CLOSE] + [near(step) for step in NEAR] + [corner(step) for step in CORNERS]
    for device in greeted:
        pl.semaphore_signal(barrier, inc=1, device_id=device, device_id_type=MESH)

    lane = lax.broadcasted_iota(jnp.int32, (8, 128), 1)
    first_half = lane < 64
    first_half_40 = lax.broadcasted_iota(jnp.int32, (40, 128), 1) < 64

    loads[0].wait()
    best = jnp.zeros((16, 128), jnp.float32)
    for z in range(4):
        state = [us[(f * 4 + z) * 16 : (f * 4 + z) * 16 + 16, :] for f in range(5)]
        inverse = 1.0 / state[0]
        pressure = pressure_of(state, inverse)
        best = jnp.maximum(best, fastest_of(state, inverse, pressure))
        for f, entry in enumerate(flux_entries(state, inverse, pressure, 2)):
            fy[(f * 4 + z) * 16 : (f * 4 + z) * 16 + 16, :] = entry
        for f, entry in enumerate(flux_entries(state, inverse, pressure, 3)):
            fz[f, 3 + z] = entry
        for f in range(5):
            uz[f, 3 + z] = state[f]
    best = jnp.maximum(best[0:8], best[8:16])
    loads[1].wait()
    for f in range(5):
        cp[f * 8 : f * 8 + 8, :] = jnp.concatenate(
            [cs[f * 16 : f * 16 + 8, :], cs[f * 16 + 8 : f * 16 + 16, :]], axis=1
        )
    coarse = [cp[f * 8 : f * 8 + 8, :] for f in range(5)]
    coarse_inverse = 1.0 / coarse[0]
    coarse_pressure = pressure_of(coarse, coarse_inverse)
    coarse_best = fastest_of(coarse, coarse_inverse, coarse_pressure)
    best = jnp.where(
        first_half,
        jnp.maximum(best, swap_halves(best)),
        jnp.maximum(coarse_best, swap_halves(coarse_best)),
    )
    sp1[31:32, :] = jnp.max(best, axis=0, keepdims=True)

    for load in loads[2:]:
        load.wait()
    eighth = jnp.bitwise_and(lane, 7)
    group_of_lane = lax.shift_right_logical(lane, 3)
    packed = [jnp.zeros((8, 128), jnp.float32) for _ in range(2)]
    for c in range(3):
        for z in range(4):
            n = c * 4 + z
            for h in range(2):
                tile = noise[n * 16 + h * 8 : n * 16 + h * 8 + 8, :]
                nx[n, 8 + h * 8 : 16 + h * 8, :] = tile
                packed[h] = jnp.where(group_of_lane == n, pltpu.roll(tile, (n * 8 + 4) % 128, 1), packed[h])
        for pair in range(2):
            row = (c * 4 + 2 * pair) * 16
            halves[(c * 2 + pair) * 16 : (c * 2 + pair) * 16 + 16, :] = (
                noise[row : row + 16, :] + noise[row + 16 : row + 32, :]
            )
    for h in range(2):
        pk[0, h * 8 : h * 8 + 8, :] = packed[h]
    from_lane = lax.broadcasted_iota(jnp.int32, (128, 128), 0)
    to_lane = lax.broadcasted_iota(jnp.int32, (128, 128), 1)
    restricted = jnp.zeros((24, 128), jnp.float32)
    for pair in range(2):
        rows = jnp.concatenate(
            [
                halves[pl.ds((c * 2 + pair) * 16, 8, stride=2), :]
                + halves[pl.ds((c * 2 + pair) * 16 + 1, 8, stride=2), :]
                for c in range(3)
            ],
            axis=0,
        )
        pick = (lax.shift_right_logical(from_lane, 1) + 64 * pair == to_lane).astype(jnp.float32)
        restricted = restricted + lax.dot(
            rows, pick, precision=lax.Precision.HIGHEST, preferred_element_type=jnp.float32
        )
    restricted = restricted * RESTRICT_SCALE
    coarse_packed = jnp.zeros((8, 128), jnp.float32)
    for c in range(3):
        tile = restricted[c * 8 : c * 8 + 8]
        nx[12 + c, 8:16, :] = tile
        nx[12 + c, 16:24, :] = tile
        swapped = swap_halves(tile)
        for p in range(2):
            m = c * 2 + p
            doubled = jnp.where(first_half, tile, swapped) if p == 0 else jnp.where(first_half, swapped, tile)
            coarse_packed = jnp.where(group_of_lane == m, pltpu.roll(doubled, m * 8 + 4, 1), coarse_packed)
    pk[1, 0:8, :] = coarse_packed
    pk[1, 8:16, :] = coarse_packed
    for f in range(5):
        gs[gz, f] = coarse[f]

    pl.semaphore_wait(barrier, len(greeted))
    next_z, last_z = near((0, 1)), near((0, GZ - 1))
    next_x, last_x = along(1), along(GX - 1)
    next_y, last_y = near((1, 0)), near((GY - 1, 0))

    def send(index, src, dst, device):
        copy = pltpu.make_async_remote_copy(
            src_ref=src, dst_ref=dst, send_sem=hs.at[index], recv_sem=hr.at[index],
            device_id=device, device_id_type=MESH,
        )
        copy.start()
        return copy

    for n, step in enumerate(NEAR):
        pltpu.make_async_remote_copy(
            src_ref=sp1.at[pl.ds(31, 1)], dst_ref=sp1.at[pl.ds(n, 1)], send_sem=s1_send,
            recv_sem=s1_recv, device_id=near(step), device_id_type=MESH,
        ).start()
    for step in (4, GX - 4):
        pl.semaphore_signal(far_sem, inc=1, device_id=along(step), device_id_type=MESH)
    noise_xy = [
        send(0, nx.at[:, pl.ds(16, 8)], nx.at[:, pl.ds(0, 8)], next_x),
        send(1, nx.at[:, pl.ds(8, 8)], nx.at[:, pl.ds(24, 8)], last_x),
        send(2, pk, hb.at[0, :, pl.ds(8, 16)], next_y),
        send(3, pk, hb.at[1, :, pl.ds(8, 16)], last_y),
        send(4, pk.at[:, pl.ds(8, 8)], hb.at[0, :, pl.ds(0, 8)], corner(CORNERS[0])),
        send(5, pk.at[:, pl.ds(8, 8)], hb.at[1, :, pl.ds(0, 8)], corner(CORNERS[1])),
        send(6, pk.at[:, pl.ds(0, 8)], hb.at[0, :, pl.ds(24, 8)], corner(CORNERS[2])),
        send(7, pk.at[:, pl.ds(0, 8)], hb.at[1, :, pl.ds(24, 8)], corner(CORNERS[3])),
    ]
    state_z = [
        send(12, uz.at[:, pl.ds(4, 3)], uz.at[:, pl.ds(0, 3)], next_z),
        send(13, uz.at[:, pl.ds(3, 3)], uz.at[:, pl.ds(7, 3)], last_z),
    ]

    def column(ref, send_sem, recv_sem):
        copies = []
        for step in range(1, GZ):
            copy = pltpu.make_async_remote_copy(
                src_ref=ref.at[gz], dst_ref=ref.at[gz], send_sem=send_sem, recv_sem=recv_sem.at[step - 1],
                device_id=near((0, step)), device_id_type=MESH,
            )
            copy.start()
            origin = lax.rem(gz + GZ - step, GZ)
            copies.append(
                pltpu.make_async_remote_copy(
                    src_ref=ref.at[gz], dst_ref=ref.at[origin], send_sem=send_sem,
                    recv_sem=recv_sem.at[step - 1], device_id=next_z, device_id_type=MESH,
                )
            )
        whole = pltpu.make_async_remote_copy(
            src_ref=ref.at[pl.ds(0, GZ - 1)], dst_ref=ref.at[pl.ds(0, GZ - 1)], send_sem=send_sem,
            recv_sem=recv_sem.at[0], device_id=next_z, device_id_type=MESH,
        )
        return copies, whole

    state_column, state_column_sent = column(gs, gs_send, gs_recv)

    for k in range(16):
        for group in range(2):
            ux[(3 + k) * 32 + group * 8 : (3 + k) * 32 + group * 8 + 8, :] = us[
                pl.ds(group * 128 + k, 8, stride=16), :
            ]
        ux[(3 + k) * 32 + 16 : (3 + k) * 32 + 20, :] = us[pl.ds(256 + k, 4, stride=16), :]
    for k in range(8):
        row = cp[pl.ds(k, 5, stride=8), :]
        ux[(3 + k) * 32 + 24 : (3 + k) * 32 + 29, :] = row
        ux[(11 + k) * 32 + 24 : (11 + k) * 32 + 29, :] = row

    state_x = [
        send(8, ux.at[pl.ds(16 * 32, 96)], ux.at[pl.ds(0, 96)], next_x),
        send(9, ux.at[pl.ds(3 * 32, 96)], ux.at[pl.ds(19 * 32, 96)], last_x),
    ]

    for t in range(2):
        ty[t, 8:136, :] = us[t * 128 : t * 128 + 128, :].T
        ty[3 + t, 8:136, :] = fy[t * 128 : t * 128 + 128, :].T
    tail = us[256:320, :]
    ty[2, 8:136, :] = jnp.concatenate([tail, tail], axis=0).T
    tail = fy[256:320, :]
    ty[5, 8:136, :] = jnp.concatenate([tail, tail], axis=0).T
    for f, entry in enumerate(flux_entries(coarse, coarse_inverse, coarse_pressure, 2)):
        fcp[f * 8 : f * 8 + 8, :] = entry
    for t, ref in ((6, cp), (7, fcp)):
        both = ref[0:40, :]
        swapped = swap_halves(both)
        front = jnp.where(first_half_40, both, swapped)
        back = jnp.where(first_half_40, swapped, both)
        ty[t, 8:136, :] = jnp.concatenate([front, front[0:24], back, back[0:24]], axis=0).T
    state_y = [
        send(10, ty.at[:, pl.ds(128, 8)], ty.at[:, pl.ds(0, 8)], next_y),
        send(11, ty.at[:, pl.ds(8, 8)], ty.at[:, pl.ds(136, 8)], last_y),
    ]

    def flux_x(k, carry):
        base = k * 32
        state = [ux[pl.ds(base + 4 * f, 4), :] for f in range(5)]
        for f, entry in enumerate(flux_alone(state, 1)):
            fx[pl.ds(base + 4 * f, 4), :] = entry
        return carry

    lax.fori_loop(3, 19, flux_x, 0)
    for f, entry in enumerate(flux_entries(coarse, coarse_inverse, coarse_pressure, 1)):
        fcp[f * 8 : f * 8 + 8, :] = entry
    for k in range(8):
        fx[(3 + k) * 32 + 24 : (3 + k) * 32 + 29, :] = fcp[pl.ds(k, 5, stride=8), :]

    def total_wait(ref, count, send_sem, recv_sem):
        return pltpu.make_async_remote_copy(
            src_ref=ref.at[pl.ds(0, count)], dst_ref=ref.at[pl.ds(0, count)], send_sem=send_sem,
            recv_sem=recv_sem, device_id=next_x, device_id_type=MESH,
        )

    first_round = total_wait(sp1, 31, s1_send, s1_recv)
    first_round.wait_recv()
    sp2[15:16, :] = jnp.max(sp1[...], axis=0, keepdims=True)
    pl.semaphore_wait(far_sem, 2)
    for n, step in enumerate(ALONG):
        pltpu.make_async_remote_copy(
            src_ref=sp2.at[pl.ds(15, 1)], dst_ref=sp2.at[pl.ds(n, 1)], send_sem=s2_send,
            recv_sem=s2_recv, device_id=along(step), device_id_type=MESH,
        ).start()

    for copy in noise_xy:
        copy.wait_recv()

    def noise_along_x(n, carry):
        total = taps[0, 0] * nx[n, 4:20, :]
        for t in range(1, 9):
            total = total + taps[0, t] * nx[n, 4 + t : 20 + t, :]
        wx[pl.ds(pl.multiple_of(n * 16, 16), 16), :] = total
        return carry

    lax.fori_loop(0, 12, noise_along_x, 0)
    for c in range(3):
        total = taps[0, 0] * nx[12 + c, 4:12, :]
        for t in range(1, 9):
            base = 4 + t if t <= 4 else 12 + t
            total = total + taps[0, t] * nx[12 + c, base : base + 8, :]
        swapped = swap_halves(total)
        wx[192 + c * 8 : 200 + c * 8, :] = jnp.where(first_half, total, swapped)
        wx[216 + c * 8 : 224 + c * 8, :] = jnp.where(first_half, swapped, total)
    for b in range(2):
        for r in range(4):
            hb[0, b, r * 8 : r * 8 + 8, :] = jnp.where(
                eighth < 4, hb[0, b, r * 8 : r * 8 + 8, :], hb[1, b, r * 8 : r * 8 + 8, :]
            )
    beside = taps[0, 0] * hb[0, 0, 4:20, :]
    for t in range(1, 9):
        beside = beside + taps[0, t] * hb[0, 0, 4 + t : 20 + t, :]
    coarse_beside = taps[0, 0] * hb[0, 1, 4:12, :]
    for t in range(1, 9):
        base = 4 + t if t <= 4 else 12 + t
        coarse_beside = coarse_beside + taps[0, t] * hb[0, 1, base : base + 8, :]

    turned = jnp.concatenate([beside, coarse_beside, jnp.zeros((104, 128), jnp.float32)], axis=0).T
    rims = [jnp.zeros((8, 128), jnp.float32) for _ in range(2)]
    sixteenth = lax.shift_right_logical(lane, 4)
    for n in range(12):
        shift = (n % 8) * 16
        rolled = pltpu.roll(turned[n * 8 : n * 8 + 8], shift, 1) if shift else turned[n * 8 : n * 8 + 8]
        rims[n // 8] = jnp.where(sixteenth == n % 8, rolled, rims[n // 8])
    for c in range(3):
        for p in range(2):
            m = c * 2 + p
            target = 64 + p * 24 + c * 8
            rolled = pltpu.roll(turned[m * 8 : m * 8 + 8], target - 16, 1)
            rims[1] = jnp.where(group_of_lane == target // 8, rolled, rims[1])
    for t in range(2):
        nt[t, 8:136, :] = wx[t * 128 : t * 128 + 128, :].T
        nt[t, 4:8, :] = rims[t][0:4]
        nt[t, 136:140, :] = rims[t][4:8]
    total = taps[1, 0] * nt[0, 4:132, :]
    for t in range(1, 9):
        total = total + taps[1, t] * nt[0, 4 + t : 132 + t, :]
    total = total.T
    for n in range(8):
        nz[n // 4, 4 + n % 4] = total[n * 16 : n * 16 + 16]
    left = taps[1, 0] * nt[1, 4:132, :]
    for t in range(1, 5):
        left = left + taps[1, t] * nt[1, 4 + t : 132 + t, :]
    total = left
    for t in range(5, 9):
        total = total + taps[1, t] * nt[1, 4 + t : 132 + t, :]
    own = left[0:64]
    for t in range(5, 9):
        own = own + taps[1, t] * nt[1, 68 + t : 132 + t, :]
    front = jnp.where(lax.broadcasted_iota(jnp.int32, (64, 128), 1) < 64, total[0:64], own)
    total = jnp.concatenate([front, total[64:128]], axis=0).T
    for n in range(8, 12):
        nz[n // 4, 4 + n % 4] = total[(n - 8) * 16 : (n - 8) * 16 + 16]
    for c in range(3):
        gr[gz, c] = jnp.where(
            first_half, total[64 + c * 8 : 72 + c * 8], swap_halves(total[88 + c * 8 : 96 + c * 8])
        )
    noise_z = [
        send(14, nz.at[:, pl.ds(4, 4)], nz.at[:, pl.ds(0, 4)], next_z),
        send(15, nz.at[:, pl.ds(4, 4)], nz.at[:, pl.ds(8, 4)], last_z),
    ]
    noise_column, noise_column_sent = column(gr, gr_send, gr_recv)

    for copy in state_x:
        copy.wait_recv()
    lax.fori_loop(0, 3, flux_x, 0)
    lax.fori_loop(19, 22, flux_x, 0)
    for k in (0, 1, 2, 19, 20, 21):
        state = [ux[k * 32 + 24 + f : k * 32 + 25 + f, :] for f in range(5)]
        target = k if k < 3 else k - 8
        for f, entry in enumerate(flux_alone(state, 1)):
            fx[target * 32 + 24 + f : target * 32 + 25 + f, :] = entry
    for copy in state_x:
        copy.wait_send()
    for k in (11, 12, 13):
        ux[k * 32 + 24 : k * 32 + 32, :] = ux[(k + 8) * 32 + 24 : (k + 8) * 32 + 32, :]

    def steps_x(k, carry):
        for n, ref in enumerate((fx, ux)):
            for group in range(3):
                d16[n, group, k] = ref[pl.ds((k + 1) * 32 + group * 8, 8), :] - ref[
                    pl.ds(k * 32 + group * 8, 8), :
                ]
        return carry

    lax.fori_loop(0, 21, steps_x, 0)
    for n, ref in enumerate((fx, ux)):
        for k in range(13):
            d8[n, 0, k] = ref[(k + 1) * 32 + 24 : (k + 1) * 32 + 32, :] - ref[k * 32 + 24 : k * 32 + 32, :]

    for copy in state_y:
        copy.wait_recv()
    for n in range(2):

        def steps_y(t, carry):
            rows = [ty[3 - 3 * n + t, pl.ds(5 + k, 8, stride=16), :] for k in range(22)]
            for k in range(21):
                d16[n, 3 + t, k] = rows[k + 1] - rows[k]
            return carry

        lax.fori_loop(0, 3, steps_y, 0)
    for copy in state_y:
        copy.wait_send()
    for n, t in enumerate((7, 6)):
        ty[t, 72:80, :] = ty[t, 136:144, :]
        rows = [ty[t, pl.ds(5 + k, 8, stride=8), :] for k in range(14)]
        for k in range(13):
            d8[n, 1, k] = rows[k + 1] - rows[k]

    for copy in state_z:
        copy.wait_recv()
    for k in (0, 1, 2, 7, 8, 9):
        state = [uz[f, k] for f in range(5)]
        for f, entry in enumerate(flux_alone(state, 3)):
            fz[f, k] = entry

    def steps_z(f, carry):
        for n, ref in enumerate((fz, uz)):
            for h in range(2):
                for k in range(9):
                    d4 = ref[f, k + 1, h * 8 : h * 8 + 8, :] - ref[f, k, h * 8 : h * 8 + 8, :]
                    dz[n, f * 2 + h, k] = d4
        return carry

    lax.fori_loop(0, 5, steps_z, 0)
    block = jnp.int32(0)
    for j in range(GZ):
        block = block + j * (owner[j] == gz).astype(jnp.int32)

    def mixed(left, right):
        return jnp.where(first_half, swap_halves(left), swap_halves(right))

    around = [lax.rem(block + GZ + m, GZ) for m in range(-2, 3)]
    for copy in state_column:
        copy.wait_recv()
    pairs_u, pairs_f = [], []
    for j in around:
        state = [gs[owner[j], f] for f in range(5)]
        pairs_u.append(state)
        pairs_f.append(flux_alone(state, 3))
    for n, pairs in enumerate((pairs_f, pairs_u)):
        for f in range(5):
            planes = []
            for j in range(-3, 4):
                m = (j + 4) // 2
                planes.append(pairs[m][f] if j % 2 == 0 else mixed(pairs[m][f], pairs[m + 1][f]))
            for k in range(6):
                d1[n, f, k] = planes[k + 1] - planes[k]

    second_round = total_wait(sp2, 15, s2_send, s2_recv)
    second_round.wait_recv()
    speeds = jnp.max(sp2[...], axis=0, keepdims=True)
    front_row = lax.broadcasted_iota(jnp.int32, (1, 128), 1) < 64
    speed_fine = jnp.broadcast_to(
        jnp.max(jnp.where(front_row, speeds, 0.0), axis=1, keepdims=True), (8, 128)
    )
    speed_coarse = jnp.broadcast_to(
        jnp.max(jnp.where(front_row, 0.0, speeds), axis=1, keepdims=True), (8, 128)
    )

    def sweep_16(g, carry):
        out = sweep([d16[0, g, k] for k in range(21)], [d16[1, g, k] for k in range(21)], speed_fine, 16)
        for k in range(16):
            a16[pl.ds(g * 128 + k, 8, stride=16), :] = out[k]
        return carry

    def sweep_4(g, carry):
        out = sweep([dz[0, g, k] for k in range(9)], [dz[1, g, k] for k in range(9)], speed_fine, 4)
        for z in range(4):
            az[g, z] = out[z]
        return carry

    def sweep_8(g, carry):
        out = sweep([d8[0, g, k] for k in range(13)], [d8[1, g, k] for k in range(13)], speed_coarse, 8)
        for k in range(8):
            a8[pl.ds(g * 64 + k, 8, stride=8), :] = out[k]
        return carry

    def sweep_1(g, carry):
        out = sweep([d1[0, g, k] for k in range(6)], [d1[1, g, k] for k in range(6)], speed_coarse, 1)
        a1[g] = out[0]
        return carry

    lax.fori_loop(0, 6, sweep_16, 0)
    lax.fori_loop(0, 10, sweep_4, 0)
    lax.fori_loop(0, 2, sweep_8, 0)
    lax.fori_loop(0, 5, sweep_1, 0)

    for copy in noise_z:
        copy.wait_recv()
    for h in range(2):

        def noise_along_z(c, carry):
            planes = [nz[c, z, h * 8 : h * 8 + 8, :] for z in range(12)]
            for z in range(4):
                total = taps[2, 0] * planes[z]
                for t in range(1, 9):
                    total = total + taps[2, t] * planes[z + t]
                force[c * 4 + z, h * 8 : h * 8 + 8, :] = total
            return carry

        lax.fori_loop(0, 3, noise_along_z, 0)

    def sources(z, carry):
        state = [us[pl.ds(pl.multiple_of((f * 4 + z) * 16, 16), 16), :] for f in range(4)]
        push = [force[c * 4 + z] for c in range(3)]
        for c in range(3):
            force[c * 4 + z] = state[0] * push[c]
        force[12 + z] = state[1] * push[0] + state[2] * push[1] + state[3] * push[2]
        return carry

    lax.fori_loop(0, 4, sources, 0)
    for copy in noise_column:
        copy.wait_recv()
    push = []
    for c in range(3):
        pairs = [gr[j, c] for j in around]
        total = taps[2, 0] * pairs[0]
        for t in range(1, 9):
            plane = pairs[t // 2] if t % 2 == 0 else mixed(pairs[t // 2], pairs[t // 2 + 1])
            total = total + taps[2, t] * plane
        push.append(2.0 * total)
    work = coarse[1] * push[0] + coarse[2] * push[1] + coarse[3] * push[2]
    coarse_source = [None, coarse[0] * push[0], coarse[0] * push[1], coarse[0] * push[2], work]
    for f in range(1, 5):
        fcp[f * 8 : f * 8 + 8, :] = coarse_source[f]

    rate_fine = 0.1 / speed_fine
    rate_coarse = 0.1 / speed_coarse
    for t in range(3):
        wide = a16[384 + t * 128 : 512 + t * 128, :].T
        for tile in range(16 if t < 2 else 8):
            index = t * 16 + tile
            f, z, h = index // 8, (index // 2) % 4, index % 2
            row = index * 8
            change = -0.5 * (a16[row : row + 8, :] + wide[tile * 8 : tile * 8 + 8] + az[f * 2 + h, z])
            if f > 0:
                change = change + force[(f - 1) * 4 + z, h * 8 : h * 8 + 8, :]
            fine_out[row : row + 8, :] = 0.25 * us[row : row + 8, :] + rate_fine * change

    along_y = a8[64:128, :]
    turned = jnp.concatenate([along_y, along_y], axis=0).T
    along_y = jnp.where(first_half_40, turned[0:40], turned[64:104])
    for f in range(5):
        change = -0.5 * (a8[f * 8 : f * 8 + 8, :] + along_y[f * 8 : f * 8 + 8] + a1[f])
        if f > 0:
            change = change + fcp[f * 8 : f * 8 + 8, :]
        result = 0.25 * cp[f * 8 : f * 8 + 8, :] + rate_coarse * change
        coarse_out[f * 16 : f * 16 + 8, :] = result[:, 0:64]
        coarse_out[f * 16 + 8 : f * 16 + 16, :] = swap_halves(result)[:, 0:64]

    first_round.wait_send()
    second_round.wait_send()
    for copy in noise_xy + state_z + noise_z:
        copy.wait_send()
    state_column_sent.wait_send()
    noise_column_sent.wait_send()


def local(fine_start, fine_section, fine_noise, coarse_start, coarse_section, taps, owner):
    f32 = jnp.float32
    vmem = pl.BlockSpec(memory_space=pltpu.VMEM)
    hbm = pl.BlockSpec(memory_space=pltpu.HBM)
    dma = pltpu.SemaphoreType.DMA
    fine, coarse = pl.pallas_call(
        kernel,
        out_shape=(jax.ShapeDtypeStruct((320, 128), f32), jax.ShapeDtypeStruct((80, 64), f32)),
        in_specs=[hbm] * 5,
        out_specs=(vmem, vmem),
        scratch_shapes=[
            pltpu.VMEM((320, 128), f32),
            pltpu.VMEM((192, 128), f32),
            pltpu.VMEM((80, 64), f32),
            pltpu.SMEM((3, 9), f32),
            pltpu.SMEM((8,), jnp.int32),
            pltpu.VMEM((32, 128), f32),
            pltpu.VMEM((16, 128), f32),
            pltpu.VMEM((40, 128), f32),
            pltpu.VMEM((40, 128), f32),
            pltpu.VMEM((704, 128), f32),
            pltpu.VMEM((704, 128), f32),
            pltpu.VMEM((8, 144, 128), f32),
            pltpu.VMEM((320, 128), f32),
            pltpu.VMEM((5, 10, 16, 128), f32),
            pltpu.VMEM((5, 10, 16, 128), f32),
            pltpu.VMEM((3, 12, 16, 128), f32),
            pltpu.VMEM((8, 5, 8, 128), f32),
            pltpu.VMEM((8, 3, 8, 128), f32),
            pltpu.VMEM((15, 32, 128), f32),
            pltpu.VMEM((2, 16, 128), f32),
            pltpu.VMEM((2, 2, 32, 128), f32),
            pltpu.VMEM((256, 128), f32),
            pltpu.VMEM((2, 144, 128), f32),
            pltpu.VMEM((16, 16, 128), f32),
            pltpu.VMEM((96, 128), f32),
            pltpu.VMEM((2, 10, 9, 8, 128), f32),
            pltpu.VMEM((2, 6, 21, 8, 128), f32),
            pltpu.VMEM((2, 2, 13, 8, 128), f32),
            pltpu.VMEM((2, 5, 6, 8, 128), f32),
            pltpu.VMEM((10, 4, 8, 128), f32),
            pltpu.VMEM((768, 128), f32),
            pltpu.VMEM((128, 128), f32),
            pltpu.VMEM((5, 8, 128), f32),
            dma((5,)),
            pltpu.SemaphoreType.REGULAR,
            dma, dma, dma, dma, dma, dma((7,)), dma, dma((7,)), dma((16,)), dma((16,)),
        ],
        compiler_params=pltpu.CompilerParams(
            collective_id=0, has_side_effects=True, vmem_limit_bytes=24 * 1024 * 1024
        ),
        name="section",
    )(
        *(
            pltpu.with_memory_space_constraint(operand, pltpu.HBM)
            for operand in (
                fine_section.reshape(320, 128), fine_noise.reshape(192, 128),
                coarse_section.reshape(80, 64), taps, owner,
            )
        )
    )
    return (
        0.75 * fine_start + fine.reshape(fine_start.shape),
        0.75 * coarse_start + coarse.reshape(coarse_start.shape),
    )


def solution(mesh):
    cells = P(None, "gz", "gx", "gy")
    return jax.shard_map(
        local,
        mesh=mesh,
        in_specs=(cells, cells, cells, cells, cells, P(), P()),
        out_specs=(cells, cells),
        check_vma=False,
    )
```

```python
import jax
import jax.numpy as jnp
from jax import lax
from jax.experimental import pallas as pl
from jax.experimental.pallas import tpu as pltpu
from jax.sharding import PartitionSpec as P

MESH = pl.DeviceIdType.MESH
GX, GY, GZ = 16, 4, 8
GAMMA = 1.4
INDICATOR_EPS = 2e-06
RESTRICT_SCALE = 0.35355339059327373
NEAR = sorted(
    ((i, j) for i in range(GY) for j in range(GZ) if (i, j) != (0, 0)),
    key=lambda step: -((step[0] + 1) // 2 % 2 + 2 * (step[1] // 4) + min(step[1] % 4, -step[1] % 4)),
)
ALONG = [8, 7, 9, 6, 10, 5, 11, 4, 12, 3, 13, 2, 14, 1, 15]
CLOSE = [4, 12, 3, 13, 2, 14, 1, 15]
CORNERS = [(1, 1), (1, GY - 1), (GX - 1, 1), (GX - 1, GY - 1)]


def pressure_of(state, inverse):
    kinetic = 0.5 * (state[1] * state[1] + state[2] * state[2] + state[3] * state[3])
    return (GAMMA - 1.0) * (state[4] - kinetic * inverse)


def flux_entries(state, inverse, pressure, component):
    velocity = state[component] * inverse
    entries = [
        state[component],
        state[1] * velocity,
        state[2] * velocity,
        state[3] * velocity,
        (state[4] + pressure) * velocity,
    ]
    entries[component] = entries[component] + pressure
    return entries


def flux_alone(state, component):
    inverse = 1.0 / state[0]
    return flux_entries(state, inverse, pressure_of(state, inverse), component)


def fastest_of(state, inverse, pressure):
    largest = jnp.maximum(jnp.maximum(jnp.abs(state[1]), jnp.abs(state[2])), jnp.abs(state[3]))
    return largest * inverse + jnp.sqrt(GAMMA * pressure * inverse)


def prepare(steps, flux):
    cells = len(steps) - 5
    bends = [steps[k - 1] - 2.0 * steps[k] + steps[k + 1] for k in range(1, cells + 4)]
    if flux:
        linear = [
            steps[c + 2] + steps[c + 3] + (steps[c + 2] - steps[c + 4] - steps[c + 1] + steps[c + 3]) * (1.0 / 6.0)
            for c in range(cells)
        ]
    else:
        linear = [
            steps[c + 2] - steps[c + 3]
            + (steps[c + 4] - steps[c + 1] + 3.0 * (steps[c + 3] - steps[c + 2])) * (1.0 / 6.0)
            for c in range(cells)
        ]
    return list(steps) + bends + linear


def indicators(steps):
    squares = [e * e for e in steps]
    raised = [(2.0 / 3.0) * x + 0.5 * INDICATOR_EPS for x in squares]
    low, mid, high = [], [], []
    for i in range(len(steps) - 1):
        cross = steps[i] * steps[i + 1]
        base = raised[i] + raised[i + 1] - (11.0 / 6.0) * cross
        low.append(base + squares[i + 1])
        high.append(base + squares[i])
        mid.append(base + cross)
    return low, mid, high


def side(low, mid, high, first, second):
    to_mid = low * pltpu.reciprocal(mid, approx=True)
    to_high = low * pltpu.reciprocal(high, approx=True)
    w2 = 1.5 * (to_high * to_high)
    total = 3.0 * (to_mid * to_mid) + w2 + 0.5
    return (first + w2 * second) * pltpu.reciprocal(total, approx=True)


def sweep(flux, state, speed, cells):
    steps, bends = cells + 5, cells + 3
    scaled = [speed * u for u in state]
    up = [f + u for f, u in zip(flux[:steps], scaled[:steps])]
    down = [f - u for f, u in zip(flux[:steps], scaled[:steps])]
    low_u, mid_u, high_u = indicators(up[: cells + 4])
    low_d, mid_d, high_d = indicators(down)
    bend_u = [f + u for f, u in zip(flux[steps : steps + bends], scaled[steps : steps + bends])]
    bend_d = [f - u for f, u in zip(flux[steps : steps + bends], scaled[steps : steps + bends])]
    faces = []
    for j in range(cells + 1):
        right = side(low_u[j], mid_u[j + 1], high_u[j + 2], bend_u[j], bend_u[j + 1])
        left = side(high_d[j + 3], mid_d[j + 2], low_d[j + 1], bend_d[j + 2], bend_d[j + 1])
        faces.append(left - right)
    return [
        flux[steps + bends + c] + scaled[steps + bends + c] + (faces[c + 1] - faces[c]) * (1.0 / 6.0)
        for c in range(cells)
    ]


def swap_halves(values):
    return pltpu.roll(values, 64, 1)


def kernel(
    us_hbm, noise_hbm, cs_hbm, taps_hbm, owner_hbm, fine_out, coarse_out,
    us, noise, cs, taps, owner, sp1, sp2, cp, fcp, ux, fx, ty, fy, uz, fz, nz, gs, gr, nx, pk, hb, wx, nt,
    force, halves, dz, d16, d8, d1, az, a16, ay, a8, a1,
    ins, far_sem, s1_send, s1_recv, s2_send, s2_recv, gs_send, gs_recv, gr_send, gr_recv, hs, hr,
):
    loads = [
        pltpu.make_async_copy(src, dst, ins.at[n])
        for n, (src, dst) in enumerate(
            ((us_hbm, us), (cs_hbm, cs), (noise_hbm, noise), (taps_hbm, taps), (owner_hbm, owner))
        )
    ]
    for load in loads:
        load.start()
    gx, gy, gz = lax.axis_index("gx"), lax.axis_index("gy"), lax.axis_index("gz")

    def near(step):
        return {"gy": lax.rem(gy + step[0], GY), "gz": lax.rem(gz + step[1], GZ)}

    def along(step):
        return {"gx": lax.rem(gx + step, GX)}

    def corner(step):
        return {"gx": lax.rem(gx + step[0], GX), "gy": lax.rem(gy + step[1], GY)}

    barrier = pltpu.get_barrier_semaphore()
    greeted = [along(step) for step in CLOSE] + [near(step) for step in NEAR] + [corner(step) for step in CORNERS]
    for device in greeted:
        pl.semaphore_signal(barrier, inc=1, device_id=device, device_id_type=MESH)

    lane = lax.broadcasted_iota(jnp.int32, (8, 128), 1)
    first_half = lane < 64
    first_half_40 = lax.broadcasted_iota(jnp.int32, (40, 128), 1) < 64

    def cells(z):
        return [us[(f * 4 + z) * 16 : (f * 4 + z) * 16 + 16, :] for f in range(5)]

    loads[0].wait()
    best = jnp.zeros((16, 128), jnp.float32)
    for z in range(4):
        state = cells(z)
        inverse = 1.0 / state[0]
        best = jnp.maximum(best, fastest_of(state, inverse, pressure_of(state, inverse)))
    best = jnp.maximum(best[0:8], best[8:16])
    loads[1].wait()
    for f in range(5):
        cp[f * 8 : f * 8 + 8, :] = jnp.concatenate(
            [cs[f * 16 : f * 16 + 8, :], cs[f * 16 + 8 : f * 16 + 16, :]], axis=1
        )
    coarse = [cp[f * 8 : f * 8 + 8, :] for f in range(5)]
    coarse_inverse = 1.0 / coarse[0]
    coarse_pressure = pressure_of(coarse, coarse_inverse)
    coarse_best = fastest_of(coarse, coarse_inverse, coarse_pressure)
    best = jnp.where(
        first_half,
        jnp.maximum(best, swap_halves(best)),
        jnp.maximum(coarse_best, swap_halves(coarse_best)),
    )
    sp1[31:32, :] = jnp.max(best, axis=0, keepdims=True)

    pl.semaphore_wait(barrier, len(greeted))
    next_z, last_z = near((0, 1)), near((0, GZ - 1))
    next_x, last_x = along(1), along(GX - 1)
    next_y, last_y = near((1, 0)), near((GY - 1, 0))

    def send(index, src, dst, device):
        copy = pltpu.make_async_remote_copy(
            src_ref=src, dst_ref=dst, send_sem=hs.at[index], recv_sem=hr.at[index],
            device_id=device, device_id_type=MESH,
        )
        copy.start()
        return copy

    for n, step in enumerate(NEAR):
        pltpu.make_async_remote_copy(
            src_ref=sp1.at[pl.ds(31, 1)], dst_ref=sp1.at[pl.ds(n, 1)], send_sem=s1_send,
            recv_sem=s1_recv, device_id=near(step), device_id_type=MESH,
        ).start()
    for step in (4, GX - 4):
        pl.semaphore_signal(far_sem, inc=1, device_id=along(step), device_id_type=MESH)

    for load in loads[2:]:
        load.wait()
    eighth = jnp.bitwise_and(lane, 7)
    group_of_lane = lax.shift_right_logical(lane, 3)
    packed = [jnp.zeros((8, 128), jnp.float32) for _ in range(2)]
    for c in range(3):
        for z in range(4):
            n = c * 4 + z
            for h in range(2):
                tile = noise[n * 16 + h * 8 : n * 16 + h * 8 + 8, :]
                nx[n, 8 + h * 8 : 16 + h * 8, :] = tile
                packed[h] = jnp.where(group_of_lane == n, pltpu.roll(tile, (n * 8 + 4) % 128, 1), packed[h])
        for pair in range(2):
            row = (c * 4 + 2 * pair) * 16
            halves[(c * 2 + pair) * 16 : (c * 2 + pair) * 16 + 16, :] = (
                noise[row : row + 16, :] + noise[row + 16 : row + 32, :]
            )
    for h in range(2):
        pk[0, h * 8 : h * 8 + 8, :] = packed[h]
    from_lane = lax.broadcasted_iota(jnp.int32, (128, 128), 0)
    to_lane = lax.broadcasted_iota(jnp.int32, (128, 128), 1)
    restricted = jnp.zeros((24, 128), jnp.float32)
    for pair in range(2):
        rows = jnp.concatenate(
            [
                halves[pl.ds((c * 2 + pair) * 16, 8, stride=2), :]
                + halves[pl.ds((c * 2 + pair) * 16 + 1, 8, stride=2), :]
                for c in range(3)
            ],
            axis=0,
        )
        pick = (lax.shift_right_logical(from_lane, 1) + 64 * pair == to_lane).astype(jnp.float32)
        restricted = restricted + lax.dot(
            rows, pick, precision=lax.Precision.HIGHEST, preferred_element_type=jnp.float32
        )
    restricted = restricted * RESTRICT_SCALE
    coarse_packed = jnp.zeros((8, 128), jnp.float32)
    for c in range(3):
        tile = restricted[c * 8 : c * 8 + 8]
        nx[12 + c, 8:16, :] = tile
        nx[12 + c, 16:24, :] = tile
        swapped = swap_halves(tile)
        for p in range(2):
            m = c * 2 + p
            doubled = jnp.where(first_half, tile, swapped) if p == 0 else jnp.where(first_half, swapped, tile)
            coarse_packed = jnp.where(group_of_lane == m, pltpu.roll(doubled, m * 8 + 4, 1), coarse_packed)
    pk[1, 0:8, :] = coarse_packed
    pk[1, 8:16, :] = coarse_packed
    for f in range(5):
        gs[gz, f] = coarse[f]

    noise_xy = [
        send(0, nx.at[:, pl.ds(16, 8)], nx.at[:, pl.ds(0, 8)], next_x),
        send(1, nx.at[:, pl.ds(8, 8)], nx.at[:, pl.ds(24, 8)], last_x),
        send(2, pk, hb.at[0, :, pl.ds(8, 16)], next_y),
        send(3, pk, hb.at[1, :, pl.ds(8, 16)], last_y),
        send(4, pk.at[:, pl.ds(8, 8)], hb.at[0, :, pl.ds(0, 8)], corner(CORNERS[0])),
        send(5, pk.at[:, pl.ds(8, 8)], hb.at[1, :, pl.ds(0, 8)], corner(CORNERS[1])),
        send(6, pk.at[:, pl.ds(0, 8)], hb.at[0, :, pl.ds(24, 8)], corner(CORNERS[2])),
        send(7, pk.at[:, pl.ds(0, 8)], hb.at[1, :, pl.ds(24, 8)], corner(CORNERS[3])),
    ]

    for z in range(4):
        state = cells(z)
        inverse = 1.0 / state[0]
        pressure = pressure_of(state, inverse)
        for f, entry in enumerate(flux_entries(state, inverse, pressure, 2)):
            fy[(f * 4 + z) * 16 : (f * 4 + z) * 16 + 16, :] = entry
        for f, entry in enumerate(flux_entries(state, inverse, pressure, 3)):
            fz[f, 3 + z] = entry
        for f in range(5):
            uz[f, 3 + z] = state[f]

    state_z = [
        send(12, uz.at[:, pl.ds(4, 3)], uz.at[:, pl.ds(0, 3)], next_z),
        send(13, uz.at[:, pl.ds(3, 3)], uz.at[:, pl.ds(7, 3)], last_z),
    ]

    def column(ref, send_sem, recv_sem):
        copies = []
        for step in range(1, GZ):
            copy = pltpu.make_async_remote_copy(
                src_ref=ref.at[gz], dst_ref=ref.at[gz], send_sem=send_sem, recv_sem=recv_sem.at[step - 1],
                device_id=near((0, step)), device_id_type=MESH,
            )
            copy.start()
            origin = lax.rem(gz + GZ - step, GZ)
            copies.append(
                pltpu.make_async_remote_copy(
                    src_ref=ref.at[gz], dst_ref=ref.at[origin], send_sem=send_sem,
                    recv_sem=recv_sem.at[step - 1], device_id=next_z, device_id_type=MESH,
                )
            )
        whole = pltpu.make_async_remote_copy(
            src_ref=ref.at[pl.ds(0, GZ - 1)], dst_ref=ref.at[pl.ds(0, GZ - 1)], send_sem=send_sem,
            recv_sem=recv_sem.at[0], device_id=next_z, device_id_type=MESH,
        )
        return copies, whole

    state_column, state_column_sent = column(gs, gs_send, gs_recv)

    for k in range(16):
        for group in range(2):
            ux[(3 + k) * 32 + group * 8 : (3 + k) * 32 + group * 8 + 8, :] = us[
                pl.ds(group * 128 + k, 8, stride=16), :
            ]
        ux[(3 + k) * 32 + 16 : (3 + k) * 32 + 20, :] = us[pl.ds(256 + k, 4, stride=16), :]
    for k in range(8):
        row = cp[pl.ds(k, 5, stride=8), :]
        ux[(3 + k) * 32 + 24 : (3 + k) * 32 + 29, :] = row
        ux[(11 + k) * 32 + 24 : (11 + k) * 32 + 29, :] = row

    state_x = [
        send(8, ux.at[pl.ds(16 * 32, 96)], ux.at[pl.ds(0, 96)], next_x),
        send(9, ux.at[pl.ds(3 * 32, 96)], ux.at[pl.ds(19 * 32, 96)], last_x),
    ]

    for t in range(2):
        ty[t, 8:136, :] = us[t * 128 : t * 128 + 128, :].T
        ty[3 + t, 8:136, :] = fy[t * 128 : t * 128 + 128, :].T
    tail = us[256:320, :]
    ty[2, 8:136, :] = jnp.concatenate([tail, tail], axis=0).T
    tail = fy[256:320, :]
    ty[5, 8:136, :] = jnp.concatenate([tail, tail], axis=0).T
    for f, entry in enumerate(flux_entries(coarse, coarse_inverse, coarse_pressure, 2)):
        fcp[f * 8 : f * 8 + 8, :] = entry
    for t, ref in ((6, cp), (7, fcp)):
        both = ref[0:40, :]
        swapped = swap_halves(both)
        front = jnp.where(first_half_40, both, swapped)
        back = jnp.where(first_half_40, swapped, both)
        ty[t, 8:136, :] = jnp.concatenate([front, front[0:24], back, back[0:24]], axis=0).T
    state_y = [
        send(10, ty.at[:, pl.ds(128, 8)], ty.at[:, pl.ds(0, 8)], next_y),
        send(11, ty.at[:, pl.ds(8, 8)], ty.at[:, pl.ds(136, 8)], last_y),
    ]

    def flux_x(k, carry):
        base = k * 32
        state = [ux[pl.ds(base + 4 * f, 4), :] for f in range(5)]
        for f, entry in enumerate(flux_alone(state, 1)):
            fx[pl.ds(base + 4 * f, 4), :] = entry
        return carry

    lax.fori_loop(3, 19, flux_x, 0)
    for f, entry in enumerate(flux_entries(coarse, coarse_inverse, coarse_pressure, 1)):
        fcp[f * 8 : f * 8 + 8, :] = entry
    for k in range(8):
        fx[(3 + k) * 32 + 24 : (3 + k) * 32 + 29, :] = fcp[pl.ds(k, 5, stride=8), :]

    def total_wait(ref, count, send_sem, recv_sem):
        return pltpu.make_async_remote_copy(
            src_ref=ref.at[pl.ds(0, count)], dst_ref=ref.at[pl.ds(0, count)], send_sem=send_sem,
            recv_sem=recv_sem, device_id=next_x, device_id_type=MESH,
        )

    first_round = total_wait(sp1, 31, s1_send, s1_recv)
    first_round.wait_recv()
    sp2[15:16, :] = jnp.max(sp1[...], axis=0, keepdims=True)
    pl.semaphore_wait(far_sem, 2)
    for n, step in enumerate(ALONG):
        pltpu.make_async_remote_copy(
            src_ref=sp2.at[pl.ds(15, 1)], dst_ref=sp2.at[pl.ds(n, 1)], send_sem=s2_send,
            recv_sem=s2_recv, device_id=along(step), device_id_type=MESH,
        ).start()

    for copy in noise_xy:
        copy.wait_recv()

    def noise_along_x(n, carry):
        total = taps[0, 0] * nx[n, 4:20, :]
        for t in range(1, 9):
            total = total + taps[0, t] * nx[n, 4 + t : 20 + t, :]
        wx[pl.ds(pl.multiple_of(n * 16, 16), 16), :] = total
        return carry

    lax.fori_loop(0, 12, noise_along_x, 0)
    for c in range(3):
        total = taps[0, 0] * nx[12 + c, 4:12, :]
        for t in range(1, 9):
            base = 4 + t if t <= 4 else 12 + t
            total = total + taps[0, t] * nx[12 + c, base : base + 8, :]
        swapped = swap_halves(total)
        wx[192 + c * 8 : 200 + c * 8, :] = jnp.where(first_half, total, swapped)
        wx[216 + c * 8 : 224 + c * 8, :] = jnp.where(first_half, swapped, total)
    for b in range(2):
        for r in range(4):
            hb[0, b, r * 8 : r * 8 + 8, :] = jnp.where(
                eighth < 4, hb[0, b, r * 8 : r * 8 + 8, :], hb[1, b, r * 8 : r * 8 + 8, :]
            )
    beside = taps[0, 0] * hb[0, 0, 4:20, :]
    for t in range(1, 9):
        beside = beside + taps[0, t] * hb[0, 0, 4 + t : 20 + t, :]
    coarse_beside = taps[0, 0] * hb[0, 1, 4:12, :]
    for t in range(1, 9):
        base = 4 + t if t <= 4 else 12 + t
        coarse_beside = coarse_beside + taps[0, t] * hb[0, 1, base : base + 8, :]

    turned = jnp.concatenate([beside, coarse_beside, jnp.zeros((104, 128), jnp.float32)], axis=0).T
    rims = [jnp.zeros((8, 128), jnp.float32) for _ in range(2)]
    sixteenth = lax.shift_right_logical(lane, 4)
    for n in range(12):
        shift = (n % 8) * 16
        rolled = pltpu.roll(turned[n * 8 : n * 8 + 8], shift, 1) if shift else turned[n * 8 : n * 8 + 8]
        rims[n // 8] = jnp.where(sixteenth == n % 8, rolled, rims[n // 8])
    for c in range(3):
        for p in range(2):
            m = c * 2 + p
            target = 64 + p * 24 + c * 8
            rolled = pltpu.roll(turned[m * 8 : m * 8 + 8], target - 16, 1)
            rims[1] = jnp.where(group_of_lane == target // 8, rolled, rims[1])
    for t in range(2):
        nt[t, 8:136, :] = wx[t * 128 : t * 128 + 128, :].T
        nt[t, 4:8, :] = rims[t][0:4]
        nt[t, 136:140, :] = rims[t][4:8]
    total = taps[1, 0] * nt[0, 4:132, :]
    for t in range(1, 9):
        total = total + taps[1, t] * nt[0, 4 + t : 132 + t, :]
    total = total.T
    for n in range(8):
        nz[n // 4, 4 + n % 4] = total[n * 16 : n * 16 + 16]
    left = taps[1, 0] * nt[1, 4:132, :]
    for t in range(1, 5):
        left = left + taps[1, t] * nt[1, 4 + t : 132 + t, :]
    total = left
    for t in range(5, 9):
        total = total + taps[1, t] * nt[1, 4 + t : 132 + t, :]
    own = left[0:64]
    for t in range(5, 9):
        own = own + taps[1, t] * nt[1, 68 + t : 132 + t, :]
    front = jnp.where(lax.broadcasted_iota(jnp.int32, (64, 128), 1) < 64, total[0:64], own)
    total = jnp.concatenate([front, total[64:128]], axis=0).T
    for n in range(8, 12):
        nz[n // 4, 4 + n % 4] = total[(n - 8) * 16 : (n - 8) * 16 + 16]
    for c in range(3):
        gr[gz, c] = jnp.where(
            first_half, total[64 + c * 8 : 72 + c * 8], swap_halves(total[88 + c * 8 : 96 + c * 8])
        )
    noise_z = [
        send(14, nz.at[:, pl.ds(4, 4)], nz.at[:, pl.ds(0, 4)], next_z),
        send(15, nz.at[:, pl.ds(4, 4)], nz.at[:, pl.ds(8, 4)], last_z),
    ]
    noise_column, noise_column_sent = column(gr, gr_send, gr_recv)

    for copy in state_x:
        copy.wait_recv()
    lax.fori_loop(0, 3, flux_x, 0)
    lax.fori_loop(19, 22, flux_x, 0)
    for k in (0, 1, 2, 19, 20, 21):
        state = [ux[k * 32 + 24 + f : k * 32 + 25 + f, :] for f in range(5)]
        target = k if k < 3 else k - 8
        for f, entry in enumerate(flux_alone(state, 1)):
            fx[target * 32 + 24 + f : target * 32 + 25 + f, :] = entry
    for copy in state_x:
        copy.wait_send()
    for k in (11, 12, 13):
        ux[k * 32 + 24 : k * 32 + 32, :] = ux[(k + 8) * 32 + 24 : (k + 8) * 32 + 32, :]

    def store(ref, n, group, rows):
        for k, value in enumerate(prepare([rows[k + 1] - rows[k] for k in range(len(rows) - 1)], n == 0)):
            ref[n, group, k] = value

    for n, ref in enumerate((fx, ux)):

        def steps_x(group, carry):
            base = pl.multiple_of(group * 8, 8)
            store(d16, n, group, [ref[pl.ds(k * 32 + base, 8), :] for k in range(22)])
            return carry

        lax.fori_loop(0, 3, steps_x, 0)
        store(d8, n, 0, [ref[k * 32 + 24 : k * 32 + 32, :] for k in range(14)])

    for copy in state_y:
        copy.wait_recv()
    for n in range(2):

        def steps_y(t, carry):
            store(d16, n, 3 + t, [ty[3 - 3 * n + t, pl.ds(5 + k, 8, stride=16), :] for k in range(22)])
            return carry

        lax.fori_loop(0, 3, steps_y, 0)
    for copy in state_y:
        copy.wait_send()
    for n, t in enumerate((7, 6)):
        ty[t, 72:80, :] = ty[t, 136:144, :]
        store(d8, n, 1, [ty[t, pl.ds(5 + k, 8, stride=8), :] for k in range(14)])

    for copy in state_z:
        copy.wait_recv()
    for k in (0, 1, 2, 7, 8, 9):
        state = [uz[f, k] for f in range(5)]
        for f, entry in enumerate(flux_alone(state, 3)):
            fz[f, k] = entry

    def steps_z(f, carry):
        for n, ref in enumerate((fz, uz)):
            for h in range(2):
                store(dz, n, f * 2 + h, [ref[f, k, h * 8 : h * 8 + 8, :] for k in range(10)])
        return carry

    lax.fori_loop(0, 5, steps_z, 0)
    block = jnp.int32(0)
    for j in range(GZ):
        block = block + j * (owner[j] == gz).astype(jnp.int32)

    def mixed(left, right):
        return jnp.where(first_half, swap_halves(left), swap_halves(right))

    around = [lax.rem(block + GZ + m, GZ) for m in range(-2, 3)]
    for copy in state_column:
        copy.wait_recv()
    pairs_u, pairs_f = [], []
    for j in around:
        state = [gs[owner[j], f] for f in range(5)]
        pairs_u.append(state)
        pairs_f.append(flux_alone(state, 3))
    for n, pairs in enumerate((pairs_f, pairs_u)):
        for f in range(5):
            planes = []
            for j in range(-3, 4):
                m = (j + 4) // 2
                planes.append(pairs[m][f] if j % 2 == 0 else mixed(pairs[m][f], pairs[m + 1][f]))
            store(d1, n, f, planes)

    second_round = total_wait(sp2, 15, s2_send, s2_recv)
    second_round.wait_recv()
    speeds = jnp.max(sp2[...], axis=0, keepdims=True)
    front_row = lax.broadcasted_iota(jnp.int32, (1, 128), 1) < 64
    speed_fine = jnp.broadcast_to(
        jnp.max(jnp.where(front_row, speeds, 0.0), axis=1, keepdims=True), (8, 128)
    )
    speed_coarse = jnp.broadcast_to(
        jnp.max(jnp.where(front_row, 0.0, speeds), axis=1, keepdims=True), (8, 128)
    )

    def taken(ref, n, g, cells):
        return [ref[n, g, k] for k in range(3 * cells + 8)]

    def sweep_16(g):
        for k, out in enumerate(sweep(taken(d16, 0, g, 16), taken(d16, 1, g, 16), speed_fine, 16)):
            a16[pl.ds(g * 128 + k, 8, stride=16), :] = out

    def sweep_y(g, carry):
        sweep_16(3 + g)
        return carry

    def sweep_x(g, carry):
        sweep_16(g)
        row = pl.multiple_of(g * 128, 128)
        ay[pl.ds(row, 128), :] = a16[pl.ds(384 + row, 128), :].T
        return carry

    def sweep_z(g, carry):
        for z, out in enumerate(sweep(taken(dz, 0, g, 4), taken(dz, 1, g, 4), speed_fine, 4)):
            az[g, z] = out
        return carry

    def sweep_8(g, carry):
        for k, out in enumerate(sweep(taken(d8, 0, g, 8), taken(d8, 1, g, 8), speed_coarse, 8)):
            a8[pl.ds(g * 64 + k, 8, stride=8), :] = out
        return carry

    def sweep_1(g, carry):
        a1[g] = sweep(taken(d1, 0, g, 1), taken(d1, 1, g, 1), speed_coarse, 1)[0]
        return carry

    lax.fori_loop(0, 3, sweep_y, 0)
    lax.fori_loop(0, 3, sweep_x, 0)
    lax.fori_loop(0, 10, sweep_z, 0)
    lax.fori_loop(0, 2, sweep_8, 0)
    lax.fori_loop(0, 5, sweep_1, 0)

    for copy in noise_z:
        copy.wait_recv()
    for h in range(2):

        def noise_along_z(c, carry):
            planes = [nz[c, z, h * 8 : h * 8 + 8, :] for z in range(12)]
            for z in range(4):
                total = taps[2, 0] * planes[z]
                for t in range(1, 9):
                    total = total + taps[2, t] * planes[z + t]
                force[c * 4 + z, h * 8 : h * 8 + 8, :] = total
            return carry

        lax.fori_loop(0, 3, noise_along_z, 0)

    def sources(z, carry):
        state = [us[pl.ds(pl.multiple_of((f * 4 + z) * 16, 16), 16), :] for f in range(4)]
        push = [force[c * 4 + z] for c in range(3)]
        for c in range(3):
            force[c * 4 + z] = state[0] * push[c]
        force[12 + z] = state[1] * push[0] + state[2] * push[1] + state[3] * push[2]
        return carry

    lax.fori_loop(0, 4, sources, 0)
    for copy in noise_column:
        copy.wait_recv()
    push = []
    for c in range(3):
        pairs = [gr[j, c] for j in around]
        total = taps[2, 0] * pairs[0]
        for t in range(1, 9):
            plane = pairs[t // 2] if t % 2 == 0 else mixed(pairs[t // 2], pairs[t // 2 + 1])
            total = total + taps[2, t] * plane
        push.append(2.0 * total)
    work = coarse[1] * push[0] + coarse[2] * push[1] + coarse[3] * push[2]
    coarse_source = [None, coarse[0] * push[0], coarse[0] * push[1], coarse[0] * push[2], work]
    for f in range(1, 5):
        fcp[f * 8 : f * 8 + 8, :] = coarse_source[f]

    rate_fine = 0.1 / speed_fine
    rate_coarse = 0.1 / speed_coarse
    for index in range(40):
        f, z, h = index // 8, (index // 2) % 4, index % 2
        row = index * 8
        change = -0.5 * (a16[row : row + 8, :] + ay[row : row + 8, :] + az[f * 2 + h, z])
        if f > 0:
            change = change + force[(f - 1) * 4 + z, h * 8 : h * 8 + 8, :]
        fine_out[row : row + 8, :] = 0.25 * us[row : row + 8, :] + rate_fine * change

    along_y = a8[64:128, :]
    turned = jnp.concatenate([along_y, along_y], axis=0).T
    along_y = jnp.where(first_half_40, turned[0:40], turned[64:104])
    for f in range(5):
        change = -0.5 * (a8[f * 8 : f * 8 + 8, :] + along_y[f * 8 : f * 8 + 8] + a1[f])
        if f > 0:
            change = change + fcp[f * 8 : f * 8 + 8, :]
        result = 0.25 * cp[f * 8 : f * 8 + 8, :] + rate_coarse * change
        coarse_out[f * 16 : f * 16 + 8, :] = result[:, 0:64]
        coarse_out[f * 16 + 8 : f * 16 + 16, :] = swap_halves(result)[:, 0:64]

    first_round.wait_send()
    second_round.wait_send()
    for copy in noise_xy + state_z + noise_z:
        copy.wait_send()
    state_column_sent.wait_send()
    noise_column_sent.wait_send()


def local(fine_start, fine_section, fine_noise, coarse_start, coarse_section, taps, owner):
    f32 = jnp.float32
    vmem = pl.BlockSpec(memory_space=pltpu.VMEM)
    hbm = pl.BlockSpec(memory_space=pltpu.HBM)
    dma = pltpu.SemaphoreType.DMA
    fine, coarse = pl.pallas_call(
        kernel,
        out_shape=(jax.ShapeDtypeStruct((320, 128), f32), jax.ShapeDtypeStruct((80, 64), f32)),
        in_specs=[hbm] * 5,
        out_specs=(vmem, vmem),
        scratch_shapes=[
            pltpu.VMEM((320, 128), f32),
            pltpu.VMEM((192, 128), f32),
            pltpu.VMEM((80, 64), f32),
            pltpu.SMEM((3, 9), f32),
            pltpu.SMEM((8,), jnp.int32),
            pltpu.VMEM((32, 128), f32),
            pltpu.VMEM((16, 128), f32),
            pltpu.VMEM((40, 128), f32),
            pltpu.VMEM((40, 128), f32),
            pltpu.VMEM((704, 128), f32),
            pltpu.VMEM((704, 128), f32),
            pltpu.VMEM((8, 144, 128), f32),
            pltpu.VMEM((320, 128), f32),
            pltpu.VMEM((5, 10, 16, 128), f32),
            pltpu.VMEM((5, 10, 16, 128), f32),
            pltpu.VMEM((3, 12, 16, 128), f32),
            pltpu.VMEM((8, 5, 8, 128), f32),
            pltpu.VMEM((8, 3, 8, 128), f32),
            pltpu.VMEM((15, 32, 128), f32),
            pltpu.VMEM((2, 16, 128), f32),
            pltpu.VMEM((2, 2, 32, 128), f32),
            pltpu.VMEM((256, 128), f32),
            pltpu.VMEM((2, 144, 128), f32),
            pltpu.VMEM((16, 16, 128), f32),
            pltpu.VMEM((96, 128), f32),
            pltpu.VMEM((2, 10, 20, 8, 128), f32),
            pltpu.VMEM((2, 6, 56, 8, 128), f32),
            pltpu.VMEM((2, 2, 32, 8, 128), f32),
            pltpu.VMEM((2, 5, 11, 8, 128), f32),
            pltpu.VMEM((10, 4, 8, 128), f32),
            pltpu.VMEM((768, 128), f32),
            pltpu.VMEM((384, 128), f32),
            pltpu.VMEM((128, 128), f32),
            pltpu.VMEM((5, 8, 128), f32),
            dma((5,)),
            pltpu.SemaphoreType.REGULAR,
            dma, dma, dma, dma, dma, dma((7,)), dma, dma((7,)), dma((16,)), dma((16,)),
        ],
        compiler_params=pltpu.CompilerParams(
            collective_id=0, has_side_effects=True, vmem_limit_bytes=24 * 1024 * 1024
        ),
        name="section",
    )(
        *(
            pltpu.with_memory_space_constraint(operand, pltpu.HBM)
            for operand in (
                fine_section.reshape(320, 128), fine_noise.reshape(192, 128),
                coarse_section.reshape(80, 64), taps, owner,
            )
        )
    )
    return (
        0.75 * fine_start + fine.reshape(fine_start.shape),
        0.75 * coarse_start + coarse.reshape(coarse_start.shape),
    )


def solution(mesh):
    cells = P(None, "gz", "gx", "gy")
    return jax.shard_map(
        local,
        mesh=mesh,
        in_specs=(cells, cells, cells, cells, cells, P(), P()),
        out_specs=(cells, cells),
        check_vma=False,
    )
```

```python
import jax
import jax.numpy as jnp
from jax import lax
from jax.experimental import pallas as pl
from jax.experimental.pallas import tpu as pltpu
from jax.sharding import PartitionSpec as P

MESH = pl.DeviceIdType.MESH
GX, GY, GZ = 16, 4, 8
GAMMA = 1.4
INDICATOR_EPS = 2e-06
RESTRICT_SCALE = 0.35355339059327373
NEAR = sorted(
    ((i, j) for i in range(GY) for j in range(GZ) if (i, j) != (0, 0)),
    key=lambda step: -((step[0] + 1) // 2 % 2 + 2 * (step[1] // 4) + min(step[1] % 4, -step[1] % 4)),
)
ALONG = [8, 7, 9, 6, 10, 5, 11, 4, 12, 3, 13, 2, 14, 1, 15]
CLOSE = [4, 12, 3, 13, 2, 14, 1, 15]
CORNERS = [(1, 1), (1, GY - 1), (GX - 1, 1), (GX - 1, GY - 1)]


def pressure_of(state, inverse):
    kinetic = 0.5 * (state[1] * state[1] + state[2] * state[2] + state[3] * state[3])
    return (GAMMA - 1.0) * (state[4] - kinetic * inverse)


def flux_entries(state, inverse, pressure, component):
    velocity = state[component] * inverse
    entries = [
        state[component],
        state[1] * velocity,
        state[2] * velocity,
        state[3] * velocity,
        (state[4] + pressure) * velocity,
    ]
    entries[component] = entries[component] + pressure
    return entries


def flux_alone(state, component):
    inverse = 1.0 / state[0]
    return flux_entries(state, inverse, pressure_of(state, inverse), component)


def fastest_of(state, inverse, pressure):
    largest = jnp.maximum(jnp.maximum(jnp.abs(state[1]), jnp.abs(state[2])), jnp.abs(state[3]))
    return largest * inverse + jnp.sqrt(GAMMA * pressure * inverse)


def prepare(steps, flux):
    cells = len(steps) - 5
    bends = [steps[k - 1] - 2.0 * steps[k] + steps[k + 1] for k in range(1, cells + 4)]
    if flux:
        linear = [
            steps[c + 2] + steps[c + 3] + (steps[c + 2] - steps[c + 4] - steps[c + 1] + steps[c + 3]) * (1.0 / 6.0)
            for c in range(cells)
        ]
    else:
        linear = [
            steps[c + 2] - steps[c + 3]
            + (steps[c + 4] - steps[c + 1] + 3.0 * (steps[c + 3] - steps[c + 2])) * (1.0 / 6.0)
            for c in range(cells)
        ]
    return list(steps) + bends + linear


def indicators(steps):
    squares = [e * e for e in steps]
    raised = [(2.0 / 3.0) * x + 0.5 * INDICATOR_EPS for x in squares]
    low, mid, high = [], [], []
    for i in range(len(steps) - 1):
        cross = steps[i] * steps[i + 1]
        base = raised[i] + raised[i + 1] - (11.0 / 6.0) * cross
        low.append(base + squares[i + 1])
        high.append(base + squares[i])
        mid.append(base + cross)
    return low, mid, high


def side(low, mid, high, first, second):
    to_mid = low * pltpu.reciprocal(mid, approx=True)
    to_high = low * pltpu.reciprocal(high, approx=True)
    w2 = 1.5 * (to_high * to_high)
    total = 3.0 * (to_mid * to_mid) + w2 + 0.5
    return (first + w2 * second) * pltpu.reciprocal(total, approx=True)


def sweep(flux, state, speed, cells):
    steps, bends = cells + 5, cells + 3
    scaled = [speed * u for u in state]
    up = [f + u for f, u in zip(flux[:steps], scaled[:steps])]
    down = [f - u for f, u in zip(flux[:steps], scaled[:steps])]
    low_u, mid_u, high_u = indicators(up[: cells + 4])
    low_d, mid_d, high_d = indicators(down)
    bend_u = [f + u for f, u in zip(flux[steps : steps + bends], scaled[steps : steps + bends])]
    bend_d = [f - u for f, u in zip(flux[steps : steps + bends], scaled[steps : steps + bends])]
    faces = []
    for j in range(cells + 1):
        right = side(low_u[j], mid_u[j + 1], high_u[j + 2], bend_u[j], bend_u[j + 1])
        left = side(high_d[j + 3], mid_d[j + 2], low_d[j + 1], bend_d[j + 2], bend_d[j + 1])
        faces.append(left - right)
    return [
        flux[steps + bends + c] + scaled[steps + bends + c] + (faces[c + 1] - faces[c]) * (1.0 / 6.0)
        for c in range(cells)
    ]


def swap_halves(values):
    return pltpu.roll(values, 64, 1)


def kernel(
    us_hbm, noise_hbm, cs_hbm, taps_hbm, owner_hbm, fine_out, coarse_out,
    us, noise, cs, taps, owner, sp1, sp2, cp, fcp, ux, fx, ty, fy, uz, fz, nz, gs, gr, nx, pk, hb, wx, nt,
    force, halves, dz, d16, d8, d1, az, a16, ay, a8, a1,
    ins, far_sem, s1_send, s1_recv, s2_send, s2_recv, gs_send, gs_recv, gr_send, gr_recv, hs, hr,
):
    loads = [
        pltpu.make_async_copy(src, dst, ins.at[n])
        for n, (src, dst) in enumerate(
            ((us_hbm, us), (cs_hbm, cs), (noise_hbm, noise), (taps_hbm, taps), (owner_hbm, owner))
        )
    ]
    for load in loads:
        load.start()
    gx, gy, gz = lax.axis_index("gx"), lax.axis_index("gy"), lax.axis_index("gz")

    def near(step):
        return {"gy": lax.rem(gy + step[0], GY), "gz": lax.rem(gz + step[1], GZ)}

    def along(step):
        return {"gx": lax.rem(gx + step, GX)}

    def corner(step):
        return {"gx": lax.rem(gx + step[0], GX), "gy": lax.rem(gy + step[1], GY)}

    barrier = pltpu.get_barrier_semaphore()
    greeted = [along(step) for step in CLOSE] + [near(step) for step in NEAR] + [corner(step) for step in CORNERS]
    for device in greeted:
        pl.semaphore_signal(barrier, inc=1, device_id=device, device_id_type=MESH)

    lane = lax.broadcasted_iota(jnp.int32, (8, 128), 1)
    first_half = lane < 64
    first_half_40 = lax.broadcasted_iota(jnp.int32, (40, 128), 1) < 64

    def cells(z):
        return [us[(f * 4 + z) * 16 : (f * 4 + z) * 16 + 16, :] for f in range(5)]

    loads[0].wait()
    best = jnp.zeros((16, 128), jnp.float32)
    for z in range(4):
        state = cells(z)
        inverse = 1.0 / state[0]
        best = jnp.maximum(best, fastest_of(state, inverse, pressure_of(state, inverse)))
    best = jnp.maximum(best[0:8], best[8:16])
    loads[1].wait()
    for f in range(5):
        cp[f * 8 : f * 8 + 8, :] = jnp.concatenate(
            [cs[f * 16 : f * 16 + 8, :], cs[f * 16 + 8 : f * 16 + 16, :]], axis=1
        )
    coarse = [cp[f * 8 : f * 8 + 8, :] for f in range(5)]
    coarse_inverse = 1.0 / coarse[0]
    coarse_pressure = pressure_of(coarse, coarse_inverse)
    coarse_best = fastest_of(coarse, coarse_inverse, coarse_pressure)
    best = jnp.where(
        first_half,
        jnp.maximum(best, swap_halves(best)),
        jnp.maximum(coarse_best, swap_halves(coarse_best)),
    )
    sp1[31:32, :] = jnp.max(best, axis=0, keepdims=True)

    pl.semaphore_wait(barrier, len(greeted))
    next_z, last_z = near((0, 1)), near((0, GZ - 1))
    next_x, last_x = along(1), along(GX - 1)
    next_y, last_y = near((1, 0)), near((GY - 1, 0))

    def send(index, src, dst, device):
        copy = pltpu.make_async_remote_copy(
            src_ref=src, dst_ref=dst, send_sem=hs.at[index], recv_sem=hr.at[index],
            device_id=device, device_id_type=MESH,
        )
        copy.start()
        return copy

    for n, step in enumerate(NEAR):
        pltpu.make_async_remote_copy(
            src_ref=sp1.at[pl.ds(31, 1)], dst_ref=sp1.at[pl.ds(n, 1)], send_sem=s1_send,
            recv_sem=s1_recv, device_id=near(step), device_id_type=MESH,
        ).start()
    for step in (4, GX - 4):
        pl.semaphore_signal(far_sem, inc=1, device_id=along(step), device_id_type=MESH)

    for load in loads[2:]:
        load.wait()
    eighth = jnp.bitwise_and(lane, 7)
    group_of_lane = lax.shift_right_logical(lane, 3)
    packed = [jnp.zeros((8, 128), jnp.float32) for _ in range(2)]
    for c in range(3):
        for z in range(4):
            n = c * 4 + z
            for h in range(2):
                tile = noise[n * 16 + h * 8 : n * 16 + h * 8 + 8, :]
                nx[n, 8 + h * 8 : 16 + h * 8, :] = tile
                packed[h] = jnp.where(group_of_lane == n, pltpu.roll(tile, (n * 8 + 4) % 128, 1), packed[h])
        for pair in range(2):
            row = (c * 4 + 2 * pair) * 16
            halves[(c * 2 + pair) * 16 : (c * 2 + pair) * 16 + 16, :] = (
                noise[row : row + 16, :] + noise[row + 16 : row + 32, :]
            )
    for h in range(2):
        pk[0, h * 8 : h * 8 + 8, :] = packed[h]
    from_lane = lax.broadcasted_iota(jnp.int32, (128, 128), 0)
    to_lane = lax.broadcasted_iota(jnp.int32, (128, 128), 1)
    restricted = jnp.zeros((24, 128), jnp.float32)
    for pair in range(2):
        rows = jnp.concatenate(
            [
                halves[pl.ds((c * 2 + pair) * 16, 8, stride=2), :]
                + halves[pl.ds((c * 2 + pair) * 16 + 1, 8, stride=2), :]
                for c in range(3)
            ],
            axis=0,
        )
        pick = (lax.shift_right_logical(from_lane, 1) + 64 * pair == to_lane).astype(jnp.float32)
        restricted = restricted + lax.dot(
            rows, pick, precision=lax.Precision.HIGHEST, preferred_element_type=jnp.float32
        )
    restricted = restricted * RESTRICT_SCALE
    coarse_packed = jnp.zeros((8, 128), jnp.float32)
    for c in range(3):
        tile = restricted[c * 8 : c * 8 + 8]
        nx[12 + c, 8:16, :] = tile
        nx[12 + c, 16:24, :] = tile
        swapped = swap_halves(tile)
        for p in range(2):
            m = c * 2 + p
            doubled = jnp.where(first_half, tile, swapped) if p == 0 else jnp.where(first_half, swapped, tile)
            coarse_packed = jnp.where(group_of_lane == m, pltpu.roll(doubled, m * 8 + 4, 1), coarse_packed)
    pk[1, 0:8, :] = coarse_packed
    pk[1, 8:16, :] = coarse_packed
    for f in range(5):
        gs[gz, f] = coarse[f]

    noise_xy = [
        send(0, nx.at[:, pl.ds(16, 8)], nx.at[:, pl.ds(0, 8)], next_x),
        send(1, nx.at[:, pl.ds(8, 8)], nx.at[:, pl.ds(24, 8)], last_x),
        send(2, pk, hb.at[0, :, pl.ds(8, 16)], next_y),
        send(3, pk, hb.at[1, :, pl.ds(8, 16)], last_y),
        send(4, pk.at[:, pl.ds(8, 8)], hb.at[0, :, pl.ds(0, 8)], corner(CORNERS[0])),
        send(5, pk.at[:, pl.ds(8, 8)], hb.at[1, :, pl.ds(0, 8)], corner(CORNERS[1])),
        send(6, pk.at[:, pl.ds(0, 8)], hb.at[0, :, pl.ds(24, 8)], corner(CORNERS[2])),
        send(7, pk.at[:, pl.ds(0, 8)], hb.at[1, :, pl.ds(24, 8)], corner(CORNERS[3])),
    ]

    for z in range(4):
        state = cells(z)
        inverse = 1.0 / state[0]
        pressure = pressure_of(state, inverse)
        for f, entry in enumerate(flux_entries(state, inverse, pressure, 2)):
            fy[(f * 4 + z) * 16 : (f * 4 + z) * 16 + 16, :] = entry
        for f, entry in enumerate(flux_entries(state, inverse, pressure, 3)):
            fz[f, 3 + z] = entry
        for f in range(5):
            uz[f, 3 + z] = state[f]

    state_z = [
        send(12, uz.at[:, pl.ds(4, 3)], uz.at[:, pl.ds(0, 3)], next_z),
        send(13, uz.at[:, pl.ds(3, 3)], uz.at[:, pl.ds(7, 3)], last_z),
    ]

    def column(ref, send_sem, recv_sem):
        copies = []
        for step in range(1, GZ):
            copy = pltpu.make_async_remote_copy(
                src_ref=ref.at[gz], dst_ref=ref.at[gz], send_sem=send_sem, recv_sem=recv_sem.at[step - 1],
                device_id=near((0, step)), device_id_type=MESH,
            )
            copy.start()
            origin = lax.rem(gz + GZ - step, GZ)
            copies.append(
                pltpu.make_async_remote_copy(
                    src_ref=ref.at[gz], dst_ref=ref.at[origin], send_sem=send_sem,
                    recv_sem=recv_sem.at[step - 1], device_id=next_z, device_id_type=MESH,
                )
            )
        whole = pltpu.make_async_remote_copy(
            src_ref=ref.at[pl.ds(0, GZ - 1)], dst_ref=ref.at[pl.ds(0, GZ - 1)], send_sem=send_sem,
            recv_sem=recv_sem.at[0], device_id=next_z, device_id_type=MESH,
        )
        return copies, whole

    state_column, state_column_sent = column(gs, gs_send, gs_recv)

    for k in range(16):
        for group in range(2):
            ux[(3 + k) * 32 + group * 8 : (3 + k) * 32 + group * 8 + 8, :] = us[
                pl.ds(group * 128 + k, 8, stride=16), :
            ]
        ux[(3 + k) * 32 + 16 : (3 + k) * 32 + 20, :] = us[pl.ds(256 + k, 4, stride=16), :]
    for k in range(8):
        row = cp[pl.ds(k, 5, stride=8), :]
        ux[(3 + k) * 32 + 24 : (3 + k) * 32 + 29, :] = row
        ux[(11 + k) * 32 + 24 : (11 + k) * 32 + 29, :] = row

    state_x = [
        send(8, ux.at[pl.ds(16 * 32, 96)], ux.at[pl.ds(0, 96)], next_x),
        send(9, ux.at[pl.ds(3 * 32, 96)], ux.at[pl.ds(19 * 32, 96)], last_x),
    ]

    for t in range(2):
        ty[t, 8:136, :] = us[t * 128 : t * 128 + 128, :].T
        ty[3 + t, 8:136, :] = fy[t * 128 : t * 128 + 128, :].T
    tail = us[256:320, :]
    ty[2, 8:136, :] = jnp.concatenate([tail, tail], axis=0).T
    tail = fy[256:320, :]
    ty[5, 8:136, :] = jnp.concatenate([tail, tail], axis=0).T
    for f, entry in enumerate(flux_entries(coarse, coarse_inverse, coarse_pressure, 2)):
        fcp[f * 8 : f * 8 + 8, :] = entry
    for t, ref in ((6, cp), (7, fcp)):
        both = ref[0:40, :]
        swapped = swap_halves(both)
        front = jnp.where(first_half_40, both, swapped)
        back = jnp.where(first_half_40, swapped, both)
        ty[t, 8:136, :] = jnp.concatenate([front, front[0:24], back, back[0:24]], axis=0).T
    state_y = [
        send(10, ty.at[:, pl.ds(128, 8)], ty.at[:, pl.ds(0, 8)], next_y),
        send(11, ty.at[:, pl.ds(8, 8)], ty.at[:, pl.ds(136, 8)], last_y),
    ]

    def flux_x(k, carry):
        base = k * 32
        state = [ux[pl.ds(base + 4 * f, 4), :] for f in range(5)]
        for f, entry in enumerate(flux_alone(state, 1)):
            fx[pl.ds(base + 4 * f, 4), :] = entry
        return carry

    lax.fori_loop(3, 19, flux_x, 0)
    for f, entry in enumerate(flux_entries(coarse, coarse_inverse, coarse_pressure, 1)):
        fcp[f * 8 : f * 8 + 8, :] = entry
    for k in range(8):
        fx[(3 + k) * 32 + 24 : (3 + k) * 32 + 29, :] = fcp[pl.ds(k, 5, stride=8), :]

    def total_wait(ref, count, send_sem, recv_sem):
        return pltpu.make_async_remote_copy(
            src_ref=ref.at[pl.ds(0, count)], dst_ref=ref.at[pl.ds(0, count)], send_sem=send_sem,
            recv_sem=recv_sem, device_id=next_x, device_id_type=MESH,
        )

    first_round = total_wait(sp1, 31, s1_send, s1_recv)
    first_round.wait_recv()
    sp2[15:16, :] = jnp.max(sp1[...], axis=0, keepdims=True)
    pl.semaphore_wait(far_sem, 2)
    for n, step in enumerate(ALONG):
        pltpu.make_async_remote_copy(
            src_ref=sp2.at[pl.ds(15, 1)], dst_ref=sp2.at[pl.ds(n, 1)], send_sem=s2_send,
            recv_sem=s2_recv, device_id=along(step), device_id_type=MESH,
        ).start()

    for copy in noise_xy:
        copy.wait_recv()

    def noise_along_x(n, carry):
        total = taps[0, 0] * nx[n, 4:20, :]
        for t in range(1, 9):
            total = total + taps[0, t] * nx[n, 4 + t : 20 + t, :]
        wx[pl.ds(pl.multiple_of(n * 16, 16), 16), :] = total
        return carry

    lax.fori_loop(0, 12, noise_along_x, 0)
    for c in range(3):
        total = taps[0, 0] * nx[12 + c, 4:12, :]
        for t in range(1, 9):
            base = 4 + t if t <= 4 else 12 + t
            total = total + taps[0, t] * nx[12 + c, base : base + 8, :]
        swapped = swap_halves(total)
        wx[192 + c * 8 : 200 + c * 8, :] = jnp.where(first_half, total, swapped)
        wx[216 + c * 8 : 224 + c * 8, :] = jnp.where(first_half, swapped, total)
    for b in range(2):
        for r in range(4):
            hb[0, b, r * 8 : r * 8 + 8, :] = jnp.where(
                eighth < 4, hb[0, b, r * 8 : r * 8 + 8, :], hb[1, b, r * 8 : r * 8 + 8, :]
            )
    beside = taps[0, 0] * hb[0, 0, 4:20, :]
    for t in range(1, 9):
        beside = beside + taps[0, t] * hb[0, 0, 4 + t : 20 + t, :]
    coarse_beside = taps[0, 0] * hb[0, 1, 4:12, :]
    for t in range(1, 9):
        base = 4 + t if t <= 4 else 12 + t
        coarse_beside = coarse_beside + taps[0, t] * hb[0, 1, base : base + 8, :]

    turned = jnp.concatenate([beside, coarse_beside, jnp.zeros((104, 128), jnp.float32)], axis=0).T
    rims = [jnp.zeros((8, 128), jnp.float32) for _ in range(2)]
    sixteenth = lax.shift_right_logical(lane, 4)
    for n in range(12):
        shift = (n % 8) * 16
        rolled = pltpu.roll(turned[n * 8 : n * 8 + 8], shift, 1) if shift else turned[n * 8 : n * 8 + 8]
        rims[n // 8] = jnp.where(sixteenth == n % 8, rolled, rims[n // 8])
    for c in range(3):
        for p in range(2):
            m = c * 2 + p
            target = 64 + p * 24 + c * 8
            rolled = pltpu.roll(turned[m * 8 : m * 8 + 8], target - 16, 1)
            rims[1] = jnp.where(group_of_lane == target // 8, rolled, rims[1])
    for t in range(2):
        nt[t, 8:136, :] = wx[t * 128 : t * 128 + 128, :].T
        nt[t, 4:8, :] = rims[t][0:4]
        nt[t, 136:140, :] = rims[t][4:8]
    total = taps[1, 0] * nt[0, 4:132, :]
    for t in range(1, 9):
        total = total + taps[1, t] * nt[0, 4 + t : 132 + t, :]
    total = total.T
    for n in range(8):
        nz[n // 4, 4 + n % 4] = total[n * 16 : n * 16 + 16]
    left = taps[1, 0] * nt[1, 4:132, :]
    for t in range(1, 5):
        left = left + taps[1, t] * nt[1, 4 + t : 132 + t, :]
    total = left
    for t in range(5, 9):
        total = total + taps[1, t] * nt[1, 4 + t : 132 + t, :]
    own = left[0:64]
    for t in range(5, 9):
        own = own + taps[1, t] * nt[1, 68 + t : 132 + t, :]
    front = jnp.where(lax.broadcasted_iota(jnp.int32, (64, 128), 1) < 64, total[0:64], own)
    total = jnp.concatenate([front, total[64:128]], axis=0).T
    for n in range(8, 12):
        nz[n // 4, 4 + n % 4] = total[(n - 8) * 16 : (n - 8) * 16 + 16]
    for c in range(3):
        gr[gz, c] = jnp.where(
            first_half, total[64 + c * 8 : 72 + c * 8], swap_halves(total[88 + c * 8 : 96 + c * 8])
        )
    noise_z = [
        send(14, nz.at[:, pl.ds(4, 4)], nz.at[:, pl.ds(0, 4)], next_z),
        send(15, nz.at[:, pl.ds(4, 4)], nz.at[:, pl.ds(8, 4)], last_z),
    ]
    noise_column, noise_column_sent = column(gr, gr_send, gr_recv)

    for copy in state_x:
        copy.wait_recv()
    lax.fori_loop(0, 3, flux_x, 0)
    lax.fori_loop(19, 22, flux_x, 0)
    for k in (0, 1, 2, 19, 20, 21):
        state = [ux[k * 32 + 24 + f : k * 32 + 25 + f, :] for f in range(5)]
        target = k if k < 3 else k - 8
        for f, entry in enumerate(flux_alone(state, 1)):
            fx[target * 32 + 24 + f : target * 32 + 25 + f, :] = entry
    for copy in state_x:
        copy.wait_send()
    for k in (11, 12, 13):
        ux[k * 32 + 24 : k * 32 + 32, :] = ux[(k + 8) * 32 + 24 : (k + 8) * 32 + 32, :]

    def store(ref, n, group, rows):
        for k, value in enumerate(prepare([rows[k + 1] - rows[k] for k in range(len(rows) - 1)], n == 0)):
            ref[n, group, k] = value

    for n, ref in enumerate((fx, ux)):

        def steps_x(group, carry):
            base = pl.multiple_of(group * 8, 8)
            store(d16, n, group, [ref[pl.ds(k * 32 + base, 8), :] for k in range(22)])
            return carry

        lax.fori_loop(0, 3, steps_x, 0)
        store(d8, n, 0, [ref[k * 32 + 24 : k * 32 + 32, :] for k in range(14)])

    for copy in state_y:
        copy.wait_recv()
    for n in range(2):

        def steps_y(t, carry):
            store(d16, n, 3 + t, [ty[3 - 3 * n + t, pl.ds(5 + k, 8, stride=16), :] for k in range(22)])
            return carry

        lax.fori_loop(0, 3, steps_y, 0)
    for copy in state_y:
        copy.wait_send()
    for n, t in enumerate((7, 6)):
        ty[t, 72:80, :] = ty[t, 136:144, :]
        store(d8, n, 1, [ty[t, pl.ds(5 + k, 8, stride=8), :] for k in range(14)])

    for copy in state_z:
        copy.wait_recv()
    for k in (0, 1, 2, 7, 8, 9):
        state = [uz[f, k] for f in range(5)]
        for f, entry in enumerate(flux_alone(state, 3)):
            fz[f, k] = entry

    def steps_z(f, carry):
        for n, ref in enumerate((fz, uz)):
            for h in range(2):
                store(dz, n, f * 2 + h, [ref[f, k, h * 8 : h * 8 + 8, :] for k in range(10)])
        return carry

    lax.fori_loop(0, 5, steps_z, 0)
    block = jnp.int32(0)
    for j in range(GZ):
        block = block + j * (owner[j] == gz).astype(jnp.int32)

    def mixed(left, right):
        return jnp.where(first_half, swap_halves(left), swap_halves(right))

    around = [lax.rem(block + GZ + m, GZ) for m in range(-2, 3)]
    for copy in state_column:
        copy.wait_recv()
    pairs_u, pairs_f = [], []
    for j in around:
        state = [gs[owner[j], f] for f in range(5)]
        pairs_u.append(state)
        pairs_f.append(flux_alone(state, 3))
    for n, pairs in enumerate((pairs_f, pairs_u)):
        for f in range(5):
            planes = []
            for j in range(-3, 4):
                m = (j + 4) // 2
                planes.append(pairs[m][f] if j % 2 == 0 else mixed(pairs[m][f], pairs[m + 1][f]))
            store(d1, n, f, planes)

    second_round = total_wait(sp2, 15, s2_send, s2_recv)
    second_round.wait_recv()
    speeds = jnp.max(sp2[...], axis=0, keepdims=True)
    front_row = lax.broadcasted_iota(jnp.int32, (1, 128), 1) < 64
    speed_fine = jnp.broadcast_to(
        jnp.max(jnp.where(front_row, speeds, 0.0), axis=1, keepdims=True), (8, 128)
    )
    speed_coarse = jnp.broadcast_to(
        jnp.max(jnp.where(front_row, 0.0, speeds), axis=1, keepdims=True), (8, 128)
    )

    def taken(ref, n, g, cells):
        return [ref[n, g, k] for k in range(3 * cells + 8)]

    def sweep_16(g):
        for k, out in enumerate(sweep(taken(d16, 0, g, 16), taken(d16, 1, g, 16), speed_fine, 16)):
            a16[pl.ds(g * 128 + k, 8, stride=16), :] = out

    def sweep_y(g, carry):
        sweep_16(3 + g)
        return carry

    def sweep_x(g, carry):
        sweep_16(g)
        row = pl.multiple_of(g * 128, 128)
        ay[pl.ds(row, 128), :] = a16[pl.ds(384 + row, 128), :].T
        return carry

    def sweep_z(g):
        for z, out in enumerate(sweep(taken(dz, 0, g, 4), taken(dz, 1, g, 4), speed_fine, 4)):
            az[g, z] = out

    def sweep_five(half, carry):
        for n in range(5):
            sweep_z(half * 5 + n)
        return carry

    lax.fori_loop(0, 3, sweep_y, 0)
    lax.fori_loop(0, 3, sweep_x, 0)
    lax.fori_loop(0, 2, sweep_five, 0)
    for g in range(2):
        for k, out in enumerate(sweep(taken(d8, 0, g, 8), taken(d8, 1, g, 8), speed_coarse, 8)):
            a8[pl.ds(g * 64 + k, 8, stride=8), :] = out
    for g in range(5):
        a1[g] = sweep(taken(d1, 0, g, 1), taken(d1, 1, g, 1), speed_coarse, 1)[0]

    for copy in noise_z:
        copy.wait_recv()
    for h in range(2):

        def noise_along_z(c, carry):
            planes = [nz[c, z, h * 8 : h * 8 + 8, :] for z in range(12)]
            for z in range(4):
                total = taps[2, 0] * planes[z]
                for t in range(1, 9):
                    total = total + taps[2, t] * planes[z + t]
                force[c * 4 + z, h * 8 : h * 8 + 8, :] = total
            return carry

        lax.fori_loop(0, 3, noise_along_z, 0)

    def sources(z, carry):
        state = [us[pl.ds(pl.multiple_of((f * 4 + z) * 16, 16), 16), :] for f in range(4)]
        push = [force[c * 4 + z] for c in range(3)]
        for c in range(3):
            force[c * 4 + z] = state[0] * push[c]
        force[12 + z] = state[1] * push[0] + state[2] * push[1] + state[3] * push[2]
        return carry

    lax.fori_loop(0, 4, sources, 0)
    for copy in noise_column:
        copy.wait_recv()
    push = []
    for c in range(3):
        pairs = [gr[j, c] for j in around]
        total = taps[2, 0] * pairs[0]
        for t in range(1, 9):
            plane = pairs[t // 2] if t % 2 == 0 else mixed(pairs[t // 2], pairs[t // 2 + 1])
            total = total + taps[2, t] * plane
        push.append(2.0 * total)
    work = coarse[1] * push[0] + coarse[2] * push[1] + coarse[3] * push[2]
    coarse_source = [None, coarse[0] * push[0], coarse[0] * push[1], coarse[0] * push[2], work]
    for f in range(1, 5):
        fcp[f * 8 : f * 8 + 8, :] = coarse_source[f]

    rate_fine = 0.1 / speed_fine
    rate_coarse = 0.1 / speed_coarse
    for index in range(40):
        f, z, h = index // 8, (index // 2) % 4, index % 2
        row = index * 8
        change = -0.5 * (a16[row : row + 8, :] + ay[row : row + 8, :] + az[f * 2 + h, z])
        if f > 0:
            change = change + force[(f - 1) * 4 + z, h * 8 : h * 8 + 8, :]
        fine_out[row : row + 8, :] = 0.25 * us[row : row + 8, :] + rate_fine * change

    along_y = a8[64:128, :]
    turned = jnp.concatenate([along_y, along_y], axis=0).T
    along_y = jnp.where(first_half_40, turned[0:40], turned[64:104])
    for f in range(5):
        change = -0.5 * (a8[f * 8 : f * 8 + 8, :] + along_y[f * 8 : f * 8 + 8] + a1[f])
        if f > 0:
            change = change + fcp[f * 8 : f * 8 + 8, :]
        result = 0.25 * cp[f * 8 : f * 8 + 8, :] + rate_coarse * change
        coarse_out[f * 16 : f * 16 + 8, :] = result[:, 0:64]
        coarse_out[f * 16 + 8 : f * 16 + 16, :] = swap_halves(result)[:, 0:64]

    first_round.wait_send()
    second_round.wait_send()
    for copy in noise_xy + state_z + noise_z:
        copy.wait_send()
    state_column_sent.wait_send()
    noise_column_sent.wait_send()


def local(fine_start, fine_section, fine_noise, coarse_start, coarse_section, taps, owner):
    f32 = jnp.float32
    vmem = pl.BlockSpec(memory_space=pltpu.VMEM)
    hbm = pl.BlockSpec(memory_space=pltpu.HBM)
    dma = pltpu.SemaphoreType.DMA
    fine, coarse = pl.pallas_call(
        kernel,
        out_shape=(jax.ShapeDtypeStruct((320, 128), f32), jax.ShapeDtypeStruct((80, 64), f32)),
        in_specs=[hbm] * 5,
        out_specs=(vmem, vmem),
        scratch_shapes=[
            pltpu.VMEM((320, 128), f32),
            pltpu.VMEM((192, 128), f32),
            pltpu.VMEM((80, 64), f32),
            pltpu.SMEM((3, 9), f32),
            pltpu.SMEM((8,), jnp.int32),
            pltpu.VMEM((32, 128), f32),
            pltpu.VMEM((16, 128), f32),
            pltpu.VMEM((40, 128), f32),
            pltpu.VMEM((40, 128), f32),
            pltpu.VMEM((704, 128), f32),
            pltpu.VMEM((704, 128), f32),
            pltpu.VMEM((8, 144, 128), f32),
            pltpu.VMEM((320, 128), f32),
            pltpu.VMEM((5, 10, 16, 128), f32),
            pltpu.VMEM((5, 10, 16, 128), f32),
            pltpu.VMEM((3, 12, 16, 128), f32),
            pltpu.VMEM((8, 5, 8, 128), f32),
            pltpu.VMEM((8, 3, 8, 128), f32),
            pltpu.VMEM((15, 32, 128), f32),
            pltpu.VMEM((2, 16, 128), f32),
            pltpu.VMEM((2, 2, 32, 128), f32),
            pltpu.VMEM((256, 128), f32),
            pltpu.VMEM((2, 144, 128), f32),
            pltpu.VMEM((16, 16, 128), f32),
            pltpu.VMEM((96, 128), f32),
            pltpu.VMEM((2, 10, 20, 8, 128), f32),
            pltpu.VMEM((2, 6, 56, 8, 128), f32),
            pltpu.VMEM((2, 2, 32, 8, 128), f32),
            pltpu.VMEM((2, 5, 11, 8, 128), f32),
            pltpu.VMEM((10, 4, 8, 128), f32),
            pltpu.VMEM((768, 128), f32),
            pltpu.VMEM((384, 128), f32),
            pltpu.VMEM((128, 128), f32),
            pltpu.VMEM((5, 8, 128), f32),
            dma((5,)),
            pltpu.SemaphoreType.REGULAR,
            dma, dma, dma, dma, dma, dma((7,)), dma, dma((7,)), dma((16,)), dma((16,)),
        ],
        compiler_params=pltpu.CompilerParams(
            collective_id=0, has_side_effects=True, vmem_limit_bytes=24 * 1024 * 1024
        ),
        name="section",
    )(
        *(
            pltpu.with_memory_space_constraint(operand, pltpu.HBM)
            for operand in (
                fine_section.reshape(320, 128), fine_noise.reshape(192, 128),
                coarse_section.reshape(80, 64), taps, owner,
            )
        )
    )
    return (
        0.75 * fine_start + fine.reshape(fine_start.shape),
        0.75 * coarse_start + coarse.reshape(coarse_start.shape),
    )


def solution(mesh):
    cells = P(None, "gz", "gx", "gy")
    return jax.shard_map(
        local,
        mesh=mesh,
        in_specs=(cells, cells, cells, cells, cells, P(), P()),
        out_specs=(cells, cells),
        check_vma=False,
    )
```

```python
import jax
import jax.numpy as jnp
from jax import lax
from jax.experimental import pallas as pl
from jax.experimental.pallas import tpu as pltpu
from jax.sharding import PartitionSpec as P

MESH = pl.DeviceIdType.MESH
GX, GY, GZ = 16, 4, 8
GAMMA = 1.4
INDICATOR_EPS = 2e-06
RESTRICT_SCALE = 0.35355339059327373
NEAR = sorted(
    ((i, j) for i in range(GY) for j in range(GZ) if (i, j) != (0, 0)),
    key=lambda step: -((step[0] + 1) // 2 % 2 + 2 * (step[1] // 4) + min(step[1] % 4, -step[1] % 4)),
)
ALONG = [8, 7, 9, 6, 10, 5, 11, 4, 12, 3, 13, 2, 14, 1, 15]
CLOSE = [4, 12, 3, 13, 2, 14, 1, 15]
CORNERS = [(1, 1), (1, GY - 1), (GX - 1, 1), (GX - 1, GY - 1)]


def pressure_of(state, inverse):
    kinetic = 0.5 * (state[1] * state[1] + state[2] * state[2] + state[3] * state[3])
    return (GAMMA - 1.0) * (state[4] - kinetic * inverse)


def flux_entries(state, inverse, pressure, component):
    velocity = state[component] * inverse
    entries = [
        state[component],
        state[1] * velocity,
        state[2] * velocity,
        state[3] * velocity,
        (state[4] + pressure) * velocity,
    ]
    entries[component] = entries[component] + pressure
    return entries


def flux_alone(state, component):
    inverse = 1.0 / state[0]
    return flux_entries(state, inverse, pressure_of(state, inverse), component)


def fastest_of(state, inverse, pressure):
    largest = jnp.maximum(jnp.maximum(jnp.abs(state[1]), jnp.abs(state[2])), jnp.abs(state[3]))
    return largest * inverse + jnp.sqrt(GAMMA * pressure * inverse)


def prepare(steps, flux):
    cells = len(steps) - 5
    bends = [steps[k - 1] - 2.0 * steps[k] + steps[k + 1] for k in range(1, cells + 4)]
    if flux:
        linear = [
            steps[c + 2] + steps[c + 3] + (steps[c + 2] - steps[c + 4] - steps[c + 1] + steps[c + 3]) * (1.0 / 6.0)
            for c in range(cells)
        ]
    else:
        linear = [
            steps[c + 2] - steps[c + 3]
            + (steps[c + 4] - steps[c + 1] + 3.0 * (steps[c + 3] - steps[c + 2])) * (1.0 / 6.0)
            for c in range(cells)
        ]
    return list(steps) + bends + linear


def indicators(steps):
    squares = [e * e for e in steps]
    raised = [(2.0 / 3.0) * x + 0.5 * INDICATOR_EPS for x in squares]
    low, mid, high = [], [], []
    for i in range(len(steps) - 1):
        cross = steps[i] * steps[i + 1]
        base = raised[i] + raised[i + 1] - (11.0 / 6.0) * cross
        low.append(base + squares[i + 1])
        high.append(base + squares[i])
        mid.append(base + cross)
    return low, mid, high


def side(low, mid, high, first, second):
    to_mid = low * pltpu.reciprocal(mid, approx=True)
    to_high = low * pltpu.reciprocal(high, approx=True)
    w2 = 1.5 * (to_high * to_high)
    total = 3.0 * (to_mid * to_mid) + w2 + 0.5
    return (first + w2 * second) * pltpu.reciprocal(total, approx=True)


def sweep(flux, state, speed, cells):
    steps, bends = cells + 5, cells + 3
    scaled = [speed * u for u in state]
    up = [f + u for f, u in zip(flux[:steps], scaled[:steps])]
    down = [f - u for f, u in zip(flux[:steps], scaled[:steps])]
    low_u, mid_u, high_u = indicators(up[: cells + 4])
    low_d, mid_d, high_d = indicators(down)
    bend_u = [f + u for f, u in zip(flux[steps : steps + bends], scaled[steps : steps + bends])]
    bend_d = [f - u for f, u in zip(flux[steps : steps + bends], scaled[steps : steps + bends])]
    faces = []
    for j in range(cells + 1):
        right = side(low_u[j], mid_u[j + 1], high_u[j + 2], bend_u[j], bend_u[j + 1])
        left = side(high_d[j + 3], mid_d[j + 2], low_d[j + 1], bend_d[j + 2], bend_d[j + 1])
        faces.append(left - right)
    return [
        flux[steps + bends + c] + scaled[steps + bends + c] + (faces[c + 1] - faces[c]) * (1.0 / 6.0)
        for c in range(cells)
    ]


def swap_halves(values):
    return pltpu.roll(values, 64, 1)


def kernel(
    us_hbm, noise_hbm, cs_hbm, taps_hbm, owner_hbm, fine_out, coarse_out,
    us, noise, cs, taps, owner, sp1, sp2, cp, fcp, ux, fx, ty, fy, uz, fz, nz, gs, gr, nx, pk, hb, wx, nt,
    halves, dz, d16, d8, d1, az, a16, ay, a8, a1,
    ins, far_sem, s1_send, s1_recv, s2_send, s2_recv, gs_send, gs_recv, gr_send, gr_recv, hs, hr,
):
    loads = [
        pltpu.make_async_copy(src, dst, ins.at[n])
        for n, (src, dst) in enumerate(
            ((us_hbm, us), (cs_hbm, cs), (noise_hbm, noise), (taps_hbm, taps), (owner_hbm, owner))
        )
    ]
    for load in loads:
        load.start()
    gx, gy, gz = lax.axis_index("gx"), lax.axis_index("gy"), lax.axis_index("gz")

    def near(step):
        return {"gy": lax.rem(gy + step[0], GY), "gz": lax.rem(gz + step[1], GZ)}

    def along(step):
        return {"gx": lax.rem(gx + step, GX)}

    def corner(step):
        return {"gx": lax.rem(gx + step[0], GX), "gy": lax.rem(gy + step[1], GY)}

    barrier = pltpu.get_barrier_semaphore()
    greeted = [along(step) for step in CLOSE] + [near(step) for step in NEAR] + [corner(step) for step in CORNERS]
    for device in greeted:
        pl.semaphore_signal(barrier, inc=1, device_id=device, device_id_type=MESH)

    lane = lax.broadcasted_iota(jnp.int32, (8, 128), 1)
    first_half = lane < 64
    first_half_40 = lax.broadcasted_iota(jnp.int32, (40, 128), 1) < 64

    def cells(z):
        return [us[(f * 4 + z) * 16 : (f * 4 + z) * 16 + 16, :] for f in range(5)]

    loads[0].wait()
    best = jnp.zeros((16, 128), jnp.float32)
    for z in range(4):
        state = cells(z)
        inverse = 1.0 / state[0]
        best = jnp.maximum(best, fastest_of(state, inverse, pressure_of(state, inverse)))
    best = jnp.maximum(best[0:8], best[8:16])
    loads[1].wait()
    for f in range(5):
        cp[f * 8 : f * 8 + 8, :] = jnp.concatenate(
            [cs[f * 16 : f * 16 + 8, :], cs[f * 16 + 8 : f * 16 + 16, :]], axis=1
        )
    coarse = [cp[f * 8 : f * 8 + 8, :] for f in range(5)]
    coarse_inverse = 1.0 / coarse[0]
    coarse_pressure = pressure_of(coarse, coarse_inverse)
    coarse_best = fastest_of(coarse, coarse_inverse, coarse_pressure)
    best = jnp.where(
        first_half,
        jnp.maximum(best, swap_halves(best)),
        jnp.maximum(coarse_best, swap_halves(coarse_best)),
    )
    sp1[31:32, :] = jnp.max(best, axis=0, keepdims=True)

    pl.semaphore_wait(barrier, len(greeted))
    next_z, last_z = near((0, 1)), near((0, GZ - 1))
    next_x, last_x = along(1), along(GX - 1)
    next_y, last_y = near((1, 0)), near((GY - 1, 0))

    def send(index, src, dst, device):
        copy = pltpu.make_async_remote_copy(
            src_ref=src, dst_ref=dst, send_sem=hs.at[index], recv_sem=hr.at[index],
            device_id=device, device_id_type=MESH,
        )
        copy.start()
        return copy

    for n, step in enumerate(NEAR):
        pltpu.make_async_remote_copy(
            src_ref=sp1.at[pl.ds(31, 1)], dst_ref=sp1.at[pl.ds(n, 1)], send_sem=s1_send,
            recv_sem=s1_recv, device_id=near(step), device_id_type=MESH,
        ).start()
    for step in (4, GX - 4):
        pl.semaphore_signal(far_sem, inc=1, device_id=along(step), device_id_type=MESH)

    for load in loads[2:]:
        load.wait()
    eighth = jnp.bitwise_and(lane, 7)
    group_of_lane = lax.shift_right_logical(lane, 3)
    packed = [jnp.zeros((8, 128), jnp.float32) for _ in range(2)]
    for c in range(3):
        for z in range(4):
            n = c * 4 + z
            for h in range(2):
                tile = noise[n * 16 + h * 8 : n * 16 + h * 8 + 8, :]
                nx[n, 8 + h * 8 : 16 + h * 8, :] = tile
                packed[h] = jnp.where(group_of_lane == n, pltpu.roll(tile, (n * 8 + 4) % 128, 1), packed[h])
        for pair in range(2):
            row = (c * 4 + 2 * pair) * 16
            halves[(c * 2 + pair) * 16 : (c * 2 + pair) * 16 + 16, :] = (
                noise[row : row + 16, :] + noise[row + 16 : row + 32, :]
            )
    for h in range(2):
        pk[0, h * 8 : h * 8 + 8, :] = packed[h]
    from_lane = lax.broadcasted_iota(jnp.int32, (128, 128), 0)
    to_lane = lax.broadcasted_iota(jnp.int32, (128, 128), 1)
    restricted = jnp.zeros((24, 128), jnp.float32)
    for pair in range(2):
        rows = jnp.concatenate(
            [
                halves[pl.ds((c * 2 + pair) * 16, 8, stride=2), :]
                + halves[pl.ds((c * 2 + pair) * 16 + 1, 8, stride=2), :]
                for c in range(3)
            ],
            axis=0,
        )
        pick = (lax.shift_right_logical(from_lane, 1) + 64 * pair == to_lane).astype(jnp.float32)
        restricted = restricted + lax.dot(
            rows, pick, precision=lax.Precision.HIGHEST, preferred_element_type=jnp.float32
        )
    restricted = restricted * RESTRICT_SCALE
    coarse_packed = jnp.zeros((8, 128), jnp.float32)
    for c in range(3):
        tile = restricted[c * 8 : c * 8 + 8]
        nx[12 + c, 8:16, :] = tile
        nx[12 + c, 16:24, :] = tile
        swapped = swap_halves(tile)
        for p in range(2):
            m = c * 2 + p
            doubled = jnp.where(first_half, tile, swapped) if p == 0 else jnp.where(first_half, swapped, tile)
            coarse_packed = jnp.where(group_of_lane == m, pltpu.roll(doubled, m * 8 + 4, 1), coarse_packed)
    pk[1, 0:8, :] = coarse_packed
    pk[1, 8:16, :] = coarse_packed
    for f in range(5):
        gs[gz, f] = coarse[f]

    noise_xy = [
        send(0, nx.at[:, pl.ds(16, 8)], nx.at[:, pl.ds(0, 8)], next_x),
        send(1, nx.at[:, pl.ds(8, 8)], nx.at[:, pl.ds(24, 8)], last_x),
        send(2, pk, hb.at[0, :, pl.ds(8, 16)], next_y),
        send(3, pk, hb.at[1, :, pl.ds(8, 16)], last_y),
        send(4, pk.at[:, pl.ds(8, 8)], hb.at[0, :, pl.ds(0, 8)], corner(CORNERS[0])),
        send(5, pk.at[:, pl.ds(8, 8)], hb.at[1, :, pl.ds(0, 8)], corner(CORNERS[1])),
        send(6, pk.at[:, pl.ds(0, 8)], hb.at[0, :, pl.ds(24, 8)], corner(CORNERS[2])),
        send(7, pk.at[:, pl.ds(0, 8)], hb.at[1, :, pl.ds(24, 8)], corner(CORNERS[3])),
    ]

    for z in range(4):
        state = cells(z)
        inverse = 1.0 / state[0]
        pressure = pressure_of(state, inverse)
        for f, entry in enumerate(flux_entries(state, inverse, pressure, 2)):
            fy[(f * 4 + z) * 16 : (f * 4 + z) * 16 + 16, :] = entry
        for f, entry in enumerate(flux_entries(state, inverse, pressure, 3)):
            fz[f, 3 + z] = entry
        for f in range(5):
            uz[f, 3 + z] = state[f]

    state_z = [
        send(12, uz.at[:, pl.ds(4, 3)], uz.at[:, pl.ds(0, 3)], next_z),
        send(13, uz.at[:, pl.ds(3, 3)], uz.at[:, pl.ds(7, 3)], last_z),
    ]

    def column(ref, send_sem, recv_sem):
        copies = []
        for step in range(1, GZ):
            copy = pltpu.make_async_remote_copy(
                src_ref=ref.at[gz], dst_ref=ref.at[gz], send_sem=send_sem, recv_sem=recv_sem.at[step - 1],
                device_id=near((0, step)), device_id_type=MESH,
            )
            copy.start()
            origin = lax.rem(gz + GZ - step, GZ)
            copies.append(
                pltpu.make_async_remote_copy(
                    src_ref=ref.at[gz], dst_ref=ref.at[origin], send_sem=send_sem,
                    recv_sem=recv_sem.at[step - 1], device_id=next_z, device_id_type=MESH,
                )
            )
        whole = pltpu.make_async_remote_copy(
            src_ref=ref.at[pl.ds(0, GZ - 1)], dst_ref=ref.at[pl.ds(0, GZ - 1)], send_sem=send_sem,
            recv_sem=recv_sem.at[0], device_id=next_z, device_id_type=MESH,
        )
        return copies, whole

    state_column, state_column_sent = column(gs, gs_send, gs_recv)

    for k in range(16):
        for group in range(2):
            ux[(3 + k) * 32 + group * 8 : (3 + k) * 32 + group * 8 + 8, :] = us[
                pl.ds(group * 128 + k, 8, stride=16), :
            ]
        ux[(3 + k) * 32 + 16 : (3 + k) * 32 + 20, :] = us[pl.ds(256 + k, 4, stride=16), :]
    for k in range(8):
        row = cp[pl.ds(k, 5, stride=8), :]
        ux[(3 + k) * 32 + 24 : (3 + k) * 32 + 29, :] = row
        ux[(11 + k) * 32 + 24 : (11 + k) * 32 + 29, :] = row

    state_x = [
        send(8, ux.at[pl.ds(16 * 32, 96)], ux.at[pl.ds(0, 96)], next_x),
        send(9, ux.at[pl.ds(3 * 32, 96)], ux.at[pl.ds(19 * 32, 96)], last_x),
    ]

    for t in range(2):
        ty[t, 8:136, :] = us[t * 128 : t * 128 + 128, :].T
        ty[3 + t, 8:136, :] = fy[t * 128 : t * 128 + 128, :].T
    tail = us[256:320, :]
    ty[2, 8:136, :] = jnp.concatenate([tail, tail], axis=0).T
    tail = fy[256:320, :]
    ty[5, 8:136, :] = jnp.concatenate([tail, tail], axis=0).T
    for f, entry in enumerate(flux_entries(coarse, coarse_inverse, coarse_pressure, 2)):
        fcp[f * 8 : f * 8 + 8, :] = entry
    for t, ref in ((6, cp), (7, fcp)):
        both = ref[0:40, :]
        swapped = swap_halves(both)
        front = jnp.where(first_half_40, both, swapped)
        back = jnp.where(first_half_40, swapped, both)
        ty[t, 8:136, :] = jnp.concatenate([front, front[0:24], back, back[0:24]], axis=0).T
    state_y = [
        send(10, ty.at[:, pl.ds(128, 8)], ty.at[:, pl.ds(0, 8)], next_y),
        send(11, ty.at[:, pl.ds(8, 8)], ty.at[:, pl.ds(136, 8)], last_y),
    ]

    def flux_x(k, carry):
        base = k * 32
        state = [ux[pl.ds(base + 4 * f, 4), :] for f in range(5)]
        for f, entry in enumerate(flux_alone(state, 1)):
            fx[pl.ds(base + 4 * f, 4), :] = entry
        return carry

    lax.fori_loop(3, 19, flux_x, 0)
    for f, entry in enumerate(flux_entries(coarse, coarse_inverse, coarse_pressure, 1)):
        fcp[f * 8 : f * 8 + 8, :] = entry
    for k in range(8):
        fx[(3 + k) * 32 + 24 : (3 + k) * 32 + 29, :] = fcp[pl.ds(k, 5, stride=8), :]

    def total_wait(ref, count, send_sem, recv_sem):
        return pltpu.make_async_remote_copy(
            src_ref=ref.at[pl.ds(0, count)], dst_ref=ref.at[pl.ds(0, count)], send_sem=send_sem,
            recv_sem=recv_sem, device_id=next_x, device_id_type=MESH,
        )

    first_round = total_wait(sp1, 31, s1_send, s1_recv)
    first_round.wait_recv()
    sp2[15:16, :] = jnp.max(sp1[...], axis=0, keepdims=True)
    pl.semaphore_wait(far_sem, 2)
    for n, step in enumerate(ALONG):
        pltpu.make_async_remote_copy(
            src_ref=sp2.at[pl.ds(15, 1)], dst_ref=sp2.at[pl.ds(n, 1)], send_sem=s2_send,
            recv_sem=s2_recv, device_id=along(step), device_id_type=MESH,
        ).start()

    for copy in noise_xy:
        copy.wait_recv()

    def noise_along_x(n, carry):
        total = taps[0, 0] * nx[n, 4:20, :]
        for t in range(1, 9):
            total = total + taps[0, t] * nx[n, 4 + t : 20 + t, :]
        wx[pl.ds(pl.multiple_of(n * 16, 16), 16), :] = total
        return carry

    lax.fori_loop(0, 12, noise_along_x, 0)
    for c in range(3):
        total = taps[0, 0] * nx[12 + c, 4:12, :]
        for t in range(1, 9):
            base = 4 + t if t <= 4 else 12 + t
            total = total + taps[0, t] * nx[12 + c, base : base + 8, :]
        swapped = swap_halves(total)
        wx[192 + c * 8 : 200 + c * 8, :] = jnp.where(first_half, total, swapped)
        wx[216 + c * 8 : 224 + c * 8, :] = jnp.where(first_half, swapped, total)
    for b in range(2):
        for r in range(4):
            hb[0, b, r * 8 : r * 8 + 8, :] = jnp.where(
                eighth < 4, hb[0, b, r * 8 : r * 8 + 8, :], hb[1, b, r * 8 : r * 8 + 8, :]
            )
    beside = taps[0, 0] * hb[0, 0, 4:20, :]
    for t in range(1, 9):
        beside = beside + taps[0, t] * hb[0, 0, 4 + t : 20 + t, :]
    coarse_beside = taps[0, 0] * hb[0, 1, 4:12, :]
    for t in range(1, 9):
        base = 4 + t if t <= 4 else 12 + t
        coarse_beside = coarse_beside + taps[0, t] * hb[0, 1, base : base + 8, :]

    turned = jnp.concatenate([beside, coarse_beside, jnp.zeros((104, 128), jnp.float32)], axis=0).T
    rims = [jnp.zeros((8, 128), jnp.float32) for _ in range(2)]
    sixteenth = lax.shift_right_logical(lane, 4)
    for n in range(12):
        shift = (n % 8) * 16
        rolled = pltpu.roll(turned[n * 8 : n * 8 + 8], shift, 1) if shift else turned[n * 8 : n * 8 + 8]
        rims[n // 8] = jnp.where(sixteenth == n % 8, rolled, rims[n // 8])
    for c in range(3):
        for p in range(2):
            m = c * 2 + p
            target = 64 + p * 24 + c * 8
            rolled = pltpu.roll(turned[m * 8 : m * 8 + 8], target - 16, 1)
            rims[1] = jnp.where(group_of_lane == target // 8, rolled, rims[1])
    for t in range(2):
        nt[t, 8:136, :] = wx[t * 128 : t * 128 + 128, :].T
        nt[t, 4:8, :] = rims[t][0:4]
        nt[t, 136:140, :] = rims[t][4:8]
    total = taps[1, 0] * nt[0, 4:132, :]
    for t in range(1, 9):
        total = total + taps[1, t] * nt[0, 4 + t : 132 + t, :]
    total = total.T
    for n in range(8):
        nz[n // 4, 4 + n % 4] = total[n * 16 : n * 16 + 16]
    left = taps[1, 0] * nt[1, 4:132, :]
    for t in range(1, 5):
        left = left + taps[1, t] * nt[1, 4 + t : 132 + t, :]
    total = left
    for t in range(5, 9):
        total = total + taps[1, t] * nt[1, 4 + t : 132 + t, :]
    own = left[0:64]
    for t in range(5, 9):
        own = own + taps[1, t] * nt[1, 68 + t : 132 + t, :]
    front = jnp.where(lax.broadcasted_iota(jnp.int32, (64, 128), 1) < 64, total[0:64], own)
    total = jnp.concatenate([front, total[64:128]], axis=0).T
    for n in range(8, 12):
        nz[n // 4, 4 + n % 4] = total[(n - 8) * 16 : (n - 8) * 16 + 16]
    for c in range(3):
        gr[gz, c] = jnp.where(
            first_half, total[64 + c * 8 : 72 + c * 8], swap_halves(total[88 + c * 8 : 96 + c * 8])
        )
    noise_z = [
        send(14, nz.at[:, pl.ds(4, 4)], nz.at[:, pl.ds(0, 4)], next_z),
        send(15, nz.at[:, pl.ds(4, 4)], nz.at[:, pl.ds(8, 4)], last_z),
    ]
    noise_column, noise_column_sent = column(gr, gr_send, gr_recv)

    for copy in state_x:
        copy.wait_recv()
    lax.fori_loop(0, 3, flux_x, 0)
    lax.fori_loop(19, 22, flux_x, 0)
    for k in (0, 1, 2, 19, 20, 21):
        state = [ux[k * 32 + 24 + f : k * 32 + 25 + f, :] for f in range(5)]
        target = k if k < 3 else k - 8
        for f, entry in enumerate(flux_alone(state, 1)):
            fx[target * 32 + 24 + f : target * 32 + 25 + f, :] = entry
    for copy in state_x:
        copy.wait_send()
    for k in (11, 12, 13):
        ux[k * 32 + 24 : k * 32 + 32, :] = ux[(k + 8) * 32 + 24 : (k + 8) * 32 + 32, :]

    def store(ref, n, group, rows):
        for k, value in enumerate(prepare([rows[k + 1] - rows[k] for k in range(len(rows) - 1)], n == 0)):
            ref[n, group, k] = value

    for n, ref in enumerate((fx, ux)):

        def steps_x(group, carry):
            base = pl.multiple_of(group * 8, 8)
            store(d16, n, group, [ref[pl.ds(k * 32 + base, 8), :] for k in range(22)])
            return carry

        lax.fori_loop(0, 3, steps_x, 0)
        store(d8, n, 0, [ref[k * 32 + 24 : k * 32 + 32, :] for k in range(14)])

    for copy in state_y:
        copy.wait_recv()
    for n in range(2):

        def steps_y(t, carry):
            store(d16, n, 3 + t, [ty[3 - 3 * n + t, pl.ds(5 + k, 8, stride=16), :] for k in range(22)])
            return carry

        lax.fori_loop(0, 3, steps_y, 0)
    for copy in state_y:
        copy.wait_send()
    for n, t in enumerate((7, 6)):
        ty[t, 72:80, :] = ty[t, 136:144, :]
        store(d8, n, 1, [ty[t, pl.ds(5 + k, 8, stride=8), :] for k in range(14)])

    for copy in state_z:
        copy.wait_recv()
    for k in (0, 1, 2, 7, 8, 9):
        state = [uz[f, k] for f in range(5)]
        for f, entry in enumerate(flux_alone(state, 3)):
            fz[f, k] = entry

    def steps_z(f, carry):
        for n, ref in enumerate((fz, uz)):
            for h in range(2):
                store(dz, n, f * 2 + h, [ref[f, k, h * 8 : h * 8 + 8, :] for k in range(10)])
        return carry

    lax.fori_loop(0, 5, steps_z, 0)
    block = jnp.int32(0)
    for j in range(GZ):
        block = block + j * (owner[j] == gz).astype(jnp.int32)

    def mixed(left, right):
        return jnp.where(first_half, swap_halves(left), swap_halves(right))

    around = [lax.rem(block + GZ + m, GZ) for m in range(-2, 3)]
    for copy in state_column:
        copy.wait_recv()
    pairs_u, pairs_f = [], []
    for j in around:
        state = [gs[owner[j], f] for f in range(5)]
        pairs_u.append(state)
        pairs_f.append(flux_alone(state, 3))
    for n, pairs in enumerate((pairs_f, pairs_u)):
        for f in range(5):
            planes = []
            for j in range(-3, 4):
                m = (j + 4) // 2
                planes.append(pairs[m][f] if j % 2 == 0 else mixed(pairs[m][f], pairs[m + 1][f]))
            store(d1, n, f, planes)

    second_round = total_wait(sp2, 15, s2_send, s2_recv)
    second_round.wait_recv()
    speeds = jnp.max(sp2[...], axis=0, keepdims=True)
    front_row = lax.broadcasted_iota(jnp.int32, (1, 128), 1) < 64
    speed_fine = jnp.broadcast_to(
        jnp.max(jnp.where(front_row, speeds, 0.0), axis=1, keepdims=True), (8, 128)
    )
    speed_coarse = jnp.broadcast_to(
        jnp.max(jnp.where(front_row, 0.0, speeds), axis=1, keepdims=True), (8, 128)
    )

    def taken(ref, n, g, cells):
        return [ref[n, g, k] for k in range(3 * cells + 8)]

    def sweep_16(g):
        for k, out in enumerate(sweep(taken(d16, 0, g, 16), taken(d16, 1, g, 16), speed_fine, 16)):
            a16[pl.ds(g * 128 + k, 8, stride=16), :] = out

    def sweep_y(g, carry):
        sweep_16(3 + g)
        return carry

    def sweep_x(g, carry):
        sweep_16(g)
        row = pl.multiple_of(g * 128, 128)
        ay[pl.ds(row, 128), :] = a16[pl.ds(384 + row, 128), :].T
        return carry

    def sweep_z(g):
        for z, out in enumerate(sweep(taken(dz, 0, g, 4), taken(dz, 1, g, 4), speed_fine, 4)):
            az[g, z] = out

    def sweep_five(half, carry):
        for n in range(5):
            sweep_z(half * 5 + n)
        return carry

    lax.fori_loop(0, 3, sweep_y, 0)
    lax.fori_loop(0, 3, sweep_x, 0)
    lax.fori_loop(0, 2, sweep_five, 0)
    for g in range(2):
        for k, out in enumerate(sweep(taken(d8, 0, g, 8), taken(d8, 1, g, 8), speed_coarse, 8)):
            a8[pl.ds(g * 64 + k, 8, stride=8), :] = out
    for g in range(5):
        a1[g] = sweep(taken(d1, 0, g, 1), taken(d1, 1, g, 1), speed_coarse, 1)[0]

    for copy in noise_z:
        copy.wait_recv()
    for copy in noise_column:
        copy.wait_recv()
    push = []
    for c in range(3):
        pairs = [gr[j, c] for j in around]
        total = taps[2, 0] * pairs[0]
        for t in range(1, 9):
            plane = pairs[t // 2] if t % 2 == 0 else mixed(pairs[t // 2], pairs[t // 2 + 1])
            total = total + taps[2, t] * plane
        push.append(2.0 * total)
    work = coarse[1] * push[0] + coarse[2] * push[1] + coarse[3] * push[2]
    coarse_source = [None, coarse[0] * push[0], coarse[0] * push[1], coarse[0] * push[2], work]
    for f in range(1, 5):
        fcp[f * 8 : f * 8 + 8, :] = coarse_source[f]

    rate_fine = 0.1 / speed_fine
    rate_coarse = 0.1 / speed_coarse
    for z in range(4):
        for h in range(2):
            part = slice(h * 8, h * 8 + 8)
            push = []
            for c in range(3):
                total = taps[2, 0] * nz[c, z, part, :]
                for t in range(1, 9):
                    total = total + taps[2, t] * nz[c, z + t, part, :]
                push.append(total)
            state = [us[(f * 4 + z) * 16 + h * 8 : (f * 4 + z) * 16 + h * 8 + 8, :] for f in range(5)]
            work = state[1] * push[0] + state[2] * push[1] + state[3] * push[2]
            source = [None, state[0] * push[0], state[0] * push[1], state[0] * push[2], work]
            for f in range(5):
                row = (f * 4 + z) * 16 + h * 8
                change = -0.5 * (a16[row : row + 8, :] + ay[row : row + 8, :] + az[f * 2 + h, z])
                if f > 0:
                    change = change + source[f]
                fine_out[row : row + 8, :] = 0.25 * state[f] + rate_fine * change

    along_y = a8[64:128, :]
    turned = jnp.concatenate([along_y, along_y], axis=0).T
    along_y = jnp.where(first_half_40, turned[0:40], turned[64:104])
    for f in range(5):
        change = -0.5 * (a8[f * 8 : f * 8 + 8, :] + along_y[f * 8 : f * 8 + 8] + a1[f])
        if f > 0:
            change = change + fcp[f * 8 : f * 8 + 8, :]
        result = 0.25 * cp[f * 8 : f * 8 + 8, :] + rate_coarse * change
        coarse_out[f * 16 : f * 16 + 8, :] = result[:, 0:64]
        coarse_out[f * 16 + 8 : f * 16 + 16, :] = swap_halves(result)[:, 0:64]

    first_round.wait_send()
    second_round.wait_send()
    for copy in noise_xy + state_z + noise_z:
        copy.wait_send()
    state_column_sent.wait_send()
    noise_column_sent.wait_send()


def local(fine_start, fine_section, fine_noise, coarse_start, coarse_section, taps, owner):
    f32 = jnp.float32
    vmem = pl.BlockSpec(memory_space=pltpu.VMEM)
    hbm = pl.BlockSpec(memory_space=pltpu.HBM)
    dma = pltpu.SemaphoreType.DMA
    fine, coarse = pl.pallas_call(
        kernel,
        out_shape=(jax.ShapeDtypeStruct((320, 128), f32), jax.ShapeDtypeStruct((80, 64), f32)),
        in_specs=[hbm] * 5,
        out_specs=(vmem, vmem),
        scratch_shapes=[
            pltpu.VMEM((320, 128), f32),
            pltpu.VMEM((192, 128), f32),
            pltpu.VMEM((80, 64), f32),
            pltpu.SMEM((3, 9), f32),
            pltpu.SMEM((8,), jnp.int32),
            pltpu.VMEM((32, 128), f32),
            pltpu.VMEM((16, 128), f32),
            pltpu.VMEM((40, 128), f32),
            pltpu.VMEM((40, 128), f32),
            pltpu.VMEM((704, 128), f32),
            pltpu.VMEM((704, 128), f32),
            pltpu.VMEM((8, 144, 128), f32),
            pltpu.VMEM((320, 128), f32),
            pltpu.VMEM((5, 10, 16, 128), f32),
            pltpu.VMEM((5, 10, 16, 128), f32),
            pltpu.VMEM((3, 12, 16, 128), f32),
            pltpu.VMEM((8, 5, 8, 128), f32),
            pltpu.VMEM((8, 3, 8, 128), f32),
            pltpu.VMEM((15, 32, 128), f32),
            pltpu.VMEM((2, 16, 128), f32),
            pltpu.VMEM((2, 2, 32, 128), f32),
            pltpu.VMEM((256, 128), f32),
            pltpu.VMEM((2, 144, 128), f32),
            pltpu.VMEM((96, 128), f32),
            pltpu.VMEM((2, 10, 20, 8, 128), f32),
            pltpu.VMEM((2, 6, 56, 8, 128), f32),
            pltpu.VMEM((2, 2, 32, 8, 128), f32),
            pltpu.VMEM((2, 5, 11, 8, 128), f32),
            pltpu.VMEM((10, 4, 8, 128), f32),
            pltpu.VMEM((768, 128), f32),
            pltpu.VMEM((384, 128), f32),
            pltpu.VMEM((128, 128), f32),
            pltpu.VMEM((5, 8, 128), f32),
            dma((5,)),
            pltpu.SemaphoreType.REGULAR,
            dma, dma, dma, dma, dma, dma((7,)), dma, dma((7,)), dma((16,)), dma((16,)),
        ],
        compiler_params=pltpu.CompilerParams(
            collective_id=0, has_side_effects=True, vmem_limit_bytes=24 * 1024 * 1024
        ),
        name="section",
    )(
        *(
            pltpu.with_memory_space_constraint(operand, pltpu.HBM)
            for operand in (
                fine_section.reshape(320, 128), fine_noise.reshape(192, 128),
                coarse_section.reshape(80, 64), taps, owner,
            )
        )
    )
    return (
        0.75 * fine_start + fine.reshape(fine_start.shape),
        0.75 * coarse_start + coarse.reshape(coarse_start.shape),
    )


def solution(mesh):
    cells = P(None, "gz", "gx", "gy")
    return jax.shard_map(
        local,
        mesh=mesh,
        in_specs=(cells, cells, cells, cells, cells, P(), P()),
        out_specs=(cells, cells),
        check_vma=False,
    )
```
